32 devices in a mesh: lat: 16 (over z, y, x), mp: 2 (over core).
Axes of the slice: x: 2, y: 2, z: 4, core: 2. Of those that a mesh axis runs over, the one named last changes fastest.
Arguments:
- field: bfloat16 [32, 180, 768], P('lat', None, 'mp'), may hold values from -6 to 6
- row_group: int32 [32], replicated, may hold values from 0 to 7, as said below
- row_valid: int32 [32], replicated, may hold values from 0 to 1, as said below
- norm1_gain: float32 [768], P('mp'), may hold values from 0.5 to 1.5
- norm1_bias: float32 [768], P('mp'), may hold values from -4 to 4
- spec_w1: bfloat16 [2, 8, 96, 96], P(None, 'mp'), may hold values from -0.4375 to 0.4375
- spec_b1: float32 [2, 8, 96], P(None, 'mp'), may hold values from -4 to 4
- spec_w2: bfloat16 [2, 8, 96, 96], P(None, 'mp'), may hold values from -0.4375 to 0.4375
- spec_b2: float32 [2, 8, 96], P(None, 'mp'), may hold values from -0.3125 to 0.3125
- norm2_gain: float32 [768], P('mp'), may hold values from 0.5 to 1.5
- norm2_bias: float32 [768], P('mp'), may hold values from -4 to 4
- fc1_weight: bfloat16 [768, 3072], P(None, 'mp'), may hold values from -0.21875 to 0.21875
- fc1_bias: float32 [3072], P('mp'), may hold values from -6 to 6
- fc2_weight: bfloat16 [3072, 768], P('mp'), may hold values from -0.109375 to 0.109375
- fc2_bias: float32 [768], P('mp'), may hold values from -4 to 4
- cotangent: bfloat16 [32, 180, 768], P('lat', None, 'mp'), may hold values from -8 to 8
Outputs:
- out_field: bfloat16 [32, 180, 768], P('lat', None, 'mp')
- grad_field: float32 [32, 180, 768], P('lat', None, 'mp')
- grad_norm1_gain: float32 [768], P('mp')
- grad_norm1_bias: float32 [768], P('mp')
- grad_spec_w1: float32 [2, 8, 96, 96], P(None, 'mp')
- grad_spec_b1: float32 [2, 8, 96], P(None, 'mp')
- grad_spec_w2: float32 [2, 8, 96, 96], P(None, 'mp')
- grad_spec_b2: float32 [2, 8, 96], P(None, 'mp')
- grad_norm2_gain: float32 [768], P('mp')
- grad_norm2_bias: float32 [768], P('mp')
- grad_fc1_weight: float32 [768, 3072], P('lat', 'mp')
- grad_fc1_bias: float32 [3072], P('mp')
- grad_fc2_weight: float32 [3072, 768], P('mp', 'lat')
- grad_fc2_bias: float32 [768], P('mp')
The draws below stay inside these ranges and needn't reach their ends.
Inputs may be any that keep to these rules, and one draw needn't show every extreme that they name: `row_group`: among rows with row_valid 1, group 0 has exactly 17 rows, always including the first row, the row in the middle and the last row; each group from 1 to 7 has exactly 2. Rows of a group lie anywhere. `row_valid`: exactly 1 row is 0.
All inputs are finite; a program needn't handle non-finite values.
Results may differ from the reference program's by a relative error of at most 0.0095.
The reference program's roundings to bfloat16 on the way count: a program that leaves them out, or rounds other values in their place, can miss the bound.
Values may be sent and summed in bfloat16 or wider, within the bound.
No kernel may reach another device: no remote copies, remote signals or barrier semaphores. Data moves between devices by JAX's collectives and lax.ppermute only.
A program may use at most 256 MiB of HBM per device.

```python
import math
import jax
import jax.numpy as jnp
from jax import lax

D = 768
FF = 3072
BLOCKS = 8
LON_FINE = 180
LON_COARSE = 45
GROUPS = 8
BS = 96
ROWS = 32
COARSE_LEN = 2
FINE_LEN = 17


def row_layout(key):
    order = jax.random.permutation(key, ROWS).astype(jnp.int32)
    indices = jnp.arange(ROWS, dtype=jnp.int32)
    priority = jnp.argsort(order, stable=True).astype(jnp.int32)
    priority = jnp.where(indices == 0, -3, jnp.where(indices == ROWS // 2, -2, jnp.where(indices == ROWS - 1, -1, priority))).astype(jnp.int32)
    ranking = jnp.argsort(jnp.argsort(priority, stable=True), stable=True).astype(jnp.int32)
    grouping = jnp.where(ranking < FINE_LEN, 0, 1 + (ranking - FINE_LEN) // COARSE_LEN).astype(jnp.int32)
    validity = (ranking < FINE_LEN + (GROUPS - 1) * COARSE_LEN).astype(jnp.int32)
    return (grouping, validity)


def draw_row_group(key, part):
    grouping, validity = row_layout(key)
    key = jax.random.fold_in(key, 11)
    filler = jax.random.randint(key, (ROWS,), 0, GROUPS, dtype=jnp.int32)
    return jnp.where(validity > 0, grouping, filler).astype(jnp.int32)


def draw_row_valid(key, part):
    grouping, validity = row_layout(key)
    return validity.astype(jnp.int32)


def draw_cotangent(key, part):
    key = jax.random.fold_in(key, 13)
    noise_key, offset_key = jax.random.split(key)
    noise = jax.random.normal(noise_key, (ROWS, LON_FINE, D), jnp.float32)
    offset = 0.7 * jax.random.normal(offset_key, (ROWS, LON_FINE, 1), jnp.float32)
    return jnp.clip(noise + offset, -8.0, 8.0).astype(jnp.bfloat16)


def level_of(rng, shape, cuts, low, high):
    gain = 1.0
    for dim, parts in cuts:
        steps = jax.random.uniform(jax.random.fold_in(jax.random.fold_in(rng, 6), dim), (parts,), jnp.float32, low / len(cuts), high / len(cuts))
        gain = gain * jnp.repeat(jnp.exp(steps), shape[dim] // parts).reshape((-1,) + (1,) * (len(shape) - 1 - dim))
    return gain


def gaussian(own_key, shape, width, reach, cuts=(), held_as=jnp.bfloat16):
    result = jax.random.normal(own_key, shape, jnp.float32) * width
    if len(cuts) > 0:
        result = level_of(own_key, shape, cuts, -0.22, 0.18) * result
    return jnp.clip(result, min=-reach, max=reach).astype(held_as)


def setup_inputs(seed: int = 0) -> dict:
    key_list = jax.random.split(jax.random.key(seed), 17)
    field = gaussian(key_list[0], (ROWS, LON_FINE, D), 1.0, 6.0, ((0, 16), (2, 2)))
    row_group = draw_row_group(jax.random.fold_in(key_list[16], 71), 0)
    row_valid = draw_row_valid(jax.random.fold_in(key_list[16], 71), 0)
    norm1_gain = jnp.clip(1.0 + 0.1 * jax.random.normal(key_list[3], (D,), jnp.float32), 0.5, 1.5)
    norm1_bias = gaussian(key_list[4], (D,), 0.3, 4.0, ((0, 2),), jnp.float32)
    spec_w1 = gaussian(key_list[5], (2, BLOCKS, BS, BS), (2 * BS) ** -0.5, 0.4375, ((1, 2),))
    spec_b1 = gaussian(key_list[6], (2, BLOCKS, BS), 0.3, 4.0, ((1, 2),), jnp.float32)
    spec_w2 = gaussian(key_list[7], (2, BLOCKS, BS, BS), (2 * BS) ** -0.5, 0.4375, ((1, 2),))
    spec_b2 = gaussian(key_list[8], (2, BLOCKS, BS), 0.02, 0.3125, ((1, 2),), jnp.float32)
    norm2_gain = jnp.clip(1.0 + 0.1 * jax.random.normal(key_list[9], (D,), jnp.float32), 0.5, 1.5)
    norm2_bias = gaussian(key_list[10], (D,), 0.3, 4.0, ((0, 2),), jnp.float32)
    fc1_weight = gaussian(key_list[11], (D, FF), D ** -0.5, 0.21875, ((1, 2),))
    fc1_bias = gaussian(key_list[12], (FF,), 0.5, 6.0, ((0, 2),), jnp.float32)
    fc2_weight = gaussian(key_list[13], (FF, D), FF ** -0.5, 0.109375, ((0, 2),))
    fc2_bias = gaussian(key_list[14], (D,), 0.3, 4.0, ((0, 2),), jnp.float32)
    cotangent = draw_cotangent(jax.random.fold_in(key_list[16], 71), 0)
    return dict(field=field, row_group=row_group, row_valid=row_valid, norm1_gain=norm1_gain, norm1_bias=norm1_bias, spec_w1=spec_w1, spec_b1=spec_b1, spec_w2=spec_w2, spec_b2=spec_b2, norm2_gain=norm2_gain, norm2_bias=norm2_bias, fc1_weight=fc1_weight, fc1_bias=fc1_bias, fc2_weight=fc2_weight, fc2_bias=fc2_bias, cotangent=cotangent)


EPSILON = 1e-05
SHRINK = 0.01
HIGHEST = lax.Precision.HIGHEST

@jax.custom_vjp
def low(v):
    return lax.optimization_barrier(v.astype(jnp.bfloat16)).astype(jnp.float32)

@jax.custom_vjp
def low_back(v):
    return v

def low_keep(v):
    return (low(v), None)

def low_pass(kept, grad):
    return (grad,)

def back_keep(v):
    return (v, None)

def back_low(kept, grad):
    return (low(grad),)
low.defvjp(low_keep, low_pass)
low_back.defvjp(back_keep, back_low)

def row_tables(row_group, row_valid):
    member = (row_group[:, None] == jnp.arange(GROUPS, dtype=jnp.int32)[None, :]).astype(jnp.int32) * row_valid[:, None]
    counts = lax.optimization_barrier(jnp.sum(member, axis=0)).astype(jnp.int32)
    before = (jnp.cumsum(member, axis=0) - member).astype(jnp.int32)
    offset = lax.optimization_barrier(jnp.sum(before * member, axis=1)).astype(jnp.int32)
    length = jnp.maximum(lax.optimization_barrier(jnp.sum(member * counts[None, :], axis=1)), 1).astype(jnp.int32)
    return (offset, length)

def latitude_pair(left_info, right_info, turn_sign):
    off_left, len_left, grp_left, val_left = left_info
    off_right, len_right, grp_right, val_right = right_info
    phases = off_left[:, None] * off_right[None, :] % len_left[:, None]
    lengths = len_left[:, None].astype(jnp.float32)
    angles = 2.0 * math.pi * phases.astype(jnp.float32) / lengths
    kept_pair = ((grp_left[:, None] == grp_right[None, :]) & (val_left[:, None] > 0) & (val_right[None, :] > 0)).astype(jnp.float32)
    scaling = kept_pair * lax.rsqrt(lengths)
    return (scaling * jnp.cos(angles), turn_sign * scaling * jnp.sin(angles))

def longitude_tables(widths, columns):
    indices = jnp.arange(columns, dtype=jnp.int32)
    phases = (indices[:, None] * indices[None, :])[None, :, :] % widths[:, None, None]
    lengths = widths[:, None, None].astype(jnp.float32)
    angles = 2.0 * math.pi * phases.astype(jnp.float32) / lengths
    inside = ((indices[None, :, None] < widths[:, None, None]) & (indices[None, None, :] < widths[:, None, None])).astype(jnp.float32)
    scaling = inside * lax.rsqrt(lengths)
    return (scaling * jnp.cos(angles), scaling * jnp.sin(angles))

def complex_rows(real_mat, imag_mat, values, channels):
    leading = jnp.einsum('ab,bwc->awc', real_mat, values, precision=HIGHEST)
    trailing = jnp.einsum('ab,bwc->awc', imag_mat, values, precision=HIGHEST)
    return jnp.concatenate([leading[..., :channels] - trailing[..., channels:], leading[..., channels:] + trailing[..., :channels]], axis=-1)

def lon_forward(lon_cos, lon_sin, values):
    return jnp.concatenate([jnp.einsum('rkw,rwc->rkc', lon_cos, values, precision=HIGHEST), -jnp.einsum('rkw,rwc->rkc', lon_sin, values, precision=HIGHEST)], axis=-1)

def lon_back(lon_cos, lon_sin, values, channels):
    return jnp.einsum('rkw,rwc->rkc', lon_cos, values[..., :channels], precision=HIGHEST) - jnp.einsum('rkw,rwc->rkc', lon_sin, values[..., channels:], precision=HIGHEST)

def smooth_gate(values):
    return jax.nn.gelu(values, approximate=True)

def shrinkage(values):
    return values - SHRINK * jnp.tanh(values / SHRINK)

def norm_rows(values, gain_vec, bias_vec):
    average = lax.optimization_barrier(jnp.mean(values, axis=-1, keepdims=True))
    centred = values - average
    spread = lax.optimization_barrier(jnp.mean(centred * centred, axis=-1, keepdims=True))
    return centred * lax.rsqrt(spread + EPSILON) * gain_vec + bias_vec

def complex_layer(real_in, imag_in, weight, bias):

    def product_of(values, matrix):
        return jnp.einsum('rwnb,nbc->rwnc', values, matrix, precision=HIGHEST)
    real_out = product_of(real_in, weight[0]) - product_of(imag_in, weight[1]) + bias[0]
    imag_out = product_of(real_in, weight[1]) + product_of(imag_in, weight[0]) + bias[1]
    return (real_out, imag_out)

def forward(incoming, norm1_gain, norm1_bias, spec_w1, spec_b1, spec_w2, spec_b2, norm2_gain, norm2_bias, fc1_weight, fc1_bias, fc2_weight, fc2_bias, tables):
    token_mask, lon_cos, lon_sin, lat_fwd, lat_inv = tables
    normed = norm_rows(incoming, norm1_gain, norm1_bias)
    spec_in = lon_forward(lon_cos, lon_sin, normed * token_mask)
    spectrum = low(complex_rows(lat_fwd[0], lat_fwd[1], spec_in, D))
    low_real = spectrum[..., :D].reshape(ROWS, LON_FINE, BLOCKS, BS)
    low_imag = spectrum[..., D:].reshape(ROWS, LON_FINE, BLOCKS, BS)
    first_real, first_imag = complex_layer(low_real, low_imag, spec_w1, spec_b1)
    first_real = low_back(first_real)
    first_imag = low_back(first_imag)
    hidden_real = low(smooth_gate(first_real))
    hidden_imag = low(smooth_gate(first_imag))
    second_real, second_imag = complex_layer(hidden_real, hidden_imag, spec_w2, spec_b2)
    second_real = low_back(second_real)
    second_imag = low_back(second_imag)
    shrunk = jnp.concatenate([shrinkage(second_real).reshape(ROWS, LON_FINE, D), shrinkage(second_imag).reshape(ROWS, LON_FINE, D)], axis=-1)
    spatial = complex_rows(lat_inv[0], lat_inv[1], shrunk, D)
    filtered = lon_back(lon_cos, lon_sin, spatial, D) * token_mask
    mixed_one = incoming + filtered + normed
    normed_low = low(norm_rows(mixed_one, norm2_gain, norm2_bias)).reshape(ROWS * LON_FINE, D)
    pre_act = low_back(jnp.dot(normed_low, fc1_weight, precision=HIGHEST) + fc1_bias)
    act_low = low(smooth_gate(pre_act))
    mlp_out = jnp.dot(act_low, fc2_weight, precision=HIGHEST) + fc2_bias
    return mixed_one + mlp_out.reshape(ROWS, LON_FINE, D)

def reference(field, row_group, row_valid, norm1_gain, norm1_bias, spec_w1, spec_b1, spec_w2, spec_b2, norm2_gain, norm2_bias, fc1_weight, fc1_bias, fc2_weight, fc2_bias, cotangent):
    offset, length = row_tables(row_group, row_valid)
    row_info = (offset, length, row_group, row_valid)
    widths = jnp.where(row_group == 0, LON_FINE, LON_COARSE).astype(jnp.int32)
    lon_cos, lon_sin = longitude_tables(widths, LON_FINE)
    positions = jnp.arange(LON_FINE, dtype=jnp.int32)
    token_mask = ((row_valid[:, None] > 0) & (positions[None, :] < widths[:, None])).astype(jnp.float32)[..., None]
    lat_fwd = latitude_pair(row_info, row_info, -1.0)
    lat_inv = latitude_pair(row_info, row_info, 1.0)
    tables = (token_mask, lon_cos, lon_sin, lat_fwd, lat_inv)
    weights = tuple((entry_value.astype(jnp.float32) for entry_value in (norm1_gain, norm1_bias, spec_w1, spec_b1, spec_w2, spec_b2, norm2_gain, norm2_bias, fc1_weight, fc1_bias, fc2_weight, fc2_bias)))

    def run_layer(incoming, *params):
        return forward(incoming, *params, tables)
    primal, pullback = jax.vjp(run_layer, field.astype(jnp.float32), *weights)
    gradients = pullback(cotangent.astype(jnp.float32))
    return (primal.astype(jnp.bfloat16), gradients[0], gradients[1], gradients[2], gradients[3], gradients[4], gradients[5], gradients[6], gradients[7], gradients[8], gradients[9], gradients[10], gradients[11], gradients[12])
```

```python
import math

import jax
import jax.numpy as jnp
import numpy as np
from jax import lax
from jax.sharding import PartitionSpec as P

LON_FINE = 180
LON_COARSE = 45
GROUPS = 8
EPSILON = 1e-05
SHRINK = 0.01
HALVES = LON_FINE // 2 + 1
BF = jnp.bfloat16
F32 = jnp.float32


def split_two(values):
    high = lax.reduce_precision(values, 8, 7)
    return high.astype(BF), (values - high).astype(BF)


def mm(left, right):
    return lax.dot_general(left, right, (((1,), (0,)), ((), ())), preferred_element_type=F32)


def mm_t(left, right):
    return lax.dot_general(left, right, (((0,), (0,)), ((), ())), preferred_element_type=F32)


def mm_nt(left, right):
    return lax.dot_general(left, right, (((1,), (1,)), ((), ())), preferred_element_type=F32)


def longitude_constant(width, parts, share, rows_dev, columns):
    freq = np.arange(parts * share).reshape(parts, share)
    cols = np.arange(columns)
    phases = (freq[..., None] * cols) % width
    angles = 2.0 * np.pi * phases / width
    inside = (freq[..., None] * 2 <= width) & (cols < width)
    scale = inside / np.sqrt(width)
    pair = np.stack([scale * np.cos(angles), -scale * np.sin(angles)], axis=1)
    full = np.zeros((parts, rows_dev, 2, share, rows_dev, columns), np.float32)
    for r in range(rows_dev):
        full[:, r, :, :, r, :] = pair
    return full.reshape(parts * rows_dev * 2 * share, rows_dev * columns)


def np_split(values):
    high = values.astype(jnp.bfloat16)
    low = (values - high.astype(np.float32)).astype(jnp.bfloat16)
    return high, low


def row_tables(row_group, row_valid):
    member = (row_group[:, None] == jnp.arange(GROUPS, dtype=jnp.int32)[None, :]).astype(
        jnp.int32
    ) * row_valid[:, None]
    counts = jnp.sum(member, axis=0)
    before = jnp.cumsum(member, axis=0) - member
    offset = jnp.sum(before * member, axis=1)
    length = jnp.maximum(jnp.sum(member * counts[None, :], axis=1), 1)
    return (offset, length)


def latitude_tables(row_group, row_valid):
    offset, length = row_tables(row_group, row_valid)
    phases = offset[:, None] * offset[None, :] % length[:, None]
    lengths = length[:, None].astype(F32)
    angles = 2.0 * math.pi * phases.astype(F32) / lengths
    kept = (
        (row_group[:, None] == row_group[None, :])
        & (row_valid[:, None] > 0)
        & (row_valid[None, :] > 0)
    ).astype(F32) * lax.rsqrt(lengths)
    return kept * jnp.cos(angles), kept * jnp.sin(angles)


def latitude_matrix(row_group, row_valid, rows, rows_dev, share, first_freq):
    cos_mat, sin_mat = latitude_tables(row_group, row_valid)
    both = jnp.concatenate([cos_mat, sin_mat], axis=1)
    width = jnp.where(row_group == 0, LON_FINE, LON_COARSE).astype(jnp.int32)
    freq = first_freq + jnp.arange(share, dtype=jnp.int32)
    lone = (freq[None, :] == 0) | (2 * freq[None, :] == width[:, None])
    keep = jnp.stack([jnp.ones((rows, share), F32), 1.0 - lone.astype(F32)]).reshape(-1)
    keep = jnp.concatenate([keep, keep])[:, None]
    left = np.kron(np.eye(rows), np.ones((share, 1))).astype(np.float32)
    right = np.zeros((2, 2, 2, rows, rows, 2, share), np.float32)
    signs = {
        (0, 0): ((1, 0), (0, 1)),
        (1, 0): ((0, 1), (-1, 0)),
        (0, 1): ((1, 0), (0, -1)),
        (1, 1): ((0, -1), (-1, 0)),
    }
    eye = np.eye(rows)[:, :, None]
    for (part, sign), (cos_sign, sin_sign) in signs.items():
        for inner in range(2):
            right[part, sign, 0, :, :, inner, :] = cos_sign[inner] * eye
            right[part, sign, 1, :, :, inner, :] = sin_sign[inner] * eye
    right = right.reshape(4, 2 * rows, rows * 2 * share)
    same = np.kron(np.ones((rows, 2 * rows)), np.eye(share)).astype(np.float32)

    def expand(values):
        spread = mm(jnp.asarray(left, BF), values).astype(BF)
        return jnp.concatenate(
            [mm(spread, jnp.asarray(right[i], BF)) * same for i in range(4)], axis=0
        )

    high, low = split_two(both)
    return (expand(high) * keep).astype(BF), (expand(low) * keep).astype(BF)


def times_split(pair, values):
    high, low = split_two(values)
    return mm(pair[0], high) + mm(pair[1], high) + mm(pair[0], low)


def times_split_t(pair, values):
    high, low = split_two(values)
    return mm_t(pair[0], high) + mm_t(pair[1], high) + mm_t(pair[0], low)


GELU_A = math.sqrt(2.0 / math.pi)
GELU_B = 0.044715


def gelu_pair(v):
    square = v * v
    tanh = jnp.tanh(GELU_A * v * (1.0 + GELU_B * square))
    half = 0.5 * (1.0 + tanh)
    slope = half + 0.5 * v * (1.0 - tanh * tanh) * (GELU_A * (1.0 + 3.0 * GELU_B * square))
    return v * half, slope


def block_diagonal(weight):
    blocks, size = weight.shape[0], weight.shape[1]
    spread = jnp.tile(weight.reshape(blocks * size, size), (1, blocks))
    mask = np.kron(np.eye(blocks), np.ones((size, size))).astype(np.bool_)
    return jnp.where(mask, spread, jnp.zeros_like(spread))


def diagonal_blocks(full, blocks, size):
    return jnp.concatenate(
        [full[n * size : (n + 1) * size, n * size : (n + 1) * size] for n in range(blocks)], axis=0
    )


def normalise(values, total, square, width):
    average = total / width
    inverse = lax.rsqrt(square / width - average * average + EPSILON)
    return (values - average) * inverse, inverse


def body(
    field,
    row_group,
    row_valid,
    norm1_gain,
    norm1_bias,
    spec_w1,
    spec_b1,
    spec_w2,
    spec_b2,
    norm2_gain,
    norm2_bias,
    fc1_weight,
    fc1_bias,
    fc2_weight,
    fc2_bias,
    cotangent,
):
    rows_dev, columns, ch = field.shape
    parts, mp = lax.axis_size("lat"), lax.axis_size("mp")
    me = lax.axis_index("lat")
    rows = rows_dev * parts
    full_width = ch * mp
    tokens = rows_dev * columns
    blocks, size = spec_w1.shape[1], spec_w1.shape[2]
    hidden = fc1_weight.shape[1]
    share = -(-HALVES // parts)
    group = 2 * rows_dev * share
    patches = rows * 2 * share

    lon_fine = longitude_constant(LON_FINE, parts, share, rows_dev, columns)
    lon_coarse = longitude_constant(LON_COARSE, parts, share, rows_dev, columns)
    local_group = lax.dynamic_slice_in_dim(row_group, me * rows_dev, rows_dev)
    local_valid = lax.dynamic_slice_in_dim(row_valid, me * rows_dev, rows_dev)
    pick = jnp.broadcast_to(
        (local_group == 0)[None, :, None], (parts, rows_dev, 2 * share)
    ).reshape(-1, 1)
    lon = tuple(
        jnp.where(pick, jnp.asarray(f), jnp.asarray(c))
        for f, c in zip(np_split(lon_fine), np_split(lon_coarse))
    )
    lat = latitude_matrix(row_group, row_valid, rows, rows_dev, share, me * share)
    keep_row = jnp.broadcast_to((local_valid > 0)[:, None], (rows_dev, columns)).reshape(tokens, 1)

    x_low = field.reshape(tokens, ch)
    dy_low = cotangent.reshape(tokens, ch)
    x = x_low.astype(F32)
    dy = dy_low.astype(F32)

    sums = lax.psum(
        jnp.concatenate(
            [jnp.sum(x, axis=1, keepdims=True), jnp.sum(x * x, axis=1, keepdims=True)], axis=1
        ),
        "mp",
    )
    xh1, inv1 = normalise(x, sums[:, :1], sums[:, 1:], full_width)
    u = xh1 * norm1_gain + norm1_bias

    def to_freq(values):
        packed = times_split(lon, values).astype(BF).reshape(parts, group, ch)
        got = lax.all_to_all(packed, "lat", 0, 0, tiled=True)
        return got.reshape(patches, ch)

    def to_freq32(values):
        packed = times_split(lon, values).reshape(parts, group, ch)
        got = lax.all_to_all(packed, "lat", 0, 0, tiled=True)
        return got.reshape(patches, ch)

    w1r, w1i = block_diagonal(spec_w1[0]), block_diagonal(spec_w1[1])
    w2r, w2i = block_diagonal(spec_w2[0]), block_diagonal(spec_w2[1])
    b1 = spec_b1.reshape(2, 1, ch)
    b2 = spec_b2.reshape(2, 1, ch)

    z = to_freq32(u)
    s = times_split(lat, z).astype(BF)
    sr, si = s[:patches], s[patches:]
    a1r = mm(sr, w1r) - mm(si, w1i) + b1[0]
    a1i = mm(sr, w1i) + mm(si, w1r) + b1[1]
    h1r, slope_r = gelu_pair(a1r)
    h1i, slope_i = gelu_pair(a1i)
    h1r, h1i = h1r.astype(BF), h1i.astype(BF)
    a2r = mm(h1r, w2r) - mm(h1i, w2i) + b2[0]
    a2i = mm(h1r, w2i) + mm(h1i, w2r) + b2[1]
    tr, ti = jnp.tanh(a2r / SHRINK), jnp.tanh(a2i / SHRINK)
    shrunk = jnp.concatenate([a2r - SHRINK * tr, a2i - SHRINK * ti], axis=0)
    eo = times_split_t(lat, shrunk).astype(BF).reshape(parts, group, ch)
    eo = lax.all_to_all(eo, "lat", 0, 0, tiled=True).reshape(parts * group, ch)
    filtered = mm_t(lon[0], eo) + mm_t(lon[1], eo)
    x1 = x + filtered + u

    x1_all = lax.all_gather(x1, "mp", axis=1, tiled=True)
    gain2 = lax.all_gather(jnp.stack([norm2_gain, norm2_bias]), "mp", axis=1, tiled=True)
    dy_all = lax.all_gather(dy_low, "mp", axis=1, tiled=True)
    xh2, inv2 = normalise(
        x1_all,
        jnp.sum(x1_all, axis=1, keepdims=True),
        jnp.sum(x1_all * x1_all, axis=1, keepdims=True),
        full_width,
    )
    n = (xh2 * gain2[0] + gain2[1]).astype(BF)
    p = mm(n, fc1_weight) + fc1_bias
    q, slope = gelu_pair(p)
    q = q.astype(BF)
    dp = (mm_nt(dy_all, fc2_weight) * slope).astype(BF)
    out_part = mm(q, fc2_weight)
    dn_part = mm_nt(dp, fc1_weight)
    g_fc1 = mm_t(n, dp)
    g_fc2 = mm_t(dy_all, q)
    g_fc1_bias = jnp.sum(dp.astype(F32), axis=0)
    scaled = dn_part * gain2[0]
    stat2 = lax.psum(
        jnp.concatenate(
            [
                jnp.sum(scaled, axis=1, keepdims=True),
                jnp.sum(scaled * xh2, axis=1, keepdims=True),
            ],
            axis=1,
        ),
        "mp",
    )
    both = jnp.stack([out_part, dn_part]).astype(BF).reshape(2, tokens, mp, ch)
    both = lax.all_to_all(both.transpose(2, 0, 1, 3), "mp", 0, 0, tiled=True)
    both = jnp.sum(both.astype(F32), axis=0)
    out_field = (x1 + both[0] + fc2_bias).astype(BF)
    dn = both[1]

    weights = jnp.stack(
        [g_fc1.reshape(parts, full_width // parts, hidden), g_fc2.reshape(parts, full_width // parts, hidden)],
        axis=1,
    ).astype(BF)
    weights = lax.all_to_all(weights, "lat", 0, 0, tiled=True)
    weights = jnp.sum(weights.astype(F32), axis=0)

    mine = lax.axis_index("mp") * ch
    xh2_own = lax.dynamic_slice_in_dim(xh2, mine, ch, axis=1)
    dx1 = dy + inv2 * (
        dn * norm2_gain - stat2[:, :1] / full_width - xh2_own * (stat2[:, 1:] / full_width)
    )
    g_norm2_gain = jnp.sum(dn * xh2_own, axis=0)
    g_norm2_bias = jnp.sum(dn, axis=0)

    dz = to_freq(jnp.where(keep_row, dx1, 0.0))
    dsh = mm(lat[0], dz) + mm(lat[1], dz)
    dar = (dsh[:patches] * (tr * tr)).astype(BF)
    dai = (dsh[patches:] * (ti * ti)).astype(BF)
    g_w2r = mm_t(h1r, dar) + mm_t(h1i, dai)
    g_w2i = mm_t(h1r, dai) - mm_t(h1i, dar)
    dhr = mm_nt(dar, w2r) + mm_nt(dai, w2i)
    dhi = mm_nt(dai, w2r) - mm_nt(dar, w2i)
    dcr = (dhr * slope_r).astype(BF)
    dci = (dhi * slope_i).astype(BF)
    g_w1r = mm_t(sr, dcr) + mm_t(si, dci)
    g_w1i = mm_t(sr, dci) - mm_t(si, dcr)
    dspectrum = jnp.concatenate(
        [mm_nt(dcr, w1r) + mm_nt(dci, w1i), mm_nt(dci, w1r) - mm_nt(dcr, w1i)], axis=0
    )
    deo = times_split_t(lat, dspectrum).astype(BF).reshape(parts, group, ch)
    g_spec = jnp.concatenate(
        [diagonal_blocks(g, blocks, size) for g in (g_w1r, g_w1i, g_w2r, g_w2i)], axis=0
    )
    spec_rows = g_spec.size // (parts * ch)
    g_spec = g_spec.astype(BF).reshape(parts, spec_rows, ch)
    deo = jnp.concatenate([deo, g_spec], axis=1)
    deo = lax.all_to_all(deo, "lat", 0, 0, tiled=True)
    g_spec = jnp.sum(deo[:, group:].astype(F32), axis=0)
    deo = deo[:, :group].reshape(parts * group, ch)
    du = dx1 + mm_t(lon[0], deo) + mm_t(lon[1], deo)

    scaled = du * norm1_gain
    stat1 = lax.psum(
        jnp.concatenate(
            [
                jnp.sum(scaled, axis=1, keepdims=True),
                jnp.sum(scaled * xh1, axis=1, keepdims=True),
            ],
            axis=1,
        ),
        "mp",
    )
    grad_field = dx1 + inv1 * (
        scaled - stat1[:, :1] / full_width - xh1 * (stat1[:, 1:] / full_width)
    )

    def column_sums(values):
        return jnp.sum(values.astype(F32), axis=0)

    small = [
        column_sums(du * xh1),
        column_sums(du),
        column_sums(dcr),
        column_sums(dci),
        column_sums(dar),
        column_sums(dai),
        g_norm2_gain,
        g_norm2_bias,
        column_sums(dy),
        g_fc1_bias,
    ]
    small = jnp.concatenate(small).reshape(-1, ch)
    tail = jnp.concatenate([g_spec, small], axis=0)
    tail = lax.all_to_all(
        jnp.broadcast_to(tail[None], (parts, *tail.shape)), "lat", 0, 0, tiled=True
    )
    small = jnp.sum(tail[:, spec_rows:], axis=0)
    g_spec = tail[:, :spec_rows].reshape(2, 2, blocks, size, size)
    return (
        out_field.reshape(field.shape),
        grad_field.reshape(field.shape),
        small[0],
        small[1],
        g_spec[0],
        small[2:4].reshape(2, blocks, size),
        g_spec[1],
        small[4:6].reshape(2, blocks, size),
        small[6],
        small[7],
        weights[0],
        small[9:].reshape(hidden),
        weights[1].T,
        small[8],
    )


def solution(mesh):
    placed = (
        P("lat", None, "mp"),
        P(),
        P(),
        P("mp"),
        P("mp"),
        P(None, "mp", None, None),
        P(None, "mp", None),
        P(None, "mp", None, None),
        P(None, "mp", None),
        P("mp"),
        P("mp"),
        P(None, "mp"),
        P("mp"),
        P("mp", None),
        P("mp"),
        P("lat", None, "mp"),
    )
    return jax.shard_map(
        body,
        mesh=mesh,
        in_specs=placed,
        out_specs=(
            P("lat", None, "mp"),
            P("lat", None, "mp"),
            P("mp"),
            P("mp"),
            P(None, "mp", None, None),
            P(None, "mp", None),
            P(None, "mp", None, None),
            P(None, "mp", None),
            P("mp"),
            P("mp"),
            P("lat", "mp"),
            P("mp"),
            P("mp", "lat"),
            P("mp"),
        ),
        check_vma=False,
    )
```

```python
import functools
import math

import jax
import jax.numpy as jnp
import numpy as np
from jax import lax
from jax.experimental import pallas as pl
from jax.experimental.pallas import tpu as pltpu
from jax.sharding import PartitionSpec as P

LON_FINE = 180
LON_COARSE = 45
GROUPS = 8
EPSILON = 1e-05
SHRINK = 0.01
HALVES = LON_FINE // 2 + 1
BF = jnp.bfloat16
F32 = jnp.float32


def split_two(values):
    high = lax.reduce_precision(values, 8, 7)
    return high.astype(BF), (values - high).astype(BF)


def mm(left, right):
    return lax.dot_general(left, right, (((1,), (0,)), ((), ())), preferred_element_type=F32)


def mm_t(left, right):
    return lax.dot_general(left, right, (((0,), (0,)), ((), ())), preferred_element_type=F32)


def mm_nt(left, right):
    return lax.dot_general(left, right, (((1,), (1,)), ((), ())), preferred_element_type=F32)


def np_split(values):
    high = values.astype(jnp.bfloat16)
    low = (values - high.astype(np.float32)).astype(jnp.bfloat16)
    return high, low


def row_tables(row_group, row_valid):
    member = (row_group[:, None] == jnp.arange(GROUPS, dtype=jnp.int32)[None, :]).astype(
        jnp.int32
    ) * row_valid[:, None]
    counts = jnp.sum(member, axis=0)
    before = jnp.cumsum(member, axis=0) - member
    offset = jnp.sum(before * member, axis=1)
    length = jnp.maximum(jnp.sum(member * counts[None, :], axis=1), 1)
    return (offset, length)


def latitude_tables(row_group, row_valid):
    offset, length = row_tables(row_group, row_valid)
    phases = offset[:, None] * offset[None, :] % length[:, None]
    lengths = length[:, None].astype(F32)
    angles = 2.0 * math.pi * phases.astype(F32) / lengths
    kept = (
        (row_group[:, None] == row_group[None, :])
        & (row_valid[:, None] > 0)
        & (row_valid[None, :] > 0)
    ).astype(F32) * lax.rsqrt(lengths)
    return kept * jnp.cos(angles), kept * jnp.sin(angles)


PIECES = 3
GELU_A = math.sqrt(2.0 / math.pi)
GELU_B = 0.044715


def longitude_tables(parts, share, rows_dev, columns, padded):
    freq = np.arange(parts * share).reshape(parts, share)
    cols = np.arange(columns)
    pairs = []
    for width in (LON_COARSE, LON_FINE):
        angles = 2.0 * np.pi * ((freq[..., None] * cols) % width) / width
        inside = (freq[..., None] * 2 <= width) & (cols < width)
        scale = inside / np.sqrt(width)
        pairs.append(np.stack([scale * np.cos(angles), -scale * np.sin(angles)], axis=1))
    full = np.zeros((2**rows_dev, parts, rows_dev, 2, share, rows_dev, padded), np.float32)
    for choice in range(2**rows_dev):
        for r in range(rows_dev):
            full[choice, :, r, :, :, r, :columns] = pairs[(choice >> r) & 1]
    return np_split(full.reshape(2**rows_dev, parts * rows_dev * 2 * share, rows_dev * padded))


def latitude_spread(rows, share):
    left = np.kron(np.eye(rows), np.ones((share, 1)))
    right = np.zeros((2, 2, 2, rows, rows, 2, share))
    signs = {
        (0, 0): ((1, 0), (0, 1)),
        (1, 0): ((0, 1), (-1, 0)),
        (0, 1): ((1, 0), (0, -1)),
        (1, 1): ((0, -1), (-1, 0)),
    }
    eye = np.eye(rows)[:, :, None]
    for (part, sign), (cos_sign, sin_sign) in signs.items():
        for inner in range(2):
            right[part, sign, 0, :, :, inner, :] = cos_sign[inner] * eye
            right[part, sign, 1, :, :, inner, :] = sin_sign[inner] * eye
    same = np.kron(np.ones((rows, 2 * rows)), np.eye(share))
    low = jnp.bfloat16
    return left.astype(low), right.reshape(4, 2 * rows, -1).astype(low), same.astype(low)


def split_in(values):
    high = values.astype(BF)
    return high, (values - high.astype(F32)).astype(BF)


def times(pair, values):
    high, low = split_in(values)
    return mm(pair[0], high) + mm(pair[1], high) + mm(pair[0], low)


def times_t(pair, values):
    high, low = split_in(values)
    return mm_t(pair[0], high) + mm_t(pair[1], high) + mm_t(pair[0], low)


def gelu_pair(v):
    square = v * v
    tanh = jnp.tanh(GELU_A * v * (1.0 + GELU_B * square))
    half = 0.5 * (1.0 + tanh)
    slope = half + 0.5 * v * (1.0 - tanh * tanh) * (GELU_A * (1.0 + 3.0 * GELU_B * square))
    return v * half, slope


def put_rows(ref, value, r, padded):
    ref[r * padded : r * padded + value.shape[0], :] = value


def column_sum(values):
    return jnp.sum(values, axis=0, keepdims=True)


def norm_one_kernel(columns, padded, groups, all_ref, gain, bias, high, low, freq, base, xh, inverse, pad, tables, sems):
    mp, rows_dev = all_ref.shape[0], all_ref.shape[1]
    width = mp * all_ref.shape[3]
    first = lax.axis_index("lat") * rows_dev
    choice = jnp.int32(0)
    for r in range(rows_dev):
        choice = choice + jnp.where(groups[first + r] == 0, 1 << r, 0).astype(jnp.int32)
    copies = [
        pltpu.make_async_copy(src.at[choice], tables.at[i], sems.at[i])
        for i, src in enumerate((high, low))
    ]
    for copy in copies:
        copy.start()
    pad[...] = jnp.zeros_like(pad)
    for r in range(rows_dev):
        for m in range(mp):
            pad[m, r * padded : r * padded + columns, :] = all_ref[m, r].astype(F32)
    total = sum(jnp.sum(pad[m], axis=1, keepdims=True) for m in range(mp))
    average = total / width
    spread = sum(
        jnp.sum((pad[m] - average) * (pad[m] - average), axis=1, keepdims=True) for m in range(mp)
    )
    inv = lax.rsqrt(spread / width + EPSILON)
    x = pad[lax.axis_index("mp")]
    hat = (x - average) * inv
    u = hat * gain[...] + bias[...]
    base[...] = x + u
    xh[...] = hat
    inverse[...] = inv
    for copy in copies:
        copy.wait()
    freq[...] = times((tables[0], tables[1]), u)


def latitude_kernel(share, tables, left, right, same, keep, high_out, low_out):
    high, low = split_in(tables[...])
    for values, out in ((high, high_out), (low, low_out)):
        spread = mm(left[...], values).astype(BF)
        n = left.shape[0]
        for i in range(4):
            block = mm(spread, right[i]) * same[...].astype(F32)
            if i % 2:
                block = block * keep[...]
            out[i * n : (i + 1) * n, :] = block.astype(BF)


def block_mask(blocks, size):
    shape = (blocks * size, blocks * size)
    row = lax.broadcasted_iota(jnp.int32, shape, 0)
    col = lax.broadcasted_iota(jnp.int32, shape, 1)
    inside = None
    for n in range(blocks):
        one = (row >= n * size) & (row < (n + 1) * size) & (col >= n * size) & (col < (n + 1) * size)
        inside = one if inside is None else inside | one
    return inside


def diagonal(packed, blocks, size):
    whole = jnp.concatenate([packed.astype(F32)] * blocks, axis=0)
    return jnp.where(block_mask(blocks, size), whole, 0.0).astype(BF)


def gather_blocks(full, blocks, size):
    col = lax.broadcasted_iota(jnp.int32, (size, blocks * size), 1)
    out = None
    for n in range(blocks):
        piece = full[n * size : (n + 1) * size, :]
        piece = jnp.where((col >= n * size) & (col < (n + 1) * size), piece, 0.0)
        out = piece if out is None else out + piece
    return out


def filter_kernel(blocks, size, z, high, low, weights, biases, eo, s_out, h_out, slope_out, gate_out):
    w1r, w1i, w2r, w2i = (diagonal(weights[i], blocks, size) for i in range(4))
    n = z.shape[0]
    s = times((high[...], low[...]), z[...]).astype(BF)
    s_out[...] = s
    sr, si = s[:n], s[n:]
    a1r = mm(sr, w1r) - mm(si, w1i) + biases[0:1, :]
    a1i = mm(sr, w1i) + mm(si, w1r) + biases[1:2, :]
    hr, slope = gelu_pair(a1r)
    hr = hr.astype(BF)
    slope_out[:n, :] = slope
    hi, slope = gelu_pair(a1i)
    hi = hi.astype(BF)
    slope_out[n:, :] = slope
    h_out[:n, :] = hr
    h_out[n:, :] = hi
    a2r = mm(hr, w2r) - mm(hi, w2i) + biases[2:3, :]
    a2i = mm(hr, w2i) + mm(hi, w2r) + biases[3:4, :]
    tr = jnp.tanh(a2r * (1.0 / SHRINK))
    ti = jnp.tanh(a2i * (1.0 / SHRINK))
    gate_out[:n, :] = tr * tr
    gate_out[n:, :] = ti * ti
    rh, rl = split_in(a2r - SHRINK * tr)
    ih, il = split_in(a2i - SHRINK * ti)
    out = mm_t(high[:n, :], rh) + mm_t(low[:n, :], rh) + mm_t(high[:n, :], rl)
    out += mm_t(high[n:, :], ih) + mm_t(low[n:, :], ih) + mm_t(high[n:, :], il)
    eo[...] = out.astype(BF)


def mix_kernel(choice, eo, high, low, base, x1):
    got = eo[...]
    x1[...] = base[...] + mm_t(high[0], got) + mm_t(low[0], got)


def second_norm(parts_of):
    width = len(parts_of) * parts_of[0].shape[1]
    total = sum(jnp.sum(v, axis=1, keepdims=True) for v in parts_of)
    average = total / width
    spread = sum(jnp.sum((v - average) * (v - average), axis=1, keepdims=True) for v in parts_of)
    return average, lax.rsqrt(spread / width + EPSILON)


def mlp_kernel(columns, padded, orders, *refs):
    mp, pieces = refs[0].shape[0], len(orders)
    dy_all, norms, places, w1, b1, w2, own = refs[:7]
    others = refs[7 : 6 + mp]
    send = refs[6 + mp]
    grads = refs[7 + mp : 7 + mp + 2 * pieces]
    gb1, n_s, nt_s, dy_s, dyt_s, x1_s, out_acc, dn_acc, pad = refs[7 + mp + 2 * pieces :]
    step, steps = pl.program_id(0), pl.num_programs(0)
    ch, width = own.shape[1], w1.shape[0]
    rows_dev = dy_all.shape[1]

    @pl.when(step == 0)
    def _():
        mine = lax.axis_index("mp")
        x1_s[mine] = own[...]
        for i, other in enumerate(others):
            x1_s[lax.rem(mine + 1 + i, mp)] = other[...]
        average, inv = second_norm([x1_s[m] for m in range(mp)])
        for m in range(mp):
            lanes = slice(m * ch, (m + 1) * ch)
            hat = (x1_s[m] - average) * inv
            n_s[:, lanes] = (hat * norms[m, 0:1, :] + norms[m, 1:2, :]).astype(BF)
            pad[...] = jnp.zeros_like(pad)
            for r in range(rows_dev):
                pad[r * padded : r * padded + columns, :] = dy_all[m, r].astype(F32)
            dy_s[:, lanes] = pad[...].astype(BF)
        me = lax.axis_index("lat")
        lane = lax.broadcasted_iota(jnp.int32, (width, width), 1)
        share = width // lax.axis_size("lat")
        target = (places[:, 0:1] ^ me) * share + places[:, 1:2]
        move = jnp.where(lane == target, 1.0, 0.0).astype(BF)
        nt_s[...] = mm_nt(move, n_s[...]).astype(BF)
        dyt_s[...] = mm_nt(move, dy_s[...]).astype(BF)
        out_acc[...] = jnp.zeros_like(out_acc)
        dn_acc[...] = jnp.zeros_like(dn_acc)

    p = mm(n_s[...], w1[...]) + b1[...]
    q, slope = gelu_pair(p)
    q = q.astype(BF)
    dp = (mm_nt(dy_s[...], w2[...]) * slope).astype(BF)
    dn_acc[...] += mm_nt(dp, w1[...])
    out_acc[...] += mm(q, w2[...])
    gb1[...] = column_sum(dp.astype(F32))
    both = (mm(nt_s[...], dp), mm(dyt_s[...], q))
    for piece, bits in enumerate(orders):
        kept, away = grads[2 * piece : 2 * piece + 2]
        count = len(bits)
        rows = width >> count

        @pl.when((step * pieces) // steps == piece)
        def _():
            for i, grad in enumerate(both):
                for spot in range(2**count):
                    who = sum(((spot >> (count - 1 - b)) & 1) * bit for b, bit in enumerate(bits))
                    block = grad[who * rows : (who + 1) * rows, :].astype(BF)
                    at = (spot % 2 ** (count - 1)) * rows
                    (away if spot >> (count - 1) else kept)[i, at : at + rows, :] = block

    @pl.when(step == steps - 1)
    def _():
        halves = [x1_s[m] for m in range(mp)]
        average, inv = second_norm(halves)
        plain, cross = 0.0, 0.0
        for m in range(mp):
            lanes = slice(m * ch, (m + 1) * ch)
            part = dn_acc[:, lanes]
            scaled = part * norms[m, 0:1, :]
            plain += jnp.sum(scaled, axis=1, keepdims=True)
            cross += jnp.sum(scaled * ((halves[m] - average) * inv), axis=1, keepdims=True)
            send[m, :, :ch] = out_acc[:, lanes].astype(BF)
            send[m, :, ch : 2 * ch] = part.astype(BF)
        spot = lax.broadcasted_iota(jnp.int32, (plain.shape[0], 128), 1)
        stat = jnp.zeros(spot.shape, BF)
        for first, value in ((0, plain), (3, cross)):
            for i in range(3):
                term = value.astype(BF)
                value = value - term.astype(F32)
                stat = jnp.where(spot == first + i, term.astype(F32), stat.astype(F32)).astype(BF)
        for m in range(mp):
            send[m, :, 2 * ch :] = stat


def back_mix_kernel(columns, padded, choice, got, dy, gain, bias2, high, low, own, *refs):
    mp, ch = got.shape[0], own.shape[1]
    others = refs[: mp - 1]
    out_field, dx1, freq, sums, pad = refs[mp - 1 :]
    rows_dev = dy.shape[0]
    width = mp * ch
    x1 = own[...]
    average, inv = second_norm([x1] + [other[...] for other in others])
    hat = (x1 - average) * inv
    total = sum(got[m].astype(F32) for m in range(mp))
    out = x1 + total[:, :ch] + bias2[...]
    dn = total[:, ch : 2 * ch]
    pad[...] = jnp.zeros_like(pad)
    for r in range(rows_dev):
        out_field[r] = out[r * padded : r * padded + columns, :].astype(BF)
        put_rows(pad, dy[r].astype(F32), r, padded)
    grad = pad[...]
    sums[0:1, :] = column_sum(dn * hat)
    sums[1:2, :] = column_sum(dn)
    sums[2:3, :] = column_sum(grad)
    sums[3:8, :] = jnp.zeros((5, ch), F32)
    stats = total[:, 2 * ch : 2 * ch + 128]
    plain = (stats[:, 0:1] + stats[:, 1:2] + stats[:, 2:3]) / width
    cross = (stats[:, 3:4] + stats[:, 4:5] + stats[:, 5:6]) / width
    grad = grad + inv * (dn * gain[...] - plain - hat * cross)
    dx1[...] = grad
    freq[...] = times((high[0], low[0]), grad).astype(BF)


def filter_back_kernel(blocks, size, group, dz, high, low, weights, s_ref, h_ref, slope_ref, gate_ref, mlp_sums, hidden_sums, send, rows, grads_s, sums_s):
    w1r, w1i, w2r, w2i = (diagonal(weights[i], blocks, size) for i in range(4))
    n = dz.shape[0]
    dsh = mm(high[...], dz[...]) + mm(low[...], dz[...])
    da = dsh * gate_ref[...]
    dar, dai = da[:n].astype(BF), da[n:].astype(BF)
    hr, hi = h_ref[:n, :], h_ref[n:, :]
    dcr = ((mm_nt(dar, w2r) + mm_nt(dai, w2i)) * slope_ref[:n, :]).astype(BF)
    dci = ((mm_nt(dai, w2r) - mm_nt(dar, w2i)) * slope_ref[n:, :]).astype(BF)
    rh, rl = split_in(mm_nt(dcr, w1r) + mm_nt(dci, w1i))
    ih, il = split_in(mm_nt(dci, w1r) - mm_nt(dcr, w1i))
    out = mm_t(high[:n, :], rh) + mm_t(low[:n, :], rh) + mm_t(high[:n, :], rl)
    out += mm_t(high[n:, :], ih) + mm_t(low[n:, :], ih) + mm_t(high[n:, :], il)
    parts = rows.shape[0]
    for d in range(parts):
        rows[d, :group, :] = out[d * group : (d + 1) * group, :]
    sr, si = s_ref[:n, :], s_ref[n:, :]
    grads = (
        mm_t(sr, dcr) + mm_t(si, dci),
        mm_t(sr, dci) - mm_t(si, dcr),
        mm_t(hr, dar) + mm_t(hi, dai),
        mm_t(hr, dai) - mm_t(hi, dar),
    )
    for i, grad in enumerate(grads):
        grads_s[i * size : (i + 1) * size, :] = gather_blocks(grad, blocks, size)
    sums_s[...] = jnp.zeros_like(sums_s)
    for i, grad in enumerate((dcr, dci, dar, dai)):
        sums_s[i : i + 1, :] = column_sum(grad.astype(F32))
    sums_s[4:7, :] = mlp_sums[0:3, :]
    sums_s[7 : 7 + hidden_sums.shape[0], :] = hidden_sums[...]
    share = grads_s.shape[0] // parts
    at = group + share
    for d in range(parts):
        rows[d, group:at, :] = grads_s[d * share : (d + 1) * share, :]
        row = sums_s[d : d + 1, :]
        first = row.astype(BF).astype(F32)
        rows[d, at : at + 1, :] = first
        rows[d, at + 1 : at + 2, :] = row - first
        if at + 2 < rows.shape[1]:
            rows[d, at + 2 :, :] = jnp.zeros((rows.shape[1] - at - 2, rows.shape[2]), F32)
    send[...] = rows[...].astype(BF)


def back_norm_kernel(group, share, choice, got, high, low, dx1, xh, gain, du_out, stat, tail, tail_s):
    parts, _, ch = got.shape
    every = got[...].astype(F32)
    deo = every[:, :group, :].reshape(parts * group, ch).astype(BF)
    at = group + share
    tail_s[...] = jnp.zeros_like(tail_s)
    tail_s[:share, :] = jnp.sum(every[:, group:at, :], axis=0)
    total = jnp.sum(every[:, at : at + 1, :], axis=0) + jnp.sum(every[:, at + 1 : at + 2, :], axis=0)
    du = dx1[...] + mm_t(high[0], deo) + mm_t(low[0], deo)
    du_out[...] = du
    hat = xh[...]
    scaled = du * gain[...]
    spot = lax.broadcasted_iota(jnp.int32, stat.shape, 1)
    stat[...] = jnp.where(
        spot == 0,
        jnp.sum(scaled, axis=1, keepdims=True),
        jnp.sum(scaled * hat, axis=1, keepdims=True),
    )
    for i, row in enumerate((total, column_sum(du * hat), column_sum(du))):
        first = row.astype(BF).astype(F32)
        tail_s[share + 2 * i : share + 2 * i + 1, :] = first
        tail_s[share + 2 * i + 1 : share + 2 * i + 2, :] = row - first
    whole_tail = tail_s[...].astype(BF)
    for d in range(parts):
        tail[d] = whole_tail


def last_kernel(columns, padded, width, du, dx1, xh, inverse, gain, stats, out):
    plain = stats[:, 0:1] / width
    cross = stats[:, 1:2] / width
    value = dx1[...] + inverse[...] * (du[...] * gain[...] - plain - xh[...] * cross)
    for r in range(out.shape[0]):
        out[r] = value[r * padded : r * padded + columns, :]


def whole(shape, extra=0):
    return pl.BlockSpec(shape, lambda *_: (0,) * len(shape))


def run(kernel, outs, args, scratch=(), picked=(), choice=None, flops=0, limit=56):
    moved = sum(math.prod(a.shape) * a.dtype.itemsize for a in args)
    moved += sum(math.prod(o.shape) * o.dtype.itemsize for o in outs)
    params = pltpu.CompilerParams(vmem_limit_bytes=limit * 2**20)
    cost = pl.CostEstimate(flops=flops, bytes_accessed=moved, transcendentals=0)
    out_shape = [jax.ShapeDtypeStruct(o.shape, o.dtype) for o in outs]
    if choice is None:
        return pl.pallas_call(
            kernel,
            out_shape=out_shape,
            in_specs=[pl.BlockSpec(memory_space=pltpu.VMEM)] * len(args),
            out_specs=[pl.BlockSpec(memory_space=pltpu.VMEM)] * len(outs),
            scratch_shapes=list(scratch),
            compiler_params=params,
            cost_estimate=cost,
        )(*args)
    specs = [
        pl.BlockSpec((1, *a.shape[1:]), lambda i, c: (c[0], 0, 0)) if i in picked else whole(a.shape)
        for i, a in enumerate(args)
    ]
    return pl.pallas_call(
        kernel,
        out_shape=out_shape,
        grid_spec=pltpu.PrefetchScalarGridSpec(
            num_scalar_prefetch=1,
            grid=(1,),
            in_specs=specs,
            out_specs=[whole(o.shape) for o in outs],
            scratch_shapes=list(scratch),
        ),
        compiler_params=params,
        cost_estimate=cost,
    )(choice, *args)


def halve(kept, away, bit, parts):
    got = lax.ppermute(away, "lat", [(d, d ^ bit) for d in range(parts)])
    half = kept.shape[1] // 2
    away = (kept[:, half:].astype(F32) + got[:, half:].astype(F32)).astype(BF)
    kept = kept[:, :half].astype(F32) + got[:, :half].astype(F32)
    return kept, away


def after(value, arrays):
    return lax.optimization_barrier((value, arrays))


def body(
    field,
    row_group,
    row_valid,
    norm1_gain,
    norm1_bias,
    spec_w1,
    spec_b1,
    spec_w2,
    spec_b2,
    norm2_gain,
    norm2_bias,
    fc1_weight,
    fc1_bias,
    fc2_weight,
    fc2_bias,
    cotangent,
):
    rows_dev, columns, ch = field.shape
    parts, mp = lax.axis_size("lat"), lax.axis_size("mp")
    me = lax.axis_index("lat")
    rows = rows_dev * parts
    full_width = ch * mp
    padded = -(-columns // 16) * 16
    tokens = rows_dev * padded
    blocks, size = spec_w1.shape[1], spec_w1.shape[2]
    hidden = fc1_weight.shape[1]
    share = -(-HALVES // parts)
    group = 2 * rows_dev * share
    patches = parts * group

    def f32(*shape):
        return jax.ShapeDtypeStruct(shape, F32)

    def bf(*shape):
        return jax.ShapeDtypeStruct(shape, BF)

    lon = [jnp.asarray(t) for t in longitude_tables(parts, share, rows_dev, columns, padded)]
    local_group = lax.dynamic_slice_in_dim(row_group, me * rows_dev, rows_dev)
    choice = sum(
        jnp.where(local_group[r] == 0, 1 << r, 0) for r in range(rows_dev)
    ).astype(jnp.int32).reshape(1)
    gain1, bias1 = norm1_gain.reshape(1, ch), norm1_bias.reshape(1, ch)

    field_all = lax.all_gather(field, "mp", axis=0)
    table = pltpu.VMEM((2, patches, tokens), BF)
    freq, base, xh1, inv1 = pl.pallas_call(
        functools.partial(norm_one_kernel, columns, padded),
        out_shape=[f32(patches, ch), f32(tokens, ch), f32(tokens, ch), f32(tokens, 1)],
        in_specs=[pl.BlockSpec(memory_space=pltpu.SMEM)]
        + [pl.BlockSpec(memory_space=pltpu.VMEM)] * 3
        + [pl.BlockSpec(memory_space=pl.ANY)] * 2,
        out_specs=[pl.BlockSpec(memory_space=pltpu.VMEM)] * 4,
        scratch_shapes=[
            pltpu.VMEM((mp, tokens, ch), F32),
            table,
            pltpu.SemaphoreType.DMA((2,)),
        ],
        compiler_params=pltpu.CompilerParams(vmem_limit_bytes=56 * 2**20),
    )(row_group, field_all, gain1, bias1, *lon)

    def to_other(values, rows_each):
        return lax.all_to_all(values.reshape(parts, rows_each, ch), "lat", 0, 0, tiled=True)

    z = to_other(freq, group).reshape(patches, ch)

    cos_mat, sin_mat = latitude_tables(row_group, row_valid)
    width = jnp.where(row_group == 0, LON_FINE, LON_COARSE).astype(jnp.int32)
    here = me * share + jnp.arange(share, dtype=jnp.int32)
    lone = (here[None, :] == 0) | (2 * here[None, :] == width[:, None])
    keep = (1.0 - lone.astype(F32)).reshape(rows * share, 1)
    lat = run(
        functools.partial(latitude_kernel, share),
        [bf(2 * patches, patches)] * 2,
        [
            jnp.concatenate([cos_mat, sin_mat], axis=1),
            *(jnp.asarray(t) for t in latitude_spread(rows, share)),
            keep,
        ],
    )
    spec = jnp.stack([spec_w1, spec_w2]).transpose(0, 1, 3, 2, 4).reshape(4, size, ch)
    spec_bias = jnp.concatenate([spec_b1.reshape(2, ch), spec_b2.reshape(2, ch)], axis=0)
    norms = lax.all_gather(jnp.stack([norm2_gain, norm2_bias]), "mp", axis=0)
    dy_all = lax.all_gather(cotangent, "mp", axis=0)
    z, norms, dy_all = lax.optimization_barrier((z, norms, dy_all))

    eo, s, h, slope, gate = run(
        functools.partial(filter_kernel, blocks, size),
        [bf(patches, ch), bf(2 * patches, ch), bf(2 * patches, ch), f32(2 * patches, ch), f32(2 * patches, ch)],
        [z, *lat, spec, spec_bias],
    )
    eo = to_other(eo, group).reshape(patches, ch)
    (x1,) = run(mix_kernel, [f32(tokens, ch)], [eo, *lon, base], (), (1, 2), choice)

    others = [
        lax.ppermute(x1, "mp", [((d + i) % mp, d) for d in range(mp)]) for i in range(1, mp)
    ]
    chunk = 256
    steps = hidden // chunk
    bits = [1 << b for b in range(parts.bit_length() - 1)]
    orders = [bits[i:3] + bits[:i] + bits[3:] for i in range(3)]
    pieces = len(orders)
    each = steps // pieces
    grad_specs = [
        pl.BlockSpec(
            (2, full_width // 2, chunk),
            functools.partial(lambda p, i: (0, 0, jnp.clip(i - p * each, 0, each - 1)), p),
        )
        for p in range(pieces)
        for _ in range(2)
    ]
    share_rows = full_width // parts
    places = np.stack(
        [np.arange(full_width) // share_rows, np.arange(full_width) % share_rows], axis=1
    ).astype(np.int32)
    send, *grads, g_fc1_bias = pl.pallas_call(
        functools.partial(mlp_kernel, columns, padded, orders),
        out_shape=[
            bf(mp, tokens, 2 * ch + 128),
            *[bf(2, full_width // 2, hidden // pieces)] * (2 * pieces),
            f32(1, hidden),
        ],
        grid=(steps,),
        in_specs=[
            whole(dy_all.shape),
            whole(norms.shape),
            whole((full_width, 2)),
            pl.BlockSpec((full_width, chunk), lambda i: (0, i)),
            pl.BlockSpec((1, chunk), lambda i: (0, i)),
            pl.BlockSpec((chunk, full_width), lambda i: (i, 0)),
            *[whole((tokens, ch))] * mp,
        ],
        out_specs=[
            whole((mp, tokens, 2 * ch + 128)),
            *grad_specs,
            pl.BlockSpec((1, chunk), lambda i: (0, i)),
        ],
        scratch_shapes=[
            pltpu.VMEM((tokens, full_width), BF),
            pltpu.VMEM((full_width, tokens), BF),
            pltpu.VMEM((tokens, full_width), BF),
            pltpu.VMEM((full_width, tokens), BF),
            pltpu.VMEM((mp, tokens, ch), F32),
            pltpu.VMEM((tokens, full_width), F32),
            pltpu.VMEM((tokens, full_width), F32),
            pltpu.VMEM((tokens, ch), F32),
        ],
        compiler_params=pltpu.CompilerParams(vmem_limit_bytes=56 * 2**20),
        cost_estimate=pl.CostEstimate(
            flops=12 * tokens * full_width * hidden, bytes_accessed=16 * 2**20, transcendentals=0
        ),
    )(
        dy_all,
        norms,
        jnp.asarray(places),
        fc1_weight,
        fc1_bias.reshape(1, hidden),
        fc2_weight,
        x1,
        *others,
    )
    got = lax.all_to_all(send, "mp", 0, 0, tiled=True)
    def exchange(states, turn):
        return [halve(*state, order[turn], parts) for state, order in zip(states, orders)]

    sums = exchange([grads[2 * p : 2 * p + 2] for p in range(pieces)], 0)

    out_field, dx1, dfreq, sums2 = run(
        functools.partial(back_mix_kernel, columns, padded),
        [bf(rows_dev, columns, ch), f32(tokens, ch), bf(patches, ch), f32(8, ch)],
        [got, cotangent, norm2_gain.reshape(1, ch), fc2_bias.reshape(1, ch), *lon, x1, *others],
        [pltpu.VMEM((tokens, ch), F32)],
        (4, 5),
        choice,
    )

    dz = to_other(dfreq, group).reshape(patches, ch)
    dz, sums = after(dz, sums)
    sums = exchange(sums, 1)
    spec_rows = 4 * size // parts
    send_rows = -(-(group + spec_rows + 2) // 8) * 8
    (sent,) = run(
        functools.partial(filter_back_kernel, blocks, size, group),
        [bf(parts, send_rows, ch)],
        [dz, *lat, spec, s, h, slope, gate, sums2, g_fc1_bias.reshape(-1, ch)],
        [
            pltpu.VMEM((parts, send_rows, ch), F32),
            pltpu.VMEM((4 * size, ch), F32),
            pltpu.VMEM((max(parts, 16), ch), F32),
        ],
    )
    sent, sums = after(sent, sums)
    sums = exchange(sums, 2)
    sent = lax.all_to_all(sent, "lat", 0, 0, tiled=True)
    sent, sums = after(sent, sums)
    kept, away = (jnp.concatenate([state[i] for state in sums], axis=2) for i in range(2))
    for bit in bits[3:-1]:
        kept, away = halve(kept, away, bit, parts)
    got_last = lax.ppermute(away, "lat", [(d, d ^ bits[-1]) for d in range(parts)])
    tail_rows = -(-(spec_rows + 6) // 16) * 16
    du, stat1, tail = run(
        functools.partial(back_norm_kernel, group, spec_rows),
        [f32(tokens, ch), f32(tokens, 2), bf(parts, tail_rows, ch)],
        [sent, *lon, dx1, xh1, gain1],
        [pltpu.VMEM((tail_rows, ch), F32)],
        (1, 2),
        choice,
    )
    stat1 = lax.psum(stat1, "mp")
    stat1, got_last = after(stat1, got_last)
    weights = kept + got_last.astype(F32)
    (grad_field,) = run(
        functools.partial(last_kernel, columns, padded, full_width),
        [f32(rows_dev, columns, ch)],
        [du, dx1, xh1, inv1, gain1, stat1],
    )

    tail = lax.all_to_all(tail, "lat", 0, 0, tiled=True).astype(F32)
    g_spec = tail[:, :spec_rows].reshape(2, 2, size, blocks, size).transpose(0, 1, 3, 2, 4)
    pairs = tail[:, spec_rows : spec_rows + 6].reshape(parts, 3, 2, ch).sum(axis=2)
    small = pairs[:, 0]
    norm1 = pairs[:, 1:].sum(axis=0)
    return (
        out_field,
        grad_field,
        norm1[0],
        norm1[1],
        g_spec[0],
        small[0:2].reshape(2, blocks, size),
        g_spec[1],
        small[2:4].reshape(2, blocks, size),
        small[4],
        small[5],
        weights[0],
        small[7 : 7 + hidden // ch].reshape(hidden),
        weights[1].T,
        small[6],
    )


def solution(mesh):
    placed = (
        P("lat", None, "mp"),
        P(),
        P(),
        P("mp"),
        P("mp"),
        P(None, "mp", None, None),
        P(None, "mp", None),
        P(None, "mp", None, None),
        P(None, "mp", None),
        P("mp"),
        P("mp"),
        P(None, "mp"),
        P("mp"),
        P("mp", None),
        P("mp"),
        P("lat", None, "mp"),
    )
    return jax.shard_map(
        body,
        mesh=mesh,
        in_specs=placed,
        out_specs=(
            P("lat", None, "mp"),
            P("lat", None, "mp"),
            P("mp"),
            P("mp"),
            P(None, "mp", None, None),
            P(None, "mp", None),
            P(None, "mp", None, None),
            P(None, "mp", None),
            P("mp"),
            P("mp"),
            P("lat", "mp"),
            P("mp"),
            P("mp", "lat"),
            P("mp"),
        ),
        check_vma=False,
    )
```

```python
import functools
import math

import jax
import jax.numpy as jnp
import numpy as np
from jax import lax
from jax.experimental.layout import Layout, with_layout_constraint
from jax.experimental import pallas as pl
from jax.experimental.pallas import tpu as pltpu
from jax.sharding import PartitionSpec as P

LON_FINE = 180
LON_COARSE = 45
GROUPS = 8
EPSILON = 1e-05
SHRINK = 0.01
HALVES = LON_FINE // 2 + 1
BF = jnp.bfloat16
F32 = jnp.float32


def split_two(values):
    high = lax.reduce_precision(values, 8, 7)
    return high.astype(BF), (values - high).astype(BF)


def mm(left, right):
    return lax.dot_general(left, right, (((1,), (0,)), ((), ())), preferred_element_type=F32)


def mm_t(left, right):
    return lax.dot_general(left, right, (((0,), (0,)), ((), ())), preferred_element_type=F32)


def mm_nt(left, right):
    return lax.dot_general(left, right, (((1,), (1,)), ((), ())), preferred_element_type=F32)


def np_split(values):
    high = values.astype(jnp.bfloat16)
    low = (values - high.astype(np.float32)).astype(jnp.bfloat16)
    return high, low


def row_tables(row_group, row_valid):
    member = (row_group[:, None] == jnp.arange(GROUPS, dtype=jnp.int32)[None, :]).astype(
        jnp.int32
    ) * row_valid[:, None]
    counts = jnp.sum(member, axis=0)
    before = jnp.cumsum(member, axis=0) - member
    offset = jnp.sum(before * member, axis=1)
    length = jnp.maximum(jnp.sum(member * counts[None, :], axis=1), 1)
    return (offset, length)


def latitude_tables(row_group, row_valid):
    offset, length = row_tables(row_group, row_valid)
    phases = offset[:, None] * offset[None, :] % length[:, None]
    lengths = length[:, None].astype(F32)
    angles = 2.0 * math.pi * phases.astype(F32) / lengths
    kept = (
        (row_group[:, None] == row_group[None, :])
        & (row_valid[:, None] > 0)
        & (row_valid[None, :] > 0)
    ).astype(F32) * lax.rsqrt(lengths)
    return kept * jnp.cos(angles), kept * jnp.sin(angles)


CHUNK = 512
GELU_A = math.sqrt(2.0 / math.pi)
GELU_B = 0.044715


def longitude_tables(parts, share, rows_dev, columns, padded):
    freq = np.arange(parts * share).reshape(parts, share)
    cols = np.arange(columns)
    pairs = []
    for width in (LON_COARSE, LON_FINE):
        angles = 2.0 * np.pi * ((freq[..., None] * cols) % width) / width
        inside = (freq[..., None] * 2 <= width) & (cols < width)
        scale = inside / np.sqrt(width)
        pairs.append(np.stack([scale * np.cos(angles), -scale * np.sin(angles)], axis=1))
    full = np.zeros((2**rows_dev, parts, rows_dev, 2, share, rows_dev, padded), np.float32)
    for choice in range(2**rows_dev):
        for r in range(rows_dev):
            full[choice, :, r, :, :, r, :columns] = pairs[(choice >> r) & 1]
    return np_split(full.reshape(2**rows_dev, parts * rows_dev * 2 * share, rows_dev * padded))


def latitude_spread(rows, share):
    left = np.kron(np.eye(rows), np.ones((share, 1)))
    right = np.zeros((2, 2, 2, rows, rows, 2, share))
    signs = {
        (0, 0): ((1, 0), (0, 1)),
        (1, 0): ((0, 1), (-1, 0)),
        (0, 1): ((1, 0), (0, -1)),
        (1, 1): ((0, -1), (-1, 0)),
    }
    eye = np.eye(rows)[:, :, None]
    for (part, sign), (cos_sign, sin_sign) in signs.items():
        for inner in range(2):
            right[part, sign, 0, :, :, inner, :] = cos_sign[inner] * eye
            right[part, sign, 1, :, :, inner, :] = sin_sign[inner] * eye
    same = np.kron(np.ones((rows, 2 * rows)), np.eye(share))
    low = jnp.bfloat16
    return left.astype(low), right.reshape(4, 2 * rows, -1).astype(low), same.astype(low)


def split_in(values):
    high = values.astype(BF)
    return high, (values - high.astype(F32)).astype(BF)


def times(pair, values):
    high, low = split_in(values)
    return mm(pair[0], high) + mm(pair[1], high) + mm(pair[0], low)


def times_t(pair, values):
    high, low = split_in(values)
    return mm_t(pair[0], high) + mm_t(pair[1], high) + mm_t(pair[0], low)


def gelu_pair(v):
    square = v * v
    tanh = jnp.tanh(GELU_A * v * (1.0 + GELU_B * square))
    half = 0.5 * (1.0 + tanh)
    slope = half + 0.5 * v * (1.0 - tanh * tanh) * (GELU_A * (1.0 + 3.0 * GELU_B * square))
    return v * half, slope


def put_rows(ref, value, r, padded):
    ref[r * padded : r * padded + value.shape[0], :] = value


def column_sum(values):
    return jnp.sum(values, axis=0, keepdims=True)


def norm_one_kernel(columns, padded, groups, all_ref, gain, bias, high, low, freq, xh, inverse, pad, tables, sems):
    mp, rows_dev = all_ref.shape[0], all_ref.shape[1]
    width = mp * all_ref.shape[3]
    choice = width_choice(groups, rows_dev)
    copies = [
        pltpu.make_async_copy(src.at[choice], tables.at[i], sems.at[i])
        for i, src in enumerate((high, low))
    ]
    for copy in copies:
        copy.start()
    pad[...] = jnp.zeros_like(pad)
    for r in range(rows_dev):
        for m in range(mp):
            pad[m, r * padded : r * padded + columns, :] = all_ref[m, r].astype(F32)
    total = sum(jnp.sum(pad[m], axis=1, keepdims=True) for m in range(mp))
    average = total / width
    spread = sum(
        jnp.sum((pad[m] - average) * (pad[m] - average), axis=1, keepdims=True) for m in range(mp)
    )
    inv = lax.rsqrt(spread / width + EPSILON)
    x = pad[lax.axis_index("mp")]
    hat = (x - average) * inv
    u = hat * gain[...] + bias[...]
    xh[...] = hat
    inverse[...] = inv
    for copy in copies:
        copy.wait()
    freq[...] = times((tables[0], tables[1]), u)


def latitude_kernel(share, tables, left, right, same, keep, high_out, low_out):
    high, low = split_in(tables[...])
    for values, out in ((high, high_out), (low, low_out)):
        spread = mm(left[...], values).astype(BF)
        n = left.shape[0]
        for i in range(4):
            block = mm(spread, right[i]) * same[...].astype(F32)
            if i % 2:
                block = block * keep[...]
            out[i * n : (i + 1) * n, :] = block.astype(BF)


def block_mask(blocks, size):
    shape = (blocks * size, blocks * size)
    row = lax.broadcasted_iota(jnp.int32, shape, 0)
    col = lax.broadcasted_iota(jnp.int32, shape, 1)
    inside = None
    for n in range(blocks):
        one = (row >= n * size) & (row < (n + 1) * size) & (col >= n * size) & (col < (n + 1) * size)
        inside = one if inside is None else inside | one
    return inside


def diagonal(packed, blocks, size):
    whole = jnp.concatenate([packed.astype(F32)] * blocks, axis=0)
    return jnp.where(block_mask(blocks, size), whole, 0.0).astype(BF)


def gather_blocks(full, blocks, size):
    col = lax.broadcasted_iota(jnp.int32, (size, blocks * size), 1)
    out = None
    for n in range(blocks):
        piece = full[n * size : (n + 1) * size, :]
        piece = jnp.where((col >= n * size) & (col < (n + 1) * size), piece, 0.0)
        out = piece if out is None else out + piece
    return out


class Mover:
    def __init__(self, sems):
        self.sems, self.count, self.pending = sems, 0, []

    def start(self, src, dst):
        copy = pltpu.make_async_copy(src, dst, self.sems.at[self.count])
        self.count += 1
        copy.start()
        return copy

    def store(self, src, dst):
        self.pending.append(self.start(src, dst))

    def finish(self):
        for copy in self.pending:
            copy.wait()


def filter_kernel(blocks, size, z, high, low, weights, biases, eo, s_h, h_h, slope_h, gate_h, s_s, h_s, slope_s, gate_s, sems):
    move = Mover(sems)
    w1r, w1i, w2r, w2i = (diagonal(weights[i], blocks, size) for i in range(4))
    n = z.shape[0]
    s = times((high[...], low[...]), z[...]).astype(BF)
    s_s[...] = s
    move.store(s_s, s_h)
    sr, si = s[:n], s[n:]
    a1r = mm(sr, w1r) - mm(si, w1i) + biases[0:1, :]
    a1i = mm(sr, w1i) + mm(si, w1r) + biases[1:2, :]
    hr, slope = gelu_pair(a1r)
    hr = hr.astype(BF)
    slope_s[:n, :] = slope
    hi, slope = gelu_pair(a1i)
    hi = hi.astype(BF)
    slope_s[n:, :] = slope
    move.store(slope_s, slope_h)
    h_s[:n, :] = hr
    h_s[n:, :] = hi
    move.store(h_s, h_h)
    a2r = mm(hr, w2r) - mm(hi, w2i) + biases[2:3, :]
    a2i = mm(hr, w2i) + mm(hi, w2r) + biases[3:4, :]
    tr = jnp.tanh(a2r * (1.0 / SHRINK))
    ti = jnp.tanh(a2i * (1.0 / SHRINK))
    gate_s[:n, :] = tr * tr
    gate_s[n:, :] = ti * ti
    move.store(gate_s, gate_h)
    rh, rl = split_in(a2r - SHRINK * tr)
    ih, il = split_in(a2i - SHRINK * ti)
    out = mm_t(high[:n, :], rh) + mm_t(low[:n, :], rh) + mm_t(high[:n, :], rl)
    out += mm_t(high[n:, :], ih) + mm_t(low[n:, :], ih) + mm_t(high[n:, :], il)
    eo[...] = out.astype(BF)
    move.finish()


def second_norm(parts_of):
    width = len(parts_of) * parts_of[0].shape[1]
    total = sum(jnp.sum(v, axis=1, keepdims=True) for v in parts_of)
    average = total / width
    spread = sum(jnp.sum((v - average) * (v - average), axis=1, keepdims=True) for v in parts_of)
    return average, lax.rsqrt(spread / width + EPSILON)


def swap_matrix(places):
    width = places.shape[0]
    lane = lax.broadcasted_iota(jnp.int32, (width, width), 1)
    share = width // lax.axis_size("lat")
    target = (places[:, 0:1] ^ lax.axis_index("lat")) * share + places[:, 1:2]
    return jnp.where(lane == target, 1.0, 0.0).astype(BF)


def cotangent_kernel(columns, padded, dy_all, places, field_all, vectors, w2, dyt, dact, base, pad, dy_s):
    mp, rows_dev, ch = dy_all.shape[0], dy_all.shape[1], dy_all.shape[3]

    @pl.when(pl.program_id(0) == 0)
    def _():
        for m in range(mp):
            pad[...] = jnp.zeros_like(pad)
            for r in range(rows_dev):
                pad[r * padded : r * padded + columns, :] = dy_all[m, r].astype(F32)
            dy_s[:, m * ch : (m + 1) * ch] = pad[...].astype(BF)
        dyt[...] = mm_nt(swap_matrix(places), dy_s[...]).astype(BF)
        for m in range(mp):
            base[m] = jnp.zeros(base.shape[1:], F32)
            for r in range(rows_dev):
                base[m, r * padded : r * padded + columns, :] = field_all[m, r].astype(F32)
        average, inv = second_norm([base[m] for m in range(mp)])
        for m in range(mp):
            x = base[m]
            base[m] = x + (x - average) * inv * vectors[m, 0:1, :] + vectors[m, 1:2, :]

    dact[...] = mm_nt(dy_s[...], w2[...])


def width_choice(groups, rows_dev):
    first = lax.axis_index("lat") * rows_dev
    choice = jnp.int32(0)
    for r in range(rows_dev):
        choice = choice + jnp.where(groups[first + r] == 0, 1 << r, 0).astype(jnp.int32)
    return choice


def mlp_kernel(orders, rows_dev, groups, vectors, b1, places, eo_h, high_h, low_h, base_h, w1_h, dact_h, w2_h, dyt_h, *refs):
    mp, pieces = vectors.shape[0], len(orders)
    kept_h, away_h, gb1, norm_out, own_h = refs[:5]
    grads_h = refs[5 : 5 + 2 * pieces]
    eo, table, base, w1, dact, w2, dyt, kept_send, away_send = refs[5 + 2 * pieces : 14 + 2 * pieces]
    grads = refs[14 + 2 * pieces : 14 + 4 * pieces]
    n_s, nt_s, q_s, dp_s, sems = refs[14 + 4 * pieces :]
    ch, width, hidden = base.shape[2], w1.shape[0], w1.shape[1]
    chunk = hidden // pieces
    mine = lax.axis_index("mp")
    choice = width_choice(groups, rows_dev)
    move = Mover(sems)
    first = [
        move.start(high_h.at[choice], table.at[0]),
        move.start(low_h.at[choice], table.at[1]),
        move.start(eo_h, eo),
        move.start(base_h, base),
    ]
    spans = [slice(p * chunk, (p + 1) * chunk) for p in range(pieces)]
    swap = swap_matrix(places)
    for copy in first:
        copy.wait()
    loads = []
    for p in range(pieces):
        loads.append(
            (
                move.start(w1_h.at[:, spans[p]], w1.at[:, spans[p]]),
                move.start(dact_h.at[:, spans[p]], dact.at[:, spans[p]]),
            )
        )
    load_w2 = move.start(w2_h, w2)
    load_dyt = move.start(dyt_h, dyt)
    for m in range(mp):
        base[m] = base[m] + mm_t(table[0], eo[m]) + mm_t(table[1], eo[m])
    move.store(base.at[mine], own_h)
    average, inv = second_norm([base[m] for m in range(mp)])
    spot = lax.broadcasted_iota(jnp.int32, norm_out.shape, 1)
    norm_out[...] = jnp.where(spot == 0, average, inv)
    for m in range(mp):
        hat = (base[m] - average) * inv
        n_s[:, m * ch : (m + 1) * ch] = (hat * vectors[m, 2:3, :] + vectors[m, 3:4, :]).astype(BF)
    nt_s[...] = mm_nt(swap, n_s[...]).astype(BF)

    for piece, bits in enumerate(orders):
        span = spans[piece]
        for copy in loads[piece]:
            copy.wait()
        q, slope = gelu_pair(mm(n_s[...], w1[:, span]) + b1[:, span])
        q = q.astype(BF)
        q_s[:, span] = q
        dp = (dact[:, span] * slope).astype(BF)
        dp_s[:, span] = dp
        gb1[:, span] = column_sum(dp.astype(F32))

    dn = mm_nt(dp_s[...], w1[...])
    plain, cross = 0.0, 0.0
    for m in range(mp):
        scaled = dn[:, m * ch : (m + 1) * ch] * vectors[m, 2:3, :]
        plain += jnp.sum(scaled, axis=1, keepdims=True)
        cross += jnp.sum(scaled * ((base[m] - average) * inv), axis=1, keepdims=True)
    spot = lax.broadcasted_iota(jnp.int32, (plain.shape[0], 128), 1)
    stat = jnp.zeros(spot.shape, F32)
    for at, value in ((0, plain), (3, cross)):
        for i in range(3):
            term = value.astype(BF).astype(F32)
            value = value - term
            stat = jnp.where(spot == at + i, term, stat)
    stat = stat.astype(BF)
    load_w2.wait()
    out = mm(q_s[...], w2[...])
    for m in range(mp):
        lanes = slice(m * ch, (m + 1) * ch)

        def put(ref):
            ref[:, :ch] = out[:, lanes].astype(BF)
            ref[:, ch : 2 * ch] = dn[:, lanes].astype(BF)
            ref[:, 2 * ch :] = stat

        @pl.when(mine == m)
        def _():
            put(kept_send)

        for other in range(mp):
            if other != m:

                @pl.when(mine == other)
                def _():
                    put(away_send.at[(m - other) % mp - 1])

    move.store(away_send, away_h)
    move.store(kept_send, kept_h)
    load_dyt.wait()
    for piece, bits in enumerate(orders):
        span = spans[piece]
        kept, away = grads[2 * piece : 2 * piece + 2]
        count = len(bits)
        rows = width >> count
        for i, grad in enumerate((mm(nt_s[...], dp_s[:, span]), mm(dyt[...], q_s[:, span]))):
            for place in range(2**count):
                who = sum(((place >> (count - 1 - b)) & 1) * bit for b, bit in enumerate(bits))
                block = grad[who * rows : (who + 1) * rows, :].astype(BF)
                at = (place % 2 ** (count - 1)) * rows
                (away if place >> (count - 1) else kept)[i, at : at + rows, :] = block
            move.store(away.at[i], grads_h[2 * piece + 1].at[i])
            move.store(kept.at[i], grads_h[2 * piece].at[i])
    move.finish()


def back_mix_kernel(columns, padded, width, choice, dy, gain, bias2, high, low, norm_in, own, *refs):
    got, (out_field, dx1, freq, sums, pad) = refs[:-5], refs[-5:]
    ch, rows_dev = own.shape[1], dy.shape[0]
    x1 = own[...]
    average, inv = norm_in[:, 0:1], norm_in[:, 1:2]
    hat = (x1 - average) * inv
    total = sum(piece[...].astype(F32) for piece in got)
    out = x1 + total[:, :ch] + bias2[...]
    dn = total[:, ch : 2 * ch]
    pad[...] = jnp.zeros_like(pad)
    for r in range(rows_dev):
        out_field[r] = out[r * padded : r * padded + columns, :].astype(BF)
        put_rows(pad, dy[r].astype(F32), r, padded)
    grad = pad[...]
    sums[0:1, :] = column_sum(dn * hat)
    sums[1:2, :] = column_sum(dn)
    sums[2:3, :] = column_sum(grad)
    sums[3:8, :] = jnp.zeros((5, ch), F32)
    stats = total[:, 2 * ch : 2 * ch + 128]
    plain = (stats[:, 0:1] + stats[:, 1:2] + stats[:, 2:3]) / width
    cross = (stats[:, 3:4] + stats[:, 4:5] + stats[:, 5:6]) / width
    grad = grad + inv * (dn * gain[...] - plain - hat * cross)
    dx1[...] = grad
    freq[...] = times((high[0], low[0]), grad).astype(BF)


def filter_back_kernel(blocks, size, group, dz, high, low, weights, s_ref, h_ref, slope_ref, gate_ref, mlp_sums, hidden_sums, send, rows, grads_s, sums_s):
    w1r, w1i, w2r, w2i = (diagonal(weights[i], blocks, size) for i in range(4))
    n = dz.shape[0]
    dsh = mm(high[...], dz[...]) + mm(low[...], dz[...])
    da = dsh * gate_ref[...]
    dar, dai = da[:n].astype(BF), da[n:].astype(BF)
    hr, hi = h_ref[:n, :], h_ref[n:, :]
    dcr = ((mm_nt(dar, w2r) + mm_nt(dai, w2i)) * slope_ref[:n, :]).astype(BF)
    dci = ((mm_nt(dai, w2r) - mm_nt(dar, w2i)) * slope_ref[n:, :]).astype(BF)
    rh, rl = split_in(mm_nt(dcr, w1r) + mm_nt(dci, w1i))
    ih, il = split_in(mm_nt(dci, w1r) - mm_nt(dcr, w1i))
    out = mm_t(high[:n, :], rh) + mm_t(low[:n, :], rh) + mm_t(high[:n, :], rl)
    out += mm_t(high[n:, :], ih) + mm_t(low[n:, :], ih) + mm_t(high[n:, :], il)
    parts = rows.shape[0]
    for d in range(parts):
        rows[d, :group, :] = out[d * group : (d + 1) * group, :]
    sr, si = s_ref[:n, :], s_ref[n:, :]
    grads = (
        mm_t(sr, dcr) + mm_t(si, dci),
        mm_t(sr, dci) - mm_t(si, dcr),
        mm_t(hr, dar) + mm_t(hi, dai),
        mm_t(hr, dai) - mm_t(hi, dar),
    )
    for i, grad in enumerate(grads):
        grads_s[i * size : (i + 1) * size, :] = gather_blocks(grad, blocks, size)
    sums_s[...] = jnp.zeros_like(sums_s)
    for i, grad in enumerate((dcr, dci, dar, dai)):
        sums_s[i : i + 1, :] = column_sum(grad.astype(F32))
    sums_s[4:7, :] = mlp_sums[0:3, :]
    sums_s[7 : 7 + hidden_sums.shape[0], :] = hidden_sums[...]
    share = grads_s.shape[0] // parts
    at = group + share
    for d in range(parts):
        rows[d, group:at, :] = grads_s[d * share : (d + 1) * share, :]
        row = sums_s[d : d + 1, :]
        first = row.astype(BF).astype(F32)
        rows[d, at : at + 1, :] = first
        rows[d, at + 1 : at + 2, :] = row - first
        if at + 2 < rows.shape[1]:
            rows[d, at + 2 :, :] = jnp.zeros((rows.shape[1] - at - 2, rows.shape[2]), F32)
    send[...] = rows[...].astype(BF)


def back_norm_kernel(group, share, shares, choice, got, high, low, dx1, xh, inverse, gain, du_out, stat, tail, tail_s):
    parts, _, ch = got.shape
    every = got[...].astype(F32)
    deo = every[:, :group, :].reshape(parts * group, ch).astype(BF)
    at = group + share
    tail_s[...] = jnp.zeros_like(tail_s)
    tail_s[:share, :] = jnp.sum(every[:, group:at, :], axis=0)
    total = jnp.sum(every[:, at : at + 1, :], axis=0) + jnp.sum(every[:, at + 1 : at + 2, :], axis=0)
    du = dx1[...] + mm_t(high[0], deo) + mm_t(low[0], deo)
    du_out[...] = du
    hat = xh[...]
    scaled = du * gain[...]
    spot = lax.broadcasted_iota(jnp.int32, stat.shape, 1)
    plain = jnp.sum(scaled, axis=1, keepdims=True)
    cross = jnp.sum(scaled * hat, axis=1, keepdims=True)
    stat[...] = jnp.where(spot == 0, plain, jnp.where(spot == 1, cross, inverse[...] / shares))
    for i, row in enumerate((total, column_sum(du * hat), column_sum(du))):
        first = row.astype(BF).astype(F32)
        tail_s[share + 2 * i : share + 2 * i + 1, :] = first
        tail_s[share + 2 * i + 1 : share + 2 * i + 2, :] = row - first
    whole_tail = tail_s[...].astype(BF)
    for d in range(parts):
        tail[d] = whole_tail


def close_kernel(share, blocks, size, tail, n1g, n1b, w1, b1, w2, b2, n2g, n2b, gb1, gb2, rows):
    parts = tail.shape[0]
    for d in range(parts):
        rows[d * share : (d + 1) * share, :] = tail[d, :share, :].astype(F32)
    for i, out in enumerate((w1, w1, w2, w2)):
        for n in range(blocks):
            out[i % 2, n] = rows[i * size : (i + 1) * size, n * size : (n + 1) * size]

    def pair(d, i):
        both = tail[d, share + 2 * i : share + 2 * i + 2, :].astype(F32)
        return both[0:1] + both[1:2]

    for i, out in enumerate((b1, b1, b2, b2)):
        row = pair(i, 0)
        for n in range(blocks):
            out[i % 2, n : n + 1, :] = row[:, n * size : (n + 1) * size]
    n2g[...] = pair(4, 0)[0]
    n2b[...] = pair(5, 0)[0]
    gb2[...] = pair(6, 0)[0]
    for i in range(gb1.shape[0]):
        gb1[i : i + 1, :] = pair(7 + i, 0)
    n1g[...] = sum(pair(d, 1) for d in range(parts))[0]
    n1b[...] = sum(pair(d, 2) for d in range(parts))[0]


def whole(shape, extra=0):
    return pl.BlockSpec(shape, lambda *_: (0,) * len(shape))


def run(kernel, outs, args, scratch=(), picked=(), choice=None, flops=0, limit=56):
    moved = sum(math.prod(a.shape) * a.dtype.itemsize for a in args)
    moved += sum(math.prod(o.shape) * o.dtype.itemsize for o in outs)
    params = pltpu.CompilerParams(vmem_limit_bytes=limit * 2**20)
    cost = pl.CostEstimate(flops=flops, bytes_accessed=moved, transcendentals=0)
    out_shape = [jax.ShapeDtypeStruct(o.shape, o.dtype) for o in outs]
    if choice is None:
        return pl.pallas_call(
            kernel,
            out_shape=out_shape,
            in_specs=[pl.BlockSpec(memory_space=pltpu.VMEM)] * len(args),
            out_specs=[pl.BlockSpec(memory_space=pltpu.VMEM)] * len(outs),
            scratch_shapes=list(scratch),
            compiler_params=params,
            cost_estimate=cost,
        )(*args)
    specs = [
        pl.BlockSpec((1, *a.shape[1:]), lambda i, c: (c[0], 0, 0)) if i in picked else whole(a.shape)
        for i, a in enumerate(args)
    ]
    return pl.pallas_call(
        kernel,
        out_shape=out_shape,
        grid_spec=pltpu.PrefetchScalarGridSpec(
            num_scalar_prefetch=1,
            grid=(1,),
            in_specs=specs,
            out_specs=[whole(o.shape) for o in outs],
            scratch_shapes=list(scratch),
        ),
        compiler_params=params,
        cost_estimate=cost,
    )(choice, *args)


def added(terms):
    return sum(term.astype(F32) for term in terms)


def swapped(away, bit, parts):
    return lax.ppermute(away, "lat", [(d, d ^ bit) for d in range(parts)])


def folded(kept, got):
    half = kept.shape[1] // 2
    away = (kept[:, half:].astype(F32) + got[:, half:].astype(F32)).astype(BF)
    return kept[:, :half].astype(F32) + got[:, :half].astype(F32), away


def halve(kept, away, bit, parts):
    return folded(kept, swapped(away, bit, parts))


def tied(value, states):
    return lax.optimization_barrier((value, states))


def body(
    field,
    row_group,
    row_valid,
    norm1_gain,
    norm1_bias,
    spec_w1,
    spec_b1,
    spec_w2,
    spec_b2,
    norm2_gain,
    norm2_bias,
    fc1_weight,
    fc1_bias,
    fc2_weight,
    fc2_bias,
    cotangent,
):
    rows_dev, columns, ch = field.shape
    parts, mp = lax.axis_size("lat"), lax.axis_size("mp")
    me = lax.axis_index("lat")
    rows = rows_dev * parts
    full_width = ch * mp
    padded = -(-columns // 16) * 16
    tokens = rows_dev * padded
    blocks, size = spec_w1.shape[1], spec_w1.shape[2]
    hidden = fc1_weight.shape[1]
    share = -(-HALVES // parts)
    group = 2 * rows_dev * share
    patches = parts * group

    def f32(*shape):
        return jax.ShapeDtypeStruct(shape, F32)

    def bf(*shape):
        return jax.ShapeDtypeStruct(shape, BF)

    lon = [jnp.asarray(t) for t in longitude_tables(parts, share, rows_dev, columns, padded)]
    local_group = lax.dynamic_slice_in_dim(row_group, me * rows_dev, rows_dev)
    choice = sum(
        jnp.where(local_group[r] == 0, 1 << r, 0) for r in range(rows_dev)
    ).astype(jnp.int32).reshape(1)

    field_all = lax.all_gather(field, "mp", axis=0)
    table = pltpu.VMEM((2, patches, tokens), BF)
    freq, xh1, inv1 = pl.pallas_call(
        functools.partial(norm_one_kernel, columns, padded),
        out_shape=[f32(patches, ch), f32(tokens, ch), f32(tokens, 1)],
        in_specs=[pl.BlockSpec(memory_space=pltpu.SMEM)]
        + [pl.BlockSpec(memory_space=pltpu.VMEM)] * 3
        + [pl.BlockSpec(memory_space=pl.ANY)] * 2,
        out_specs=[pl.BlockSpec(memory_space=pltpu.VMEM)] * 3,
        scratch_shapes=[
            pltpu.VMEM((mp, tokens, ch), F32),
            table,
            pltpu.SemaphoreType.DMA((2,)),
        ],
        compiler_params=pltpu.CompilerParams(vmem_limit_bytes=56 * 2**20),
    )(row_group, field_all, norm1_gain, norm1_bias, *lon)

    def to_other(values, rows_each):
        return lax.all_to_all(values.reshape(parts, rows_each, ch), "lat", 0, 0, tiled=True)

    z = to_other(freq, group).reshape(patches, ch)

    cos_mat, sin_mat = latitude_tables(row_group, row_valid)
    width = jnp.where(row_group == 0, LON_FINE, LON_COARSE).astype(jnp.int32)
    here = me * share + jnp.arange(share, dtype=jnp.int32)
    lone = (here[None, :] == 0) | (2 * here[None, :] == width[:, None])
    keep = (1.0 - lone.astype(F32)).reshape(rows * share, 1)
    lat = run(
        functools.partial(latitude_kernel, share),
        [bf(2 * patches, patches)] * 2,
        [
            jnp.concatenate([cos_mat, sin_mat], axis=1),
            *(jnp.asarray(t) for t in latitude_spread(rows, share)),
            keep,
        ],
    )
    spec = jnp.stack([spec_w1, spec_w2]).transpose(0, 1, 3, 2, 4).reshape(4, size, ch)
    spec_bias = jnp.concatenate([spec_b1.reshape(2, ch), spec_b2.reshape(2, ch)], axis=0)
    vectors = jnp.concatenate([norm1_gain, norm1_bias, norm2_gain, norm2_bias]).reshape(4, ch)
    vectors_all = lax.all_gather(vectors, "mp", axis=0)
    dy_all = lax.all_gather(cotangent, "mp", axis=0)
    z, vectors_all, dy_all = lax.optimization_barrier((z, vectors_all, dy_all))

    saved = [bf(2 * patches, ch), bf(2 * patches, ch), f32(2 * patches, ch), f32(2 * patches, ch)]
    vmem, hbm = pl.BlockSpec(memory_space=pltpu.VMEM), pl.BlockSpec(memory_space=pl.ANY)
    eo, s, h, slope, gate = pl.pallas_call(
        functools.partial(filter_kernel, blocks, size),
        out_shape=[bf(patches, ch), *saved],
        in_specs=[vmem] * 5,
        out_specs=[vmem] + [hbm] * 4,
        scratch_shapes=[pltpu.VMEM(a.shape, a.dtype) for a in saved]
        + [pltpu.SemaphoreType.DMA((4,))],
        compiler_params=pltpu.CompilerParams(vmem_limit_bytes=56 * 2**20),
    )(z, *lat, spec, spec_bias)
    chunk = CHUNK if hidden % (3 * CHUNK) == 0 else 256
    steps = hidden // chunk
    bits = [1 << b for b in range(parts.bit_length() - 1)]
    orders = [bits[i:3] + bits[:i] + bits[3:] for i in range(3)]
    pieces = len(orders)
    share_rows = full_width // parts
    places = np.stack(
        [np.arange(full_width) // share_rows, np.arange(full_width) % share_rows], axis=1
    ).astype(np.int32)
    dyt, dact, base = pl.pallas_call(
        functools.partial(cotangent_kernel, columns, padded),
        out_shape=[bf(full_width, tokens), f32(tokens, hidden), f32(mp, tokens, ch)],
        grid=(steps,),
        in_specs=[
            whole(dy_all.shape),
            whole(places.shape),
            whole(field_all.shape),
            whole(vectors_all.shape),
            pl.BlockSpec((chunk, full_width), lambda i: (i, 0)),
        ],
        out_specs=[
            whole((full_width, tokens)),
            pl.BlockSpec((tokens, chunk), lambda i: (0, i)),
            whole((mp, tokens, ch)),
        ],
        scratch_shapes=[pltpu.VMEM((tokens, ch), F32), pltpu.VMEM((tokens, full_width), BF)],
        compiler_params=pltpu.CompilerParams(vmem_limit_bytes=56 * 2**20),
    )(dy_all, jnp.asarray(places), field_all, vectors_all, fc2_weight)
    eo = to_other(eo, group).reshape(patches, ch)
    eo, dyt, dact, base = lax.optimization_barrier((eo, dyt, dact, base))
    eo = lax.all_gather(eo, "mp", axis=0)

    send_lanes = 2 * ch + 128
    piece_shape = (2, full_width // 2, hidden // pieces)
    kept_send, away_send, g_fc1_bias, norm2, x1, *grads = pl.pallas_call(
        functools.partial(mlp_kernel, orders, rows_dev),
        out_shape=[
            bf(tokens, send_lanes),
            bf(mp - 1, tokens, send_lanes),
            f32(1, hidden),
            f32(tokens, 2),
            f32(tokens, ch),
            *[bf(*piece_shape)] * (2 * pieces),
        ],
        in_specs=[pl.BlockSpec(memory_space=pltpu.SMEM), vmem, vmem, vmem] + [hbm] * 8,
        out_specs=[hbm, hbm, vmem, vmem, hbm] + [hbm] * (2 * pieces),
        scratch_shapes=[
            pltpu.VMEM(eo.shape, BF),
            table,
            pltpu.VMEM(base.shape, F32),
            pltpu.VMEM(fc1_weight.shape, BF),
            pltpu.VMEM(dact.shape, F32),
            pltpu.VMEM(fc2_weight.shape, BF),
            pltpu.VMEM(dyt.shape, BF),
            pltpu.VMEM((tokens, send_lanes), BF),
            pltpu.VMEM((mp - 1, tokens, send_lanes), BF),
            *[pltpu.VMEM(piece_shape, BF)] * (2 * pieces),
            pltpu.VMEM((tokens, full_width), BF),
            pltpu.VMEM((full_width, tokens), BF),
            pltpu.VMEM((tokens, hidden), BF),
            pltpu.VMEM((tokens, hidden), BF),
            pltpu.SemaphoreType.DMA((16 + 8 * pieces,)),
        ],
        compiler_params=pltpu.CompilerParams(vmem_limit_bytes=56 * 2**20),
        cost_estimate=pl.CostEstimate(
            flops=10 * tokens * full_width * hidden, bytes_accessed=16 * 2**20, transcendentals=0
        ),
    )(
        row_group,
        vectors_all,
        fc1_bias.reshape(1, hidden),
        jnp.asarray(places),
        eo,
        *lon,
        base,
        fc1_weight,
        dact,
        fc2_weight,
        dyt,
    )
    got = [
        lax.ppermute(away_send[i - 1], "mp", [(d, (d + i) % mp) for d in range(mp)])
        for i in range(1, mp)
    ]

    def exchange(states, turn):
        return [halve(*state, order[turn], parts) for state, order in zip(states, orders)]

    def received(states, turn):
        return [
            (kept, swapped(away, order[turn], parts)) for (kept, away), order in zip(states, orders)
        ]

    states = [(grads[2 * p], grads[2 * p + 1]) for p in range(pieces)]
    states = exchange(states, 0)

    out_field, dx1, dfreq, sums2 = run(
        functools.partial(back_mix_kernel, columns, padded, full_width),
        [bf(rows_dev, columns, ch), f32(tokens, ch), bf(patches, ch), f32(8, ch)],
        [
            cotangent,
            norm2_gain,
            fc2_bias,
            *lon,
            norm2,
            x1,
            kept_send,
            *got,
        ],
        [pltpu.VMEM((tokens, ch), F32)],
        (3, 4),
        choice,
    )

    dz = to_other(dfreq, group).reshape(patches, ch)
    dz, out_field = lax.optimization_barrier(
        (dz, with_layout_constraint(out_field, Layout(major_to_minor=(1, 0, 2))))
    )
    dz, states = tied(dz, states)
    spec_rows = 4 * size // parts
    send_rows = -(-(group + spec_rows + 2) // 8) * 8
    (sent,) = run(
        functools.partial(filter_back_kernel, blocks, size, group),
        [bf(parts, send_rows, ch)],
        [dz, *lat, spec, s, h, slope, gate, sums2, g_fc1_bias.reshape(-1, ch)],
        [
            pltpu.VMEM((parts, send_rows, ch), F32),
            pltpu.VMEM((4 * size, ch), F32),
            pltpu.VMEM((max(parts, 16), ch), F32),
        ],
    )
    sent, states = tied(sent, received(states, 1))
    states = exchange([folded(*state) for state in states], 2)
    sent = lax.all_to_all(sent, "lat", 0, 0, tiled=True)
    sent, states = tied(sent, states)
    kept, away = (jnp.concatenate([state[i] for state in states], axis=2) for i in range(2))
    for bit in bits[3:-1]:
        kept, away = halve(kept, away, bit, parts)
    got_last = lax.ppermute(away, "lat", [(d, d ^ bits[-1]) for d in range(parts)])
    tail_rows = -(-(spec_rows + 6) // 16) * 16
    du, stat1, tail = run(
        functools.partial(back_norm_kernel, group, spec_rows, mp),
        [f32(tokens, ch), f32(tokens, 3), bf(parts, tail_rows, ch)],
        [sent, *lon, dx1, xh1, inv1, norm1_gain],
        [pltpu.VMEM((tail_rows, ch), F32)],
        (1, 2),
        choice,
    )
    stat1 = lax.psum(stat1, "mp")
    stat1, got_last = lax.optimization_barrier((stat1, got_last))
    weights = kept + got_last.astype(F32)
    grad_field = dx1 + stat1[:, 2:] * (
        du * norm1_gain - (stat1[:, :1] + xh1 * stat1[:, 1:2]) * (1.0 / full_width)
    )
    grad_field = grad_field.reshape(rows_dev, padded, ch)[:, :columns]

    tail = lax.all_to_all(tail, "lat", 0, 0, tiled=True)
    vector, weight, bias = f32(ch), f32(2, blocks, size, size), f32(2, blocks, size)
    g_n1g, g_n1b, g_w1, g_b1, g_w2, g_b2, g_n2g, g_n2b, g_fc1b, g_fc2b = run(
        functools.partial(close_kernel, spec_rows, blocks, size),
        [vector, vector, weight, bias, weight, bias, vector, vector, f32(hidden // ch, ch), vector],
        [tail],
        [pltpu.VMEM((4 * size, ch), F32)],
    )
    return (
        out_field,
        grad_field,
        g_n1g,
        g_n1b,
        g_w1,
        g_b1,
        g_w2,
        g_b2,
        g_n2g,
        g_n2b,
        weights[0],
        g_fc1b.reshape(hidden),
        weights[1].T,
        g_fc2b,
    )


def solution(mesh):
    placed = (
        P("lat", None, "mp"),
        P(),
        P(),
        P("mp"),
        P("mp"),
        P(None, "mp", None, None),
        P(None, "mp", None),
        P(None, "mp", None, None),
        P(None, "mp", None),
        P("mp"),
        P("mp"),
        P(None, "mp"),
        P("mp"),
        P("mp", None),
        P("mp"),
        P("lat", None, "mp"),
    )
    return jax.shard_map(
        body,
        mesh=mesh,
        in_specs=placed,
        out_specs=(
            P("lat", None, "mp"),
            P("lat", None, "mp"),
            P("mp"),
            P("mp"),
            P(None, "mp", None, None),
            P(None, "mp", None),
            P(None, "mp", None, None),
            P(None, "mp", None),
            P("mp"),
            P("mp"),
            P("lat", "mp"),
            P("mp"),
            P("mp", "lat"),
            P("mp"),
        ),
        check_vma=False,
    )
```

```python
import functools
import math

import jax
import jax.numpy as jnp
import numpy as np
from jax import lax
from jax.experimental.layout import Layout, with_layout_constraint
from jax.experimental import pallas as pl
from jax.experimental.pallas import tpu as pltpu
from jax.sharding import PartitionSpec as P

LON_FINE = 180
LON_COARSE = 45
GROUPS = 8
EPSILON = 1e-05
SHRINK = 0.01
HALVES = LON_FINE // 2 + 1
BF = jnp.bfloat16
F32 = jnp.float32


def split_two(values):
    high = lax.reduce_precision(values, 8, 7)
    return high.astype(BF), (values - high).astype(BF)


def mm(left, right):
    return lax.dot_general(left, right, (((1,), (0,)), ((), ())), preferred_element_type=F32)


def mm_t(left, right):
    return lax.dot_general(left, right, (((0,), (0,)), ((), ())), preferred_element_type=F32)


def mm_nt(left, right):
    return lax.dot_general(left, right, (((1,), (1,)), ((), ())), preferred_element_type=F32)


def np_split(values):
    high = values.astype(jnp.bfloat16)
    low = (values - high.astype(np.float32)).astype(jnp.bfloat16)
    return high, low


def row_tables(row_group, row_valid):
    member = (row_group[:, None] == jnp.arange(GROUPS, dtype=jnp.int32)[None, :]).astype(
        jnp.int32
    ) * row_valid[:, None]
    counts = jnp.sum(member, axis=0)
    before = jnp.cumsum(member, axis=0) - member
    offset = jnp.sum(before * member, axis=1)
    length = jnp.maximum(jnp.sum(member * counts[None, :], axis=1), 1)
    return (offset, length)


def latitude_tables(row_group, row_valid):
    offset, length = row_tables(row_group, row_valid)
    phases = offset[:, None] * offset[None, :] % length[:, None]
    lengths = length[:, None].astype(F32)
    angles = 2.0 * math.pi * phases.astype(F32) / lengths
    kept = (
        (row_group[:, None] == row_group[None, :])
        & (row_valid[:, None] > 0)
        & (row_valid[None, :] > 0)
    ).astype(F32) * lax.rsqrt(lengths)
    return kept * jnp.cos(angles), kept * jnp.sin(angles)


CHUNK = 512
GELU_A = math.sqrt(2.0 / math.pi)
GELU_B = 0.044715


def longitude_tables(parts, share, rows_dev, columns, padded):
    freq = np.arange(parts * share).reshape(parts, share)
    cols = np.arange(columns)
    pairs = []
    for width in (LON_COARSE, LON_FINE):
        angles = 2.0 * np.pi * ((freq[..., None] * cols) % width) / width
        inside = (freq[..., None] * 2 <= width) & (cols < width)
        scale = inside / np.sqrt(width)
        pairs.append(np.stack([scale * np.cos(angles), -scale * np.sin(angles)], axis=1))
    full = np.zeros((2**rows_dev, parts, rows_dev, 2, share, rows_dev, padded), np.float32)
    for choice in range(2**rows_dev):
        for r in range(rows_dev):
            full[choice, :, r, :, :, r, :columns] = pairs[(choice >> r) & 1]
    return np_split(full.reshape(2**rows_dev, parts * rows_dev * 2 * share, rows_dev * padded))


def latitude_spread(rows, share):
    left = np.kron(np.eye(rows), np.ones((share, 1)))
    right = np.zeros((2, 2, 2, rows, rows, 2, share))
    signs = {
        (0, 0): ((1, 0), (0, 1)),
        (1, 0): ((0, 1), (-1, 0)),
        (0, 1): ((1, 0), (0, -1)),
        (1, 1): ((0, -1), (-1, 0)),
    }
    eye = np.eye(rows)[:, :, None]
    for (part, sign), (cos_sign, sin_sign) in signs.items():
        for inner in range(2):
            right[part, sign, 0, :, :, inner, :] = cos_sign[inner] * eye
            right[part, sign, 1, :, :, inner, :] = sin_sign[inner] * eye
    same = np.kron(np.ones((rows, 2 * rows)), np.eye(share))
    low = jnp.bfloat16
    return left.astype(low), right.reshape(4, 2 * rows, -1).astype(low), same.astype(low)


def split_in(values):
    high = values.astype(BF)
    return high, (values - high.astype(F32)).astype(BF)


def times(pair, values):
    high, low = split_in(values)
    width = values.shape[1]
    both = mm(pair[0], jnp.concatenate([high, low], axis=1))
    return both[:, :width] + both[:, width:] + mm(pair[1], high)


def times_t(pair, values):
    high, low = split_in(values)
    width = values.shape[1]
    both = mm_t(pair[0], jnp.concatenate([high, low], axis=1))
    return both[:, :width] + both[:, width:] + mm_t(pair[1], high)


def gelu_pair(v):
    square = v * v
    tanh = jnp.tanh(GELU_A * v * (1.0 + GELU_B * square))
    half = 0.5 * (1.0 + tanh)
    slope = half + 0.5 * v * (1.0 - tanh * tanh) * (GELU_A * (1.0 + 3.0 * GELU_B * square))
    return v * half, slope


def put_rows(ref, value, r, padded):
    ref[r * padded : r * padded + value.shape[0], :] = value


def column_sum(values):
    return jnp.sum(values, axis=0, keepdims=True)


def norm_one_kernel(columns, padded, groups, all_ref, gain, bias, high, low, freq, xh, inverse, pad, tables, sems):
    mp, rows_dev = all_ref.shape[0], all_ref.shape[1]
    width = mp * all_ref.shape[3]
    choice = width_choice(groups, rows_dev)
    copies = [
        pltpu.make_async_copy(src.at[choice], tables.at[i], sems.at[i])
        for i, src in enumerate((high, low))
    ]
    for copy in copies:
        copy.start()
    pad[...] = jnp.zeros_like(pad)
    for r in range(rows_dev):
        for m in range(mp):
            pad[m, r * padded : r * padded + columns, :] = all_ref[m, r].astype(F32)
    total = sum(jnp.sum(pad[m], axis=1, keepdims=True) for m in range(mp))
    average = total / width
    spread = sum(
        jnp.sum((pad[m] - average) * (pad[m] - average), axis=1, keepdims=True) for m in range(mp)
    )
    inv = lax.rsqrt(spread / width + EPSILON)
    x = pad[lax.axis_index("mp")]
    hat = (x - average) * inv
    u = hat * gain[...] + bias[...]
    xh[...] = hat
    inverse[...] = inv
    for copy in copies:
        copy.wait()
    freq[...] = times((tables[0], tables[1]), u)


def latitude_kernel(share, tables, left, right, same, keep, high_out, low_out):
    high, low = split_in(tables[...])
    for values, out in ((high, high_out), (low, low_out)):
        spread = mm(left[...], values).astype(BF)
        n = left.shape[0]
        for i in range(4):
            block = mm(spread, right[i]) * same[...].astype(F32)
            if i % 2:
                block = block * keep[...]
            out[i * n : (i + 1) * n, :] = block.astype(BF)


def block_mask(blocks, size):
    shape = (blocks * size, blocks * size)
    row = lax.broadcasted_iota(jnp.int32, shape, 0)
    col = lax.broadcasted_iota(jnp.int32, shape, 1)
    inside = None
    for n in range(blocks):
        one = (row >= n * size) & (row < (n + 1) * size) & (col >= n * size) & (col < (n + 1) * size)
        inside = one if inside is None else inside | one
    return inside


def diagonal(packed, blocks, size):
    whole = jnp.concatenate([packed.astype(F32)] * blocks, axis=0)
    return jnp.where(block_mask(blocks, size), whole, 0.0).astype(BF)


def gather_blocks(full, blocks, size):
    col = lax.broadcasted_iota(jnp.int32, (size, blocks * size), 1)
    out = None
    for n in range(blocks):
        piece = full[n * size : (n + 1) * size, :]
        piece = jnp.where((col >= n * size) & (col < (n + 1) * size), piece, 0.0)
        out = piece if out is None else out + piece
    return out


class Mover:
    def __init__(self, sems):
        self.sems, self.count, self.pending = sems, 0, []

    def start(self, src, dst):
        copy = pltpu.make_async_copy(src, dst, self.sems.at[self.count])
        self.count += 1
        copy.start()
        return copy

    def store(self, src, dst):
        self.pending.append(self.start(src, dst))

    def finish(self):
        for copy in self.pending:
            copy.wait()


def complex_blocks(real, imag, blocks, size):
    real, imag = diagonal(real, blocks, size), diagonal(imag, blocks, size)
    return jnp.concatenate(
        [jnp.concatenate([real, imag], axis=1), jnp.concatenate([-imag, real], axis=1)], axis=0
    )


def side_by_side(values):
    half = values.shape[0] // 2
    return jnp.concatenate([values[:half], values[half:]], axis=1)


def one_below(values):
    half = values.shape[1] // 2
    return jnp.concatenate([values[:, :half], values[:, half:]], axis=0)


def filter_kernel(blocks, size, z, high, low, weights, biases, eo, s_h, h_h, slope_h, gate_h, s_s, h_s, slope_s, gate_s, sems):
    move = Mover(sems)
    first = complex_blocks(weights[0], weights[1], blocks, size)
    second = complex_blocks(weights[2], weights[3], blocks, size)
    s = side_by_side(times((high[...], low[...]), z[...]).astype(BF))
    s_s[...] = s
    move.store(s_s, s_h)
    h, slope = gelu_pair(mm(s, first) + biases[0:1, :])
    h = h.astype(BF)
    slope_s[...] = slope
    move.store(slope_s, slope_h)
    h_s[...] = h
    move.store(h_s, h_h)
    a2 = mm(h, second) + biases[1:2, :]
    tanh = jnp.tanh(a2 * (1.0 / SHRINK))
    gate_s[...] = tanh * tanh
    move.store(gate_s, gate_h)
    eo[...] = times_t((high[...], low[...]), one_below(a2 - SHRINK * tanh)).astype(BF)
    move.finish()


def second_norm(parts_of):
    width = len(parts_of) * parts_of[0].shape[1]
    total = sum(jnp.sum(v, axis=1, keepdims=True) for v in parts_of)
    average = total / width
    spread = sum(jnp.sum((v - average) * (v - average), axis=1, keepdims=True) for v in parts_of)
    return average, lax.rsqrt(spread / width + EPSILON)


def swap_matrix(places):
    width = places.shape[0]
    lane = lax.broadcasted_iota(jnp.int32, (width, width), 1)
    share = width // lax.axis_size("lat")
    target = (places[:, 0:1] ^ lax.axis_index("lat")) * share + places[:, 1:2]
    return jnp.where(lane == target, 1.0, 0.0).astype(BF)


def cotangent_kernel(columns, padded, dy_all, places, field_all, vectors, w2, dyt, dact, base, pad, dy_s):
    mp, rows_dev, ch = dy_all.shape[0], dy_all.shape[1], dy_all.shape[3]

    @pl.when(pl.program_id(0) == 0)
    def _():
        for m in range(mp):
            pad[...] = jnp.zeros_like(pad)
            for r in range(rows_dev):
                pad[r * padded : r * padded + columns, :] = dy_all[m, r].astype(F32)
            dy_s[:, m * ch : (m + 1) * ch] = pad[...].astype(BF)
        dyt[...] = mm_nt(swap_matrix(places), dy_s[...]).astype(BF)
        for m in range(mp):
            base[m] = jnp.zeros(base.shape[1:], F32)
            for r in range(rows_dev):
                base[m, r * padded : r * padded + columns, :] = field_all[m, r].astype(F32)
        average, inv = second_norm([base[m] for m in range(mp)])
        for m in range(mp):
            x = base[m]
            base[m] = x + (x - average) * inv * vectors[m, 0:1, :] + vectors[m, 1:2, :]

    dact[...] = mm_nt(dy_s[...], w2[...])


def width_choice(groups, rows_dev):
    first = lax.axis_index("lat") * rows_dev
    choice = jnp.int32(0)
    for r in range(rows_dev):
        choice = choice + jnp.where(groups[first + r] == 0, 1 << r, 0).astype(jnp.int32)
    return choice


def mlp_kernel(orders, rows_dev, groups, vectors, b1, places, eo_h, high_h, low_h, base_h, w1_h, dact_h, w2_h, dyt_h, *refs):
    mp, pieces = vectors.shape[0], len(orders)
    kept_h, away_h, gb1, norm_out, own_h = refs[:5]
    grads_h = refs[5 : 5 + 2 * pieces]
    eo, table, base, w1, dact, w2, dyt, kept_send, away_send = refs[5 + 2 * pieces : 14 + 2 * pieces]
    grads = refs[14 + 2 * pieces : 14 + 4 * pieces]
    n_s, nt_s, q_s, dp_s, sems = refs[14 + 4 * pieces :]
    ch, width, hidden = base.shape[2], w1.shape[0], w1.shape[1]
    chunk = hidden // pieces
    mine = lax.axis_index("mp")
    choice = width_choice(groups, rows_dev)
    move = Mover(sems)
    first = [
        move.start(high_h.at[choice], table.at[0]),
        move.start(low_h.at[choice], table.at[1]),
        move.start(eo_h, eo),
        move.start(base_h, base),
    ]
    spans = [slice(p * chunk, (p + 1) * chunk) for p in range(pieces)]
    swap = swap_matrix(places)
    for copy in first:
        copy.wait()
    loads = []
    for p in range(pieces):
        loads.append(
            (
                move.start(w1_h.at[:, spans[p]], w1.at[:, spans[p]]),
                move.start(dact_h.at[:, spans[p]], dact.at[:, spans[p]]),
            )
        )
    load_w2 = move.start(w2_h, w2)
    load_dyt = move.start(dyt_h, dyt)
    every = jnp.concatenate([eo[m] for m in range(mp)], axis=1)
    filtered = mm_t(table[0], every) + mm_t(table[1], every)
    for m in range(mp):
        base[m] = base[m] + filtered[:, m * ch : (m + 1) * ch]
    move.store(base.at[mine], own_h)
    average, inv = second_norm([base[m] for m in range(mp)])
    spot = lax.broadcasted_iota(jnp.int32, norm_out.shape, 1)
    norm_out[...] = jnp.where(spot == 0, average, inv)
    for m in range(mp):
        hat = (base[m] - average) * inv
        n_s[:, m * ch : (m + 1) * ch] = (hat * vectors[m, 2:3, :] + vectors[m, 3:4, :]).astype(BF)
    nt_s[...] = mm_nt(swap, n_s[...]).astype(BF)

    for piece, bits in enumerate(orders):
        span = spans[piece]
        for copy in loads[piece]:
            copy.wait()
        q, slope = gelu_pair(mm(n_s[...], w1[:, span]) + b1[:, span])
        q = q.astype(BF)
        q_s[:, span] = q
        dp = (dact[:, span] * slope).astype(BF)
        dp_s[:, span] = dp
        gb1[:, span] = column_sum(dp.astype(F32))

    dn = mm_nt(dp_s[...], w1[...])
    plain, cross = 0.0, 0.0
    for m in range(mp):
        scaled = dn[:, m * ch : (m + 1) * ch] * vectors[m, 2:3, :]
        plain += jnp.sum(scaled, axis=1, keepdims=True)
        cross += jnp.sum(scaled * ((base[m] - average) * inv), axis=1, keepdims=True)
    spot = lax.broadcasted_iota(jnp.int32, (plain.shape[0], 128), 1)
    stat = jnp.zeros(spot.shape, F32)
    for at, value in ((0, plain), (3, cross)):
        for i in range(3):
            term = value.astype(BF).astype(F32)
            value = value - term
            stat = jnp.where(spot == at + i, term, stat)
    stat = stat.astype(BF)
    load_w2.wait()
    out = mm(q_s[...], w2[...])
    for m in range(mp):
        lanes = slice(m * ch, (m + 1) * ch)

        def put(ref):
            ref[:, :ch] = out[:, lanes].astype(BF)
            ref[:, ch : 2 * ch] = dn[:, lanes].astype(BF)
            ref[:, 2 * ch :] = stat

        @pl.when(mine == m)
        def _():
            put(kept_send)

        for other in range(mp):
            if other != m:

                @pl.when(mine == other)
                def _():
                    put(away_send.at[(m - other) % mp - 1])

    move.store(away_send, away_h)
    move.store(kept_send, kept_h)
    load_dyt.wait()
    for piece, bits in enumerate(orders):
        span = spans[piece]
        kept, away = grads[2 * piece : 2 * piece + 2]
        count = len(bits)
        rows = width >> count
        for i, grad in enumerate((mm(nt_s[...], dp_s[:, span]), mm(dyt[...], q_s[:, span]))):
            for place in range(2**count):
                who = sum(((place >> (count - 1 - b)) & 1) * bit for b, bit in enumerate(bits))
                block = grad[who * rows : (who + 1) * rows, :].astype(BF)
                at = (place % 2 ** (count - 1)) * rows
                (away if place >> (count - 1) else kept)[i, at : at + rows, :] = block
            move.store(away.at[i], grads_h[2 * piece + 1].at[i])
            move.store(kept.at[i], grads_h[2 * piece].at[i])
    move.finish()


def back_mix_kernel(columns, padded, width, choice, dy, gain, bias2, high, low, norm_in, own, *refs):
    got, (out_field, dx1, freq, sums, pad) = refs[:-5], refs[-5:]
    ch, rows_dev = own.shape[1], dy.shape[1]
    mine = lax.axis_index("mp")
    x1 = own[...]
    average, inv = norm_in[:, 0:1], norm_in[:, 1:2]
    hat = (x1 - average) * inv
    total = sum(piece[...].astype(F32) for piece in got)
    out = x1 + total[:, :ch] + bias2[...]
    dn = total[:, ch : 2 * ch]
    pad[...] = jnp.zeros_like(pad)
    for r in range(rows_dev):
        out_field[r] = out[r * padded : r * padded + columns, :].astype(BF)
        put_rows(pad, dy[mine, r].astype(F32), r, padded)
    grad = pad[...]
    sums[0:1, :] = column_sum(dn * hat)
    sums[1:2, :] = column_sum(dn)
    sums[2:3, :] = column_sum(grad)
    sums[3:8, :] = jnp.zeros((5, ch), F32)
    stats = total[:, 2 * ch : 2 * ch + 128]
    plain = (stats[:, 0:1] + stats[:, 1:2] + stats[:, 2:3]) / width
    cross = (stats[:, 3:4] + stats[:, 4:5] + stats[:, 5:6]) / width
    grad = grad + inv * (dn * gain[...] - plain - hat * cross)
    dx1[...] = grad
    freq[...] = times((high[0], low[0]), grad).astype(BF)


def filter_back_kernel(blocks, size, group, dz, high, low, weights, s_ref, h_ref, slope_ref, gate_ref, mlp_sums, hidden_sums, send, rows, grads_s, sums_s):
    first = complex_blocks(weights[0], weights[1], blocks, size)
    second = complex_blocks(weights[2], weights[3], blocks, size)
    ch = dz.shape[1]
    dsh = mm(high[...], dz[...]) + mm(low[...], dz[...])
    da = (side_by_side(dsh) * gate_ref[...]).astype(BF)
    dc = (mm_nt(da, second) * slope_ref[...]).astype(BF)
    out = times_t((high[...], low[...]), one_below(mm_nt(dc, first)))
    parts = rows.shape[0]
    for d in range(parts):
        rows[d, :group, :] = out[d * group : (d + 1) * group, :]
    for i, (left, right) in enumerate(((s_ref, dc), (h_ref, da))):
        outer = mm_t(left[...], right)
        pair = (outer[:ch, :ch] + outer[ch:, ch:], outer[:ch, ch:] - outer[ch:, :ch])
        for k, grad in enumerate(pair):
            at = (2 * i + k) * size
            grads_s[at : at + size, :] = gather_blocks(grad, blocks, size)
    sums_s[...] = jnp.zeros_like(sums_s)
    for i, grad in enumerate((dc, da)):
        total = column_sum(grad.astype(F32))
        sums_s[2 * i : 2 * i + 1, :] = total[:, :ch]
        sums_s[2 * i + 1 : 2 * i + 2, :] = total[:, ch:]
    sums_s[4:7, :] = mlp_sums[0:3, :]
    for i in range(hidden_sums.shape[1] // ch):
        sums_s[7 + i : 8 + i, :] = hidden_sums[:, i * ch : (i + 1) * ch]
    share = grads_s.shape[0] // parts
    at = group + share
    for d in range(parts):
        rows[d, group:at, :] = grads_s[d * share : (d + 1) * share, :]
        row = sums_s[d : d + 1, :]
        first = row.astype(BF).astype(F32)
        rows[d, at : at + 1, :] = first
        rows[d, at + 1 : at + 2, :] = row - first
        if at + 2 < rows.shape[1]:
            rows[d, at + 2 :, :] = jnp.zeros((rows.shape[1] - at - 2, rows.shape[2]), F32)
    send[...] = rows[...].astype(BF)


def back_norm_kernel(group, share, shares, choice, got, high, low, dx1, xh, inverse, gain, du_out, stat, tail, tail_s):
    parts, _, ch = got.shape
    every = got[...].astype(F32)
    deo = every[:, :group, :].reshape(parts * group, ch).astype(BF)
    at = group + share
    tail_s[...] = jnp.zeros_like(tail_s)
    tail_s[:share, :] = jnp.sum(every[:, group:at, :], axis=0)
    total = jnp.sum(every[:, at : at + 1, :], axis=0) + jnp.sum(every[:, at + 1 : at + 2, :], axis=0)
    du = dx1[...] + mm_t(high[0], deo) + mm_t(low[0], deo)
    du_out[...] = du
    hat = xh[...]
    scaled = du * gain[...]
    spot = lax.broadcasted_iota(jnp.int32, stat.shape, 1)
    plain = jnp.sum(scaled, axis=1, keepdims=True)
    cross = jnp.sum(scaled * hat, axis=1, keepdims=True)
    stat[...] = jnp.where(spot == 0, plain, jnp.where(spot == 1, cross, inverse[...] / shares))
    for i, row in enumerate((total, column_sum(du * hat), column_sum(du))):
        first = row.astype(BF).astype(F32)
        tail_s[share + 2 * i : share + 2 * i + 1, :] = first
        tail_s[share + 2 * i + 1 : share + 2 * i + 2, :] = row - first
    whole_tail = tail_s[...].astype(BF)
    for d in range(parts):
        tail[d] = whole_tail


def close_kernel(share, blocks, size, tail, n1g, n1b, w1, b1, w2, b2, n2g, n2b, gb1, gb2, rows):
    parts = tail.shape[0]
    for d in range(parts):
        rows[d * share : (d + 1) * share, :] = tail[d, :share, :].astype(F32)
    for i, out in enumerate((w1, w1, w2, w2)):
        for n in range(blocks):
            out[i % 2, n] = rows[i * size : (i + 1) * size, n * size : (n + 1) * size]

    def pair(d, i):
        both = tail[d, share + 2 * i : share + 2 * i + 2, :].astype(F32)
        return both[0:1] + both[1:2]

    for i, out in enumerate((b1, b1, b2, b2)):
        row = pair(i, 0)
        for n in range(blocks):
            out[i % 2, n : n + 1, :] = row[:, n * size : (n + 1) * size]
    n2g[...] = pair(4, 0)[0]
    n2b[...] = pair(5, 0)[0]
    gb2[...] = pair(6, 0)[0]
    ch = tail.shape[2]
    for i in range(math.prod(gb1.shape) // ch):
        row = pair(7 + i, 0)
        if gb1.ndim == 1:
            gb1[i * ch : (i + 1) * ch] = row[0]
        else:
            gb1[i : i + 1, :] = row
    n1g[...] = sum(pair(d, 1) for d in range(parts))[0]
    n1b[...] = sum(pair(d, 2) for d in range(parts))[0]


def whole(shape, extra=0):
    return pl.BlockSpec(shape, lambda *_: (0,) * len(shape))


def run(kernel, outs, args, scratch=(), picked=(), choice=None, flops=0, limit=56):
    moved = sum(math.prod(a.shape) * a.dtype.itemsize for a in args)
    moved += sum(math.prod(o.shape) * o.dtype.itemsize for o in outs)
    params = pltpu.CompilerParams(vmem_limit_bytes=limit * 2**20)
    cost = pl.CostEstimate(flops=flops, bytes_accessed=moved, transcendentals=0)
    out_shape = [jax.ShapeDtypeStruct(o.shape, o.dtype) for o in outs]
    if choice is None:
        return pl.pallas_call(
            kernel,
            out_shape=out_shape,
            in_specs=[pl.BlockSpec(memory_space=pltpu.VMEM)] * len(args),
            out_specs=[pl.BlockSpec(memory_space=pltpu.VMEM)] * len(outs),
            scratch_shapes=list(scratch),
            compiler_params=params,
            cost_estimate=cost,
        )(*args)
    specs = [
        pl.BlockSpec((1, *a.shape[1:]), lambda i, c: (c[0], 0, 0)) if i in picked else whole(a.shape)
        for i, a in enumerate(args)
    ]
    return pl.pallas_call(
        kernel,
        out_shape=out_shape,
        grid_spec=pltpu.PrefetchScalarGridSpec(
            num_scalar_prefetch=1,
            grid=(1,),
            in_specs=specs,
            out_specs=[whole(o.shape) for o in outs],
            scratch_shapes=list(scratch),
        ),
        compiler_params=params,
        cost_estimate=cost,
    )(choice, *args)


def added(terms):
    return sum(term.astype(F32) for term in terms)


def swapped(away, bit, parts):
    return lax.ppermute(away, "lat", [(d, d ^ bit) for d in range(parts)])


def added(terms, first, end):
    return sum(t[:, first:end].astype(F32) for t in terms)


def later(value, arrays):
    return lax.optimization_barrier((value, arrays))[0]


def together(value, arrays):
    return lax.optimization_barrier((value, arrays))


def body(
    field,
    row_group,
    row_valid,
    norm1_gain,
    norm1_bias,
    spec_w1,
    spec_b1,
    spec_w2,
    spec_b2,
    norm2_gain,
    norm2_bias,
    fc1_weight,
    fc1_bias,
    fc2_weight,
    fc2_bias,
    cotangent,
):
    rows_dev, columns, ch = field.shape
    parts, mp = lax.axis_size("lat"), lax.axis_size("mp")
    me = lax.axis_index("lat")
    rows = rows_dev * parts
    full_width = ch * mp
    padded = -(-columns // 16) * 16
    tokens = rows_dev * padded
    blocks, size = spec_w1.shape[1], spec_w1.shape[2]
    hidden = fc1_weight.shape[1]
    share = -(-HALVES // parts)
    group = 2 * rows_dev * share
    patches = parts * group

    def f32(*shape):
        return jax.ShapeDtypeStruct(shape, F32)

    def bf(*shape):
        return jax.ShapeDtypeStruct(shape, BF)

    lon = [jnp.asarray(t) for t in longitude_tables(parts, share, rows_dev, columns, padded)]
    local_group = lax.dynamic_slice_in_dim(row_group, me * rows_dev, rows_dev)
    choice = sum(
        jnp.where(local_group[r] == 0, 1 << r, 0) for r in range(rows_dev)
    ).astype(jnp.int32).reshape(1)

    field_all = lax.all_gather(field, "mp", axis=0)
    table = pltpu.VMEM((2, patches, tokens), BF)
    freq, xh1, inv1 = pl.pallas_call(
        functools.partial(norm_one_kernel, columns, padded),
        out_shape=[f32(patches, ch), f32(tokens, ch), f32(tokens, 1)],
        in_specs=[pl.BlockSpec(memory_space=pltpu.SMEM)]
        + [pl.BlockSpec(memory_space=pltpu.VMEM)] * 3
        + [pl.BlockSpec(memory_space=pl.ANY)] * 2,
        out_specs=[pl.BlockSpec(memory_space=pltpu.VMEM)] * 3,
        scratch_shapes=[
            pltpu.VMEM((mp, tokens, ch), F32),
            table,
            pltpu.SemaphoreType.DMA((2,)),
        ],
        compiler_params=pltpu.CompilerParams(vmem_limit_bytes=56 * 2**20),
    )(row_group, field_all, norm1_gain, norm1_bias, *lon)

    def to_other(values, rows_each):
        return lax.all_to_all(values.reshape(parts, rows_each, ch), "lat", 0, 0, tiled=True)

    z = to_other(freq, group).reshape(patches, ch)

    cos_mat, sin_mat = latitude_tables(row_group, row_valid)
    width = jnp.where(row_group == 0, LON_FINE, LON_COARSE).astype(jnp.int32)
    here = me * share + jnp.arange(share, dtype=jnp.int32)
    lone = (here[None, :] == 0) | (2 * here[None, :] == width[:, None])
    keep = (1.0 - lone.astype(F32)).reshape(rows * share, 1)
    lat = run(
        functools.partial(latitude_kernel, share),
        [bf(2 * patches, patches)] * 2,
        [
            jnp.concatenate([cos_mat, sin_mat], axis=1),
            *(jnp.asarray(t) for t in latitude_spread(rows, share)),
            keep,
        ],
    )
    spec = jnp.stack([spec_w1, spec_w2]).transpose(0, 1, 3, 2, 4).reshape(4, size, ch)
    spec_bias = jnp.concatenate([spec_b1.reshape(1, 2 * ch), spec_b2.reshape(1, 2 * ch)], axis=0)
    vectors = jnp.concatenate([norm1_gain, norm1_bias, norm2_gain, norm2_bias]).reshape(4, ch)
    vectors_all = lax.all_gather(vectors, "mp", axis=0)
    dy_all = lax.all_gather(cotangent, "mp", axis=0)
    z, vectors_all, dy_all = lax.optimization_barrier((z, vectors_all, dy_all))

    saved = [bf(patches, 2 * ch), bf(patches, 2 * ch), f32(patches, 2 * ch), f32(patches, 2 * ch)]
    vmem, hbm = pl.BlockSpec(memory_space=pltpu.VMEM), pl.BlockSpec(memory_space=pl.ANY)
    eo, s, h, slope, gate = pl.pallas_call(
        functools.partial(filter_kernel, blocks, size),
        out_shape=[bf(patches, ch), *saved],
        in_specs=[vmem] * 5,
        out_specs=[vmem] + [hbm] * 4,
        scratch_shapes=[pltpu.VMEM(a.shape, a.dtype) for a in saved]
        + [pltpu.SemaphoreType.DMA((4,))],
        compiler_params=pltpu.CompilerParams(vmem_limit_bytes=56 * 2**20),
    )(z, *lat, spec, spec_bias)
    chunk = CHUNK if hidden % (3 * CHUNK) == 0 else 256
    steps = hidden // chunk
    bits = [1 << b for b in range(parts.bit_length() - 1)]
    orders = [bits[i:3] + bits[:i] + bits[3:] for i in range(3)]
    pieces = len(orders)
    share_rows = full_width // parts
    places = np.stack(
        [np.arange(full_width) // share_rows, np.arange(full_width) % share_rows], axis=1
    ).astype(np.int32)
    dyt, dact, base = pl.pallas_call(
        functools.partial(cotangent_kernel, columns, padded),
        out_shape=[bf(full_width, tokens), f32(tokens, hidden), f32(mp, tokens, ch)],
        grid=(steps,),
        in_specs=[
            whole(dy_all.shape),
            whole(places.shape),
            whole(field_all.shape),
            whole(vectors_all.shape),
            pl.BlockSpec((chunk, full_width), lambda i: (i, 0)),
        ],
        out_specs=[
            whole((full_width, tokens)),
            pl.BlockSpec((tokens, chunk), lambda i: (0, i)),
            whole((mp, tokens, ch)),
        ],
        scratch_shapes=[pltpu.VMEM((tokens, ch), F32), pltpu.VMEM((tokens, full_width), BF)],
        compiler_params=pltpu.CompilerParams(vmem_limit_bytes=56 * 2**20),
    )(dy_all, jnp.asarray(places), field_all, vectors_all, fc2_weight)
    eo = to_other(eo, group).reshape(patches, ch)
    eo, dyt, dact, base = lax.optimization_barrier((eo, dyt, dact, base))
    eo = lax.all_gather(eo, "mp", axis=0)

    send_lanes = 2 * ch + 128
    piece_shape = (2, full_width // 2, hidden // pieces)
    kept_send, away_send, g_fc1_bias, norm2, x1, *grads = pl.pallas_call(
        functools.partial(mlp_kernel, orders, rows_dev),
        out_shape=[
            bf(tokens, send_lanes),
            bf(mp - 1, tokens, send_lanes),
            f32(1, hidden),
            f32(tokens, 2),
            f32(tokens, ch),
            *[bf(*piece_shape)] * (2 * pieces),
        ],
        in_specs=[pl.BlockSpec(memory_space=pltpu.SMEM), vmem, vmem, vmem] + [hbm] * 8,
        out_specs=[hbm, hbm, vmem, vmem, hbm] + [hbm] * (2 * pieces),
        scratch_shapes=[
            pltpu.VMEM(eo.shape, BF),
            table,
            pltpu.VMEM(base.shape, F32),
            pltpu.VMEM(fc1_weight.shape, BF),
            pltpu.VMEM(dact.shape, F32),
            pltpu.VMEM(fc2_weight.shape, BF),
            pltpu.VMEM(dyt.shape, BF),
            pltpu.VMEM((tokens, send_lanes), BF),
            pltpu.VMEM((mp - 1, tokens, send_lanes), BF),
            *[pltpu.VMEM(piece_shape, BF)] * (2 * pieces),
            pltpu.VMEM((tokens, full_width), BF),
            pltpu.VMEM((full_width, tokens), BF),
            pltpu.VMEM((tokens, hidden), BF),
            pltpu.VMEM((tokens, hidden), BF),
            pltpu.SemaphoreType.DMA((16 + 8 * pieces,)),
        ],
        compiler_params=pltpu.CompilerParams(vmem_limit_bytes=56 * 2**20),
        cost_estimate=pl.CostEstimate(
            flops=10 * tokens * full_width * hidden, bytes_accessed=16 * 2**20, transcendentals=0
        ),
    )(
        row_group,
        vectors_all,
        fc1_bias.reshape(1, hidden),
        jnp.asarray(places),
        eo,
        *lon,
        base,
        fc1_weight,
        dact,
        fc2_weight,
        dyt,
    )
    got = [
        lax.ppermute(away_send[i - 1], "mp", [(d, (d + i) % mp) for d in range(mp)])
        for i in range(1, mp)
    ]

    def exchanged(away, turn):
        return [swapped(a, order[turn], parts) for a, order in zip(away, orders)]

    rows_each = full_width // 4
    streams = [[kept] for kept in grads[0::2]]
    got_rows = exchanged(grads[1::2], 0)
    streams = [[*terms, part] for terms, part in zip(streams, got_rows)]
    away = [added(terms, rows_each, 2 * rows_each).astype(BF) for terms in streams]

    out_field, dx1, dfreq, sums2 = run(
        functools.partial(back_mix_kernel, columns, padded, full_width),
        [bf(rows_dev, columns, ch), f32(tokens, ch), bf(patches, ch), f32(8, ch)],
        [
            dy_all,
            norm2_gain,
            fc2_bias,
            *lon,
            norm2,
            x1,
            kept_send,
            *got,
        ],
        [pltpu.VMEM((tokens, ch), F32)],
        (3, 4),
        choice,
    )

    dz = to_other(dfreq, group).reshape(patches, ch)
    dz = later(dz, away)
    got_rows = exchanged(away, 1)
    spec_rows = 4 * size // parts
    send_rows = -(-(group + spec_rows + 2) // 8) * 8
    (sent,) = run(
        functools.partial(filter_back_kernel, blocks, size, group),
        [bf(parts, send_rows, ch)],
        [dz, *lat, spec, s, h, slope, gate, sums2, g_fc1_bias],
        [
            pltpu.VMEM((parts, send_rows, ch), F32),
            pltpu.VMEM((4 * size, ch), F32),
            pltpu.VMEM((max(parts, 16), ch), F32),
        ],
    )
    sent, got_rows, out_field = lax.optimization_barrier((sent, got_rows, out_field))
    out_field = with_layout_constraint(out_field, Layout(major_to_minor=(1, 0, 2)))
    streams = [[*terms, part] for terms, part in zip(streams, got_rows)]
    half = rows_each // 2
    kept = [added(terms, 0, half) for terms in streams]
    got_rows = exchanged([added(terms, half, rows_each).astype(BF) for terms in streams], 2)
    quarter = half // 2
    pairs = list(zip(kept, got_rows))
    away = [added(pair, quarter, half).astype(BF) for pair in pairs]
    kept = [added(pair, 0, quarter) for pair in pairs]
    sent = lax.all_to_all(sent, "lat", 0, 0, tiled=True)
    sent, out_field = together(sent, out_field)
    sent, kept, away = lax.optimization_barrier((sent, kept, away))
    kept, away = (jnp.concatenate(arrays, axis=2) for arrays in (kept, away))
    for bit in bits[3:-1]:
        pair = (kept, swapped(away, bit, parts))
        quarter //= 2
        kept, away = added(pair, 0, quarter), added(pair, quarter, 2 * quarter).astype(BF)
    got_last = swapped(away, bits[-1], parts)
    tail_rows = -(-(spec_rows + 6) // 16) * 16
    du, stat1, tail = run(
        functools.partial(back_norm_kernel, group, spec_rows, mp),
        [f32(tokens, ch), f32(tokens, 3), bf(parts, tail_rows, ch)],
        [sent, *lon, dx1, xh1, inv1, norm1_gain],
        [pltpu.VMEM((tail_rows, ch), F32)],
        (1, 2),
        choice,
    )
    stat1 = lax.psum(stat1, "mp")
    stat1, got_last = together(stat1, got_last)
    weights = kept + got_last.astype(F32)
    grad_field = dx1 + stat1[:, 2:] * (
        du * norm1_gain - (stat1[:, :1] + xh1 * stat1[:, 1:2]) * (1.0 / full_width)
    )
    grad_field = grad_field.reshape(rows_dev, padded, ch)[:, :columns]

    tail = lax.all_to_all(tail, "lat", 0, 0, tiled=True)
    hidden_bias = f32(hidden) if ch % 128 == 0 else f32(hidden // ch, ch)
    vector, weight, bias = f32(ch), f32(2, blocks, size, size), f32(2, blocks, size)
    g_n1g, g_n1b, g_w1, g_b1, g_w2, g_b2, g_n2g, g_n2b, g_fc1b, g_fc2b = run(
        functools.partial(close_kernel, spec_rows, blocks, size),
        [vector, vector, weight, bias, weight, bias, vector, vector, hidden_bias, vector],
        [tail],
        [pltpu.VMEM((4 * size, ch), F32)],
    )
    return (
        out_field,
        grad_field,
        g_n1g,
        g_n1b,
        g_w1,
        g_b1,
        g_w2,
        g_b2,
        g_n2g,
        g_n2b,
        weights[0],
        g_fc1b.reshape(hidden),
        weights[1].T,
        g_fc2b,
    )


def solution(mesh):
    placed = (
        P("lat", None, "mp"),
        P(),
        P(),
        P("mp"),
        P("mp"),
        P(None, "mp", None, None),
        P(None, "mp", None),
        P(None, "mp", None, None),
        P(None, "mp", None),
        P("mp"),
        P("mp"),
        P(None, "mp"),
        P("mp"),
        P("mp", None),
        P("mp"),
        P("lat", None, "mp"),
    )
    return jax.shard_map(
        body,
        mesh=mesh,
        in_specs=placed,
        out_specs=(
            P("lat", None, "mp"),
            P("lat", None, "mp"),
            P("mp"),
            P("mp"),
            P(None, "mp", None, None),
            P(None, "mp", None),
            P(None, "mp", None, None),
            P(None, "mp", None),
            P("mp"),
            P("mp"),
            P("lat", "mp"),
            P("mp"),
            P("mp", "lat"),
            P("mp"),
        ),
        check_vma=False,
    )
```

```python
import functools
import math

import jax
import jax.numpy as jnp
import numpy as np
from jax import lax
from jax.experimental.layout import Layout, with_layout_constraint
from jax.experimental import pallas as pl
from jax.experimental.pallas import tpu as pltpu
from jax.sharding import PartitionSpec as P

LON_FINE = 180
LON_COARSE = 45
GROUPS = 8
EPSILON = 1e-05
SHRINK = 0.01
HALVES = LON_FINE // 2 + 1
BF = jnp.bfloat16
F32 = jnp.float32


def split_two(values):
    high = lax.reduce_precision(values, 8, 7)
    return high.astype(BF), (values - high).astype(BF)


def mm(left, right):
    return lax.dot_general(left, right, (((1,), (0,)), ((), ())), preferred_element_type=F32)


def mm_t(left, right):
    return lax.dot_general(left, right, (((0,), (0,)), ((), ())), preferred_element_type=F32)


def mm_nt(left, right):
    return lax.dot_general(left, right, (((1,), (1,)), ((), ())), preferred_element_type=F32)


def np_split(values):
    high = values.astype(jnp.bfloat16)
    low = (values - high.astype(np.float32)).astype(jnp.bfloat16)
    return high, low


def row_tables(row_group, row_valid):
    member = (row_group[:, None] == jnp.arange(GROUPS, dtype=jnp.int32)[None, :]).astype(
        jnp.int32
    ) * row_valid[:, None]
    counts = jnp.sum(member, axis=0)
    before = jnp.cumsum(member, axis=0) - member
    offset = jnp.sum(before * member, axis=1)
    length = jnp.maximum(jnp.sum(member * counts[None, :], axis=1), 1)
    return (offset, length)


def latitude_tables(row_group, row_valid):
    offset, length = row_tables(row_group, row_valid)
    phases = offset[:, None] * offset[None, :] % length[:, None]
    lengths = length[:, None].astype(F32)
    angles = 2.0 * math.pi * phases.astype(F32) / lengths
    kept = (
        (row_group[:, None] == row_group[None, :])
        & (row_valid[:, None] > 0)
        & (row_valid[None, :] > 0)
    ).astype(F32) * lax.rsqrt(lengths)
    return kept * jnp.cos(angles), kept * jnp.sin(angles)


CHUNK = 512
GELU_A = math.sqrt(2.0 / math.pi)
GELU_B = 0.044715


def longitude_tables(parts, share, rows_dev, columns, padded):
    freq = np.arange(parts * share).reshape(parts, share)
    cols = np.arange(columns)
    pairs = []
    for width in (LON_COARSE, LON_FINE):
        angles = 2.0 * np.pi * ((freq[..., None] * cols) % width) / width
        inside = (freq[..., None] * 2 <= width) & (cols < width)
        scale = inside / np.sqrt(width)
        pairs.append(np.stack([scale * np.cos(angles), -scale * np.sin(angles)], axis=1))
    full = np.zeros((2**rows_dev, parts, rows_dev, 2, share, rows_dev, padded), np.float32)
    for choice in range(2**rows_dev):
        for r in range(rows_dev):
            full[choice, :, r, :, :, r, :columns] = pairs[(choice >> r) & 1]
    return np_split(full.reshape(2**rows_dev, parts * rows_dev * 2 * share, rows_dev * padded))


def latitude_spread(rows, share):
    left = np.kron(np.eye(rows), np.ones((share, 1)))
    right = np.zeros((2, 2, 2, rows, rows, 2, share))
    signs = {
        (0, 0): ((1, 0), (0, 1)),
        (1, 0): ((0, 1), (-1, 0)),
        (0, 1): ((1, 0), (0, -1)),
        (1, 1): ((0, -1), (-1, 0)),
    }
    eye = np.eye(rows)[:, :, None]
    for (part, sign), (cos_sign, sin_sign) in signs.items():
        for inner in range(2):
            right[part, sign, 0, :, :, inner, :] = cos_sign[inner] * eye
            right[part, sign, 1, :, :, inner, :] = sin_sign[inner] * eye
    same = np.kron(np.ones((rows, 2 * rows)), np.eye(share))
    low = jnp.bfloat16
    return left.astype(low), right.reshape(4, 2 * rows, -1).astype(low), same.astype(low)


def split_in(values):
    high = values.astype(BF)
    return high, (values - high.astype(F32)).astype(BF)


def times(pair, values):
    high, low = split_in(values)
    width = values.shape[1]
    both = mm(pair[0], jnp.concatenate([high, low], axis=1))
    return both[:, :width] + both[:, width:] + mm(pair[1], high)


def times_t(pair, values):
    high, low = split_in(values)
    width = values.shape[1]
    both = mm_t(pair[0], jnp.concatenate([high, low], axis=1))
    return both[:, :width] + both[:, width:] + mm_t(pair[1], high)


def gelu_pair(v):
    square = v * v
    tanh = jnp.tanh(GELU_A * v * (1.0 + GELU_B * square))
    half = 0.5 * (1.0 + tanh)
    slope = half + 0.5 * v * (1.0 - tanh * tanh) * (GELU_A * (1.0 + 3.0 * GELU_B * square))
    return v * half, slope


def put_rows(ref, value, r, padded):
    ref[r * padded : r * padded + value.shape[0], :] = value


def column_sum(values):
    return jnp.sum(values, axis=0, keepdims=True)


def norm_one_kernel(columns, padded, groups, all_ref, gain, bias, high, low, freq, xh, inverse, pad, tables, sems):
    mp, rows_dev = all_ref.shape[0], all_ref.shape[1]
    width = mp * all_ref.shape[3]
    choice = width_choice(groups, rows_dev)
    copies = [
        pltpu.make_async_copy(src.at[choice], tables.at[i], sems.at[i])
        for i, src in enumerate((high, low))
    ]
    for copy in copies:
        copy.start()
    pad[...] = jnp.zeros_like(pad)
    for r in range(rows_dev):
        for m in range(mp):
            pad[m, r * padded : r * padded + columns, :] = all_ref[m, r].astype(F32)
    total = sum(jnp.sum(pad[m], axis=1, keepdims=True) for m in range(mp))
    average = total / width
    spread = sum(
        jnp.sum((pad[m] - average) * (pad[m] - average), axis=1, keepdims=True) for m in range(mp)
    )
    inv = lax.rsqrt(spread / width + EPSILON)
    x = pad[lax.axis_index("mp")]
    hat = (x - average) * inv
    u = hat * gain[...] + bias[...]
    xh[...] = hat
    inverse[...] = inv
    for copy in copies:
        copy.wait()
    freq[...] = times((tables[0], tables[1]), u)


def latitude_kernel(share, tables, left, right, same, keep, high_out, low_out):
    high, low = split_in(tables[...])
    for values, out in ((high, high_out), (low, low_out)):
        spread = mm(left[...], values).astype(BF)
        n = left.shape[0]
        for i in range(4):
            block = mm(spread, right[i]) * same[...].astype(F32)
            if i % 2:
                block = block * keep[...]
            out[i * n : (i + 1) * n, :] = block.astype(BF)


def block_mask(blocks, size):
    shape = (blocks * size, blocks * size)
    row = lax.broadcasted_iota(jnp.int32, shape, 0)
    col = lax.broadcasted_iota(jnp.int32, shape, 1)
    inside = None
    for n in range(blocks):
        one = (row >= n * size) & (row < (n + 1) * size) & (col >= n * size) & (col < (n + 1) * size)
        inside = one if inside is None else inside | one
    return inside


def diagonal(packed, blocks, size):
    whole = jnp.concatenate([packed.astype(F32)] * blocks, axis=0)
    return jnp.where(block_mask(blocks, size), whole, 0.0).astype(BF)


def gather_blocks(full, blocks, size):
    col = lax.broadcasted_iota(jnp.int32, (size, blocks * size), 1)
    out = None
    for n in range(blocks):
        piece = full[n * size : (n + 1) * size, :]
        piece = jnp.where((col >= n * size) & (col < (n + 1) * size), piece, 0.0)
        out = piece if out is None else out + piece
    return out


class Mover:
    def __init__(self, sems):
        self.sems, self.count, self.pending = sems, 0, []

    def start(self, src, dst):
        copy = pltpu.make_async_copy(src, dst, self.sems.at[self.count])
        self.count += 1
        copy.start()
        return copy

    def store(self, src, dst):
        self.pending.append(self.start(src, dst))

    def finish(self):
        for copy in self.pending:
            copy.wait()


def complex_blocks(real, imag, blocks, size):
    real, imag = diagonal(real, blocks, size), diagonal(imag, blocks, size)
    return jnp.concatenate(
        [jnp.concatenate([real, imag], axis=1), jnp.concatenate([-imag, real], axis=1)], axis=0
    )


def side_by_side(values):
    half = values.shape[0] // 2
    return jnp.concatenate([values[:half], values[half:]], axis=1)


def one_below(values):
    half = values.shape[1] // 2
    return jnp.concatenate([values[:, :half], values[:, half:]], axis=0)


def filter_kernel(blocks, size, z, high, low, weights, biases, eo, s_h, h_h, slope_h, gate_h, s_s, h_s, slope_s, gate_s, sems):
    move = Mover(sems)
    first = complex_blocks(weights[0], weights[1], blocks, size)
    second = complex_blocks(weights[2], weights[3], blocks, size)
    s = side_by_side(times((high[...], low[...]), z[...]).astype(BF))
    s_s[...] = s
    move.store(s_s, s_h)
    h, slope = gelu_pair(mm(s, first) + biases[0:1, :])
    h = h.astype(BF)
    slope_s[...] = slope
    move.store(slope_s, slope_h)
    h_s[...] = h
    move.store(h_s, h_h)
    a2 = mm(h, second) + biases[1:2, :]
    tanh = jnp.tanh(a2 * (1.0 / SHRINK))
    gate_s[...] = tanh * tanh
    move.store(gate_s, gate_h)
    eo[...] = times_t((high[...], low[...]), one_below(a2 - SHRINK * tanh)).astype(BF)
    move.finish()


def second_norm(parts_of):
    width = len(parts_of) * parts_of[0].shape[1]
    total = sum(jnp.sum(v, axis=1, keepdims=True) for v in parts_of)
    average = total / width
    spread = sum(jnp.sum((v - average) * (v - average), axis=1, keepdims=True) for v in parts_of)
    return average, lax.rsqrt(spread / width + EPSILON)


def swap_matrix(places):
    width = places.shape[0]
    lane = lax.broadcasted_iota(jnp.int32, (width, width), 1)
    share = width // lax.axis_size("lat")
    target = (places[:, 0:1] ^ lax.axis_index("lat")) * share + places[:, 1:2]
    return jnp.where(lane == target, 1.0, 0.0).astype(BF)


def cotangent_kernel(columns, padded, dy_all, places, field_all, vectors, dyt, dy_s, base, pad):
    mp, rows_dev, ch = dy_all.shape[0], dy_all.shape[1], dy_all.shape[3]

    for m in range(mp):
        pad[...] = jnp.zeros_like(pad)
        for r in range(rows_dev):
            pad[r * padded : r * padded + columns, :] = dy_all[m, r].astype(F32)
        dy_s[:, m * ch : (m + 1) * ch] = pad[...].astype(BF)
    dyt[...] = mm_nt(swap_matrix(places), dy_s[...]).astype(BF)
    for m in range(mp):
        base[m] = jnp.zeros(base.shape[1:], F32)
        for r in range(rows_dev):
            base[m, r * padded : r * padded + columns, :] = field_all[m, r].astype(F32)
    average, inv = second_norm([base[m] for m in range(mp)])
    for m in range(mp):
        x = base[m]
        base[m] = x + (x - average) * inv * vectors[m, 0:1, :] + vectors[m, 1:2, :]


def width_choice(groups, rows_dev):
    first = lax.axis_index("lat") * rows_dev
    choice = jnp.int32(0)
    for r in range(rows_dev):
        choice = choice + jnp.where(groups[first + r] == 0, 1 << r, 0).astype(jnp.int32)
    return choice


def mlp_kernel(orders, rows_dev, groups, vectors, b1, places, eo_h, high_h, low_h, base_h, w1_h, dy_h, w2_h, dyt_h, *refs):
    mp, pieces = vectors.shape[0], len(orders)
    kept_h, away_h, gb1, norm_out, own_h = refs[:5]
    grads_h = refs[5 : 5 + 2 * pieces]
    eo, table, base, w1, dy, w2, dyt, kept_send, away_send = refs[5 + 2 * pieces : 14 + 2 * pieces]
    grads = refs[14 + 2 * pieces : 14 + 4 * pieces]
    n_s, nt_s, q_s, dp_s, sems = refs[14 + 4 * pieces :]
    ch, width, hidden = base.shape[2], w1.shape[0], w1.shape[1]
    chunk = hidden // pieces
    mine = lax.axis_index("mp")
    choice = width_choice(groups, rows_dev)
    move = Mover(sems)
    first = [
        move.start(high_h.at[choice], table.at[0]),
        move.start(low_h.at[choice], table.at[1]),
        move.start(eo_h, eo),
        move.start(base_h, base),
    ]
    spans = [slice(p * chunk, (p + 1) * chunk) for p in range(pieces)]
    swap = swap_matrix(places)
    for copy in first:
        copy.wait()
    load_dy = move.start(dy_h, dy)
    loads = [
        (
            move.start(w1_h.at[:, span], w1.at[:, span]),
            move.start(w2_h.at[span, :], w2.at[span, :]),
        )
        for span in spans
    ]
    load_dyt = move.start(dyt_h, dyt)
    every = jnp.concatenate([eo[m] for m in range(mp)], axis=1)
    filtered = mm_t(table[0], every) + mm_t(table[1], every)
    for m in range(mp):
        base[m] = base[m] + filtered[:, m * ch : (m + 1) * ch]
    move.store(base.at[mine], own_h)
    average, inv = second_norm([base[m] for m in range(mp)])
    spot = lax.broadcasted_iota(jnp.int32, norm_out.shape, 1)
    norm_out[...] = jnp.where(spot == 0, average, inv)
    for m in range(mp):
        hat = (base[m] - average) * inv
        n_s[:, m * ch : (m + 1) * ch] = (hat * vectors[m, 2:3, :] + vectors[m, 3:4, :]).astype(BF)
    nt_s[...] = mm_nt(swap, n_s[...]).astype(BF)

    for piece, bits in enumerate(orders):
        span = spans[piece]
        for copy in loads[piece]:
            copy.wait()
        if piece == 0:
            load_dy.wait()
        dact = mm_nt(dy[...], w2[span, :])
        q, slope = gelu_pair(mm(n_s[...], w1[:, span]) + b1[:, span])
        q = q.astype(BF)
        q_s[:, span] = q
        dp = (dact * slope).astype(BF)
        dp_s[:, span] = dp
        gb1[:, span] = column_sum(dp.astype(F32))

    dn = mm_nt(dp_s[...], w1[...])
    plain, cross = 0.0, 0.0
    for m in range(mp):
        scaled = dn[:, m * ch : (m + 1) * ch] * vectors[m, 2:3, :]
        plain += jnp.sum(scaled, axis=1, keepdims=True)
        cross += jnp.sum(scaled * ((base[m] - average) * inv), axis=1, keepdims=True)
    spot = lax.broadcasted_iota(jnp.int32, (plain.shape[0], 128), 1)
    stat = jnp.zeros(spot.shape, F32)
    for at, value in ((0, plain), (3, cross)):
        for i in range(3):
            term = value.astype(BF).astype(F32)
            value = value - term
            stat = jnp.where(spot == at + i, term, stat)
    stat = stat.astype(BF)
    out = mm(q_s[...], w2[...])
    for m in range(mp):
        lanes = slice(m * ch, (m + 1) * ch)

        def put(ref):
            ref[:, :ch] = out[:, lanes].astype(BF)
            ref[:, ch : 2 * ch] = dn[:, lanes].astype(BF)
            ref[:, 2 * ch :] = stat

        @pl.when(mine == m)
        def _():
            put(kept_send)

        for other in range(mp):
            if other != m:

                @pl.when(mine == other)
                def _():
                    put(away_send.at[(m - other) % mp - 1])

    move.store(away_send, away_h)
    move.store(kept_send, kept_h)
    load_dyt.wait()
    for piece, bits in enumerate(orders):
        span = spans[piece]
        kept, away = grads[2 * piece : 2 * piece + 2]
        count = len(bits)
        rows = width >> count
        for i, grad in enumerate((mm(nt_s[...], dp_s[:, span]), mm(dyt[...], q_s[:, span]))):
            for place in range(2**count):
                who = sum(((place >> (count - 1 - b)) & 1) * bit for b, bit in enumerate(bits))
                block = grad[who * rows : (who + 1) * rows, :].astype(BF)
                at = (place % 2 ** (count - 1)) * rows
                (away if place >> (count - 1) else kept)[i, at : at + rows, :] = block
            move.store(away.at[i], grads_h[2 * piece + 1].at[i])
            move.store(kept.at[i], grads_h[2 * piece].at[i])
    move.finish()


def back_mix_kernel(columns, padded, width, choice, dy, gain, bias2, high, low, norm_in, own, *refs):
    got, (out_field, dx1, freq, sums, pad) = refs[:-5], refs[-5:]
    ch, rows_dev = own.shape[1], dy.shape[1]
    mine = lax.axis_index("mp")
    x1 = own[...]
    average, inv = norm_in[:, 0:1], norm_in[:, 1:2]
    hat = (x1 - average) * inv
    total = sum(piece[...].astype(F32) for piece in got)
    out = x1 + total[:, :ch] + bias2[...]
    dn = total[:, ch : 2 * ch]
    pad[...] = jnp.zeros_like(pad)
    for r in range(rows_dev):
        out_field[r] = out[r * padded : r * padded + columns, :].astype(BF)
        put_rows(pad, dy[mine, r].astype(F32), r, padded)
    grad = pad[...]
    sums[0:1, :] = column_sum(dn * hat)
    sums[1:2, :] = column_sum(dn)
    sums[2:3, :] = column_sum(grad)
    sums[3:8, :] = jnp.zeros((5, ch), F32)
    stats = total[:, 2 * ch : 2 * ch + 128]
    plain = (stats[:, 0:1] + stats[:, 1:2] + stats[:, 2:3]) / width
    cross = (stats[:, 3:4] + stats[:, 4:5] + stats[:, 5:6]) / width
    grad = grad + inv * (dn * gain[...] - plain - hat * cross)
    dx1[...] = grad
    freq[...] = times((high[0], low[0]), grad).astype(BF)


def filter_back_kernel(blocks, size, group, dz, high, low, weights, s_ref, h_ref, slope_ref, gate_ref, mlp_sums, hidden_sums, send, rows, grads_s, sums_s):
    first = complex_blocks(weights[0], weights[1], blocks, size)
    second = complex_blocks(weights[2], weights[3], blocks, size)
    ch = dz.shape[1]
    dsh = mm(high[...], dz[...]) + mm(low[...], dz[...])
    da = (side_by_side(dsh) * gate_ref[...]).astype(BF)
    dc = (mm_nt(da, second) * slope_ref[...]).astype(BF)
    out = times_t((high[...], low[...]), one_below(mm_nt(dc, first)))
    parts = rows.shape[0]
    for d in range(parts):
        rows[d, :group, :] = out[d * group : (d + 1) * group, :]
    for i, (left, right) in enumerate(((s_ref, dc), (h_ref, da))):
        outer = mm_t(left[...], right)
        pair = (outer[:ch, :ch] + outer[ch:, ch:], outer[:ch, ch:] - outer[ch:, :ch])
        for k, grad in enumerate(pair):
            at = (2 * i + k) * size
            grads_s[at : at + size, :] = gather_blocks(grad, blocks, size)
    sums_s[...] = jnp.zeros_like(sums_s)
    for i, grad in enumerate((dc, da)):
        total = column_sum(grad.astype(F32))
        sums_s[2 * i : 2 * i + 1, :] = total[:, :ch]
        sums_s[2 * i + 1 : 2 * i + 2, :] = total[:, ch:]
    sums_s[4:7, :] = mlp_sums[0:3, :]
    for i in range(hidden_sums.shape[1] // ch):
        sums_s[7 + i : 8 + i, :] = hidden_sums[:, i * ch : (i + 1) * ch]
    share = grads_s.shape[0] // parts
    at = group + share
    for d in range(parts):
        rows[d, group:at, :] = grads_s[d * share : (d + 1) * share, :]
        row = sums_s[d : d + 1, :]
        first = row.astype(BF).astype(F32)
        rows[d, at : at + 1, :] = first
        rows[d, at + 1 : at + 2, :] = row - first
        if at + 2 < rows.shape[1]:
            rows[d, at + 2 :, :] = jnp.zeros((rows.shape[1] - at - 2, rows.shape[2]), F32)
    send[...] = rows[...].astype(BF)


def back_norm_kernel(group, share, shares, choice, got, high, low, dx1, xh, inverse, gain, du_out, stat, tail, tail_s):
    parts, _, ch = got.shape
    every = got[...].astype(F32)
    deo = every[:, :group, :].reshape(parts * group, ch).astype(BF)
    at = group + share
    tail_s[...] = jnp.zeros_like(tail_s)
    tail_s[:share, :] = jnp.sum(every[:, group:at, :], axis=0)
    total = jnp.sum(every[:, at : at + 1, :], axis=0) + jnp.sum(every[:, at + 1 : at + 2, :], axis=0)
    du = dx1[...] + mm_t(high[0], deo) + mm_t(low[0], deo)
    du_out[...] = du
    hat = xh[...]
    scaled = du * gain[...]
    spot = lax.broadcasted_iota(jnp.int32, stat.shape, 1)
    plain = jnp.sum(scaled, axis=1, keepdims=True)
    cross = jnp.sum(scaled * hat, axis=1, keepdims=True)
    stat[...] = jnp.where(spot == 0, plain, jnp.where(spot == 1, cross, inverse[...] / shares))
    for i, row in enumerate((total, column_sum(du * hat), column_sum(du))):
        first = row.astype(BF).astype(F32)
        tail_s[share + 2 * i : share + 2 * i + 1, :] = first
        tail_s[share + 2 * i + 1 : share + 2 * i + 2, :] = row - first
    whole_tail = tail_s[...].astype(BF)
    for d in range(parts):
        tail[d] = whole_tail


def close_kernel(share, blocks, size, tail, n1g, n1b, w1, b1, w2, b2, n2g, n2b, gb1, gb2, rows):
    parts = tail.shape[0]
    for d in range(parts):
        rows[d * share : (d + 1) * share, :] = tail[d, :share, :].astype(F32)
    for i, out in enumerate((w1, w1, w2, w2)):
        for n in range(blocks):
            out[i % 2, n] = rows[i * size : (i + 1) * size, n * size : (n + 1) * size]

    def pair(d, i):
        both = tail[d, share + 2 * i : share + 2 * i + 2, :].astype(F32)
        return both[0:1] + both[1:2]

    for i, out in enumerate((b1, b1, b2, b2)):
        row = pair(i, 0)
        for n in range(blocks):
            out[i % 2, n : n + 1, :] = row[:, n * size : (n + 1) * size]
    n2g[...] = pair(4, 0)[0]
    n2b[...] = pair(5, 0)[0]
    gb2[...] = pair(6, 0)[0]
    ch = tail.shape[2]
    for i in range(math.prod(gb1.shape) // ch):
        row = pair(7 + i, 0)
        if gb1.ndim == 1:
            gb1[i * ch : (i + 1) * ch] = row[0]
        else:
            gb1[i : i + 1, :] = row
    n1g[...] = sum(pair(d, 1) for d in range(parts))[0]
    n1b[...] = sum(pair(d, 2) for d in range(parts))[0]


def whole(shape, extra=0):
    return pl.BlockSpec(shape, lambda *_: (0,) * len(shape))


def run(kernel, outs, args, scratch=(), picked=(), choice=None, flops=0, limit=56):
    moved = sum(math.prod(a.shape) * a.dtype.itemsize for a in args)
    moved += sum(math.prod(o.shape) * o.dtype.itemsize for o in outs)
    params = pltpu.CompilerParams(vmem_limit_bytes=limit * 2**20)
    cost = pl.CostEstimate(flops=flops, bytes_accessed=moved, transcendentals=0)
    out_shape = [jax.ShapeDtypeStruct(o.shape, o.dtype) for o in outs]
    if choice is None:
        return pl.pallas_call(
            kernel,
            out_shape=out_shape,
            in_specs=[pl.BlockSpec(memory_space=pltpu.VMEM)] * len(args),
            out_specs=[pl.BlockSpec(memory_space=pltpu.VMEM)] * len(outs),
            scratch_shapes=list(scratch),
            compiler_params=params,
            cost_estimate=cost,
        )(*args)
    specs = [
        pl.BlockSpec((1, *a.shape[1:]), lambda i, c: (c[0], 0, 0)) if i in picked else whole(a.shape)
        for i, a in enumerate(args)
    ]
    return pl.pallas_call(
        kernel,
        out_shape=out_shape,
        grid_spec=pltpu.PrefetchScalarGridSpec(
            num_scalar_prefetch=1,
            grid=(1,),
            in_specs=specs,
            out_specs=[whole(o.shape) for o in outs],
            scratch_shapes=list(scratch),
        ),
        compiler_params=params,
        cost_estimate=cost,
    )(choice, *args)


def added(terms):
    return sum(term.astype(F32) for term in terms)


def swapped(away, bit, parts):
    return lax.ppermute(away, "lat", [(d, d ^ bit) for d in range(parts)])


def added(terms, first, end):
    return sum(t[:, first:end].astype(F32) for t in terms)


def later(value, arrays):
    return lax.optimization_barrier((value, arrays))[0]


def together(value, arrays):
    return lax.optimization_barrier((value, arrays))


def body(
    field,
    row_group,
    row_valid,
    norm1_gain,
    norm1_bias,
    spec_w1,
    spec_b1,
    spec_w2,
    spec_b2,
    norm2_gain,
    norm2_bias,
    fc1_weight,
    fc1_bias,
    fc2_weight,
    fc2_bias,
    cotangent,
):
    rows_dev, columns, ch = field.shape
    parts, mp = lax.axis_size("lat"), lax.axis_size("mp")
    me = lax.axis_index("lat")
    rows = rows_dev * parts
    full_width = ch * mp
    padded = -(-columns // 16) * 16
    tokens = rows_dev * padded
    blocks, size = spec_w1.shape[1], spec_w1.shape[2]
    hidden = fc1_weight.shape[1]
    share = -(-HALVES // parts)
    group = 2 * rows_dev * share
    patches = parts * group

    def f32(*shape):
        return jax.ShapeDtypeStruct(shape, F32)

    def bf(*shape):
        return jax.ShapeDtypeStruct(shape, BF)

    lon = [jnp.asarray(t) for t in longitude_tables(parts, share, rows_dev, columns, padded)]
    local_group = lax.dynamic_slice_in_dim(row_group, me * rows_dev, rows_dev)
    choice = sum(
        jnp.where(local_group[r] == 0, 1 << r, 0) for r in range(rows_dev)
    ).astype(jnp.int32).reshape(1)

    field_all = lax.all_gather(field, "mp", axis=0)
    table = pltpu.VMEM((2, patches, tokens), BF)
    freq, xh1, inv1 = pl.pallas_call(
        functools.partial(norm_one_kernel, columns, padded),
        out_shape=[f32(patches, ch), f32(tokens, ch), f32(tokens, 1)],
        in_specs=[pl.BlockSpec(memory_space=pltpu.SMEM)]
        + [pl.BlockSpec(memory_space=pltpu.VMEM)] * 3
        + [pl.BlockSpec(memory_space=pl.ANY)] * 2,
        out_specs=[pl.BlockSpec(memory_space=pltpu.VMEM)] * 3,
        scratch_shapes=[
            pltpu.VMEM((mp, tokens, ch), F32),
            table,
            pltpu.SemaphoreType.DMA((2,)),
        ],
        compiler_params=pltpu.CompilerParams(vmem_limit_bytes=56 * 2**20),
    )(row_group, field_all, norm1_gain, norm1_bias, *lon)

    def to_other(values, rows_each):
        return lax.all_to_all(values.reshape(parts, rows_each, ch), "lat", 0, 0, tiled=True)

    z = to_other(freq, group).reshape(patches, ch)

    cos_mat, sin_mat = latitude_tables(row_group, row_valid)
    width = jnp.where(row_group == 0, LON_FINE, LON_COARSE).astype(jnp.int32)
    here = me * share + jnp.arange(share, dtype=jnp.int32)
    lone = (here[None, :] == 0) | (2 * here[None, :] == width[:, None])
    keep = (1.0 - lone.astype(F32)).reshape(rows * share, 1)
    lat = run(
        functools.partial(latitude_kernel, share),
        [bf(2 * patches, patches)] * 2,
        [
            jnp.concatenate([cos_mat, sin_mat], axis=1),
            *(jnp.asarray(t) for t in latitude_spread(rows, share)),
            keep,
        ],
    )
    spec = jnp.stack([spec_w1, spec_w2]).transpose(0, 1, 3, 2, 4).reshape(4, size, ch)
    spec_bias = jnp.concatenate([spec_b1.reshape(1, 2 * ch), spec_b2.reshape(1, 2 * ch)], axis=0)
    vectors = jnp.concatenate([norm1_gain, norm1_bias, norm2_gain, norm2_bias]).reshape(4, ch)
    vectors_all = lax.all_gather(vectors, "mp", axis=0)
    dy_all = lax.all_gather(cotangent, "mp", axis=0)
    z, vectors_all, dy_all = lax.optimization_barrier((z, vectors_all, dy_all))

    saved = [bf(patches, 2 * ch), bf(patches, 2 * ch), f32(patches, 2 * ch), f32(patches, 2 * ch)]
    vmem, hbm = pl.BlockSpec(memory_space=pltpu.VMEM), pl.BlockSpec(memory_space=pl.ANY)
    eo, s, h, slope, gate = pl.pallas_call(
        functools.partial(filter_kernel, blocks, size),
        out_shape=[bf(patches, ch), *saved],
        in_specs=[vmem] * 5,
        out_specs=[vmem] + [hbm] * 4,
        scratch_shapes=[pltpu.VMEM(a.shape, a.dtype) for a in saved]
        + [pltpu.SemaphoreType.DMA((4,))],
        compiler_params=pltpu.CompilerParams(vmem_limit_bytes=56 * 2**20),
    )(z, *lat, spec, spec_bias)
    chunk = CHUNK if hidden % (3 * CHUNK) == 0 else 256
    steps = hidden // chunk
    bits = [1 << b for b in range(parts.bit_length() - 1)]
    orders = [bits[i:3] + bits[:i] + bits[3:] for i in range(3)]
    pieces = len(orders)
    share_rows = full_width // parts
    places = np.stack(
        [np.arange(full_width) // share_rows, np.arange(full_width) % share_rows], axis=1
    ).astype(np.int32)
    dyt, dy_pad, base = run(
        functools.partial(cotangent_kernel, columns, padded),
        [bf(full_width, tokens), bf(tokens, full_width), f32(mp, tokens, ch)],
        [dy_all, jnp.asarray(places), field_all, vectors_all],
        [pltpu.VMEM((tokens, ch), F32)],
    )
    eo = to_other(eo, group).reshape(patches, ch)
    eo, dyt, dy_pad, base = lax.optimization_barrier((eo, dyt, dy_pad, base))
    eo = lax.all_gather(eo, "mp", axis=0)

    send_lanes = 2 * ch + 128
    piece_shape = (2, full_width // 2, hidden // pieces)
    kept_send, away_send, g_fc1_bias, norm2, x1, *grads = pl.pallas_call(
        functools.partial(mlp_kernel, orders, rows_dev),
        out_shape=[
            bf(tokens, send_lanes),
            bf(mp - 1, tokens, send_lanes),
            f32(1, hidden),
            f32(tokens, 2),
            f32(tokens, ch),
            *[bf(*piece_shape)] * (2 * pieces),
        ],
        in_specs=[pl.BlockSpec(memory_space=pltpu.SMEM), vmem, vmem, vmem] + [hbm] * 8,
        out_specs=[hbm, hbm, vmem, vmem, hbm] + [hbm] * (2 * pieces),
        scratch_shapes=[
            pltpu.VMEM(eo.shape, BF),
            table,
            pltpu.VMEM(base.shape, F32),
            pltpu.VMEM(fc1_weight.shape, BF),
            pltpu.VMEM(dy_pad.shape, BF),
            pltpu.VMEM(fc2_weight.shape, BF),
            pltpu.VMEM(dyt.shape, BF),
            pltpu.VMEM((tokens, send_lanes), BF),
            pltpu.VMEM((mp - 1, tokens, send_lanes), BF),
            *[pltpu.VMEM(piece_shape, BF)] * (2 * pieces),
            pltpu.VMEM((tokens, full_width), BF),
            pltpu.VMEM((full_width, tokens), BF),
            pltpu.VMEM((tokens, hidden), BF),
            pltpu.VMEM((tokens, hidden), BF),
            pltpu.SemaphoreType.DMA((16 + 8 * pieces,)),
        ],
        compiler_params=pltpu.CompilerParams(vmem_limit_bytes=56 * 2**20),
        cost_estimate=pl.CostEstimate(
            flops=10 * tokens * full_width * hidden, bytes_accessed=16 * 2**20, transcendentals=0
        ),
    )(
        row_group,
        vectors_all,
        fc1_bias.reshape(1, hidden),
        jnp.asarray(places),
        eo,
        *lon,
        base,
        fc1_weight,
        dy_pad,
        fc2_weight,
        dyt,
    )
    got = [
        lax.ppermute(away_send[i - 1], "mp", [(d, (d + i) % mp) for d in range(mp)])
        for i in range(1, mp)
    ]

    def exchanged(away, turn):
        return [swapped(a, order[turn], parts) for a, order in zip(away, orders)]

    rows_each = full_width // 4
    streams = [[kept] for kept in grads[0::2]]
    got_rows = exchanged(grads[1::2], 0)
    streams = [[*terms, part] for terms, part in zip(streams, got_rows)]
    away = [added(terms, rows_each, 2 * rows_each).astype(BF) for terms in streams]

    out_field, dx1, dfreq, sums2 = run(
        functools.partial(back_mix_kernel, columns, padded, full_width),
        [bf(rows_dev, columns, ch), f32(tokens, ch), bf(patches, ch), f32(8, ch)],
        [
            dy_all,
            norm2_gain,
            fc2_bias,
            *lon,
            norm2,
            x1,
            kept_send,
            *got,
        ],
        [pltpu.VMEM((tokens, ch), F32)],
        (3, 4),
        choice,
    )

    dz = to_other(dfreq, group).reshape(patches, ch)
    dz = later(dz, away)
    got_rows = exchanged(away, 1)
    spec_rows = 4 * size // parts
    send_rows = -(-(group + spec_rows + 2) // 8) * 8
    (sent,) = run(
        functools.partial(filter_back_kernel, blocks, size, group),
        [bf(parts, send_rows, ch)],
        [dz, *lat, spec, s, h, slope, gate, sums2, g_fc1_bias],
        [
            pltpu.VMEM((parts, send_rows, ch), F32),
            pltpu.VMEM((4 * size, ch), F32),
            pltpu.VMEM((max(parts, 16), ch), F32),
        ],
    )
    sent, got_rows, out_field = lax.optimization_barrier((sent, got_rows, out_field))
    out_field = with_layout_constraint(out_field, Layout(major_to_minor=(1, 0, 2)))
    streams = [[*terms, part] for terms, part in zip(streams, got_rows)]
    half = rows_each // 2
    kept = [added(terms, 0, half) for terms in streams]
    got_rows = exchanged([added(terms, half, rows_each).astype(BF) for terms in streams], 2)
    quarter = half // 2
    pairs = list(zip(kept, got_rows))
    away = [added(pair, quarter, half).astype(BF) for pair in pairs]
    kept = [added(pair, 0, quarter) for pair in pairs]
    sent = lax.all_to_all(sent, "lat", 0, 0, tiled=True)
    sent, out_field = together(sent, out_field)
    sent, kept, away = lax.optimization_barrier((sent, kept, away))
    kept, away = (jnp.concatenate(arrays, axis=2) for arrays in (kept, away))
    for bit in bits[3:-1]:
        pair = (kept, swapped(away, bit, parts))
        quarter //= 2
        kept, away = added(pair, 0, quarter), added(pair, quarter, 2 * quarter).astype(BF)
    got_last = swapped(away, bits[-1], parts)
    tail_rows = -(-(spec_rows + 6) // 16) * 16
    du, stat1, tail = run(
        functools.partial(back_norm_kernel, group, spec_rows, mp),
        [f32(tokens, ch), f32(tokens, 3), bf(parts, tail_rows, ch)],
        [sent, *lon, dx1, xh1, inv1, norm1_gain],
        [pltpu.VMEM((tail_rows, ch), F32)],
        (1, 2),
        choice,
    )
    stat1 = lax.psum(stat1, "mp")
    stat1, got_last = together(stat1, got_last)
    weights = kept + got_last.astype(F32)
    grad_field = dx1 + stat1[:, 2:] * (
        du * norm1_gain - (stat1[:, :1] + xh1 * stat1[:, 1:2]) * (1.0 / full_width)
    )
    grad_field = grad_field.reshape(rows_dev, padded, ch)[:, :columns]

    tail = lax.all_to_all(tail, "lat", 0, 0, tiled=True)
    hidden_bias = f32(hidden) if ch % 128 == 0 else f32(hidden // ch, ch)
    vector, weight, bias = f32(ch), f32(2, blocks, size, size), f32(2, blocks, size)
    g_n1g, g_n1b, g_w1, g_b1, g_w2, g_b2, g_n2g, g_n2b, g_fc1b, g_fc2b = run(
        functools.partial(close_kernel, spec_rows, blocks, size),
        [vector, vector, weight, bias, weight, bias, vector, vector, hidden_bias, vector],
        [tail],
        [pltpu.VMEM((4 * size, ch), F32)],
        limit=24,
    )
    return (
        out_field,
        grad_field,
        g_n1g,
        g_n1b,
        g_w1,
        g_b1,
        g_w2,
        g_b2,
        g_n2g,
        g_n2b,
        weights[0],
        g_fc1b.reshape(hidden),
        weights[1].T,
        g_fc2b,
    )


def solution(mesh):
    placed = (
        P("lat", None, "mp"),
        P(),
        P(),
        P("mp"),
        P("mp"),
        P(None, "mp", None, None),
        P(None, "mp", None),
        P(None, "mp", None, None),
        P(None, "mp", None),
        P("mp"),
        P("mp"),
        P(None, "mp"),
        P("mp"),
        P("mp", None),
        P("mp"),
        P("lat", None, "mp"),
    )
    return jax.shard_map(
        body,
        mesh=mesh,
        in_specs=placed,
        out_specs=(
            P("lat", None, "mp"),
            P("lat", None, "mp"),
            P("mp"),
            P("mp"),
            P(None, "mp", None, None),
            P(None, "mp", None),
            P(None, "mp", None, None),
            P(None, "mp", None),
            P("mp"),
            P("mp"),
            P("lat", "mp"),
            P("mp"),
            P("mp", "lat"),
            P("mp"),
        ),
        check_vma=False,
    )
```

```python
import functools
import math

import jax
import jax.numpy as jnp
import numpy as np
from jax import lax
from jax.experimental import pallas as pl
from jax.experimental.pallas import tpu as pltpu
from jax.sharding import PartitionSpec as P

LON_FINE = 180
LON_COARSE = 45
GROUPS = 8
EPSILON = 1e-05
SHRINK = 0.01
HALVES = LON_FINE // 2 + 1
BF = jnp.bfloat16
F32 = jnp.float32


def split_two(values):
    high = lax.reduce_precision(values, 8, 7)
    return high.astype(BF), (values - high).astype(BF)


def mm(left, right):
    return lax.dot_general(left, right, (((1,), (0,)), ((), ())), preferred_element_type=F32)


def mm_t(left, right):
    return lax.dot_general(left, right, (((0,), (0,)), ((), ())), preferred_element_type=F32)


def mm_nt(left, right):
    return lax.dot_general(left, right, (((1,), (1,)), ((), ())), preferred_element_type=F32)


def np_split(values):
    high = values.astype(jnp.bfloat16)
    low = (values - high.astype(np.float32)).astype(jnp.bfloat16)
    return high, low


def row_tables(row_group, row_valid):
    member = (row_group[:, None] == jnp.arange(GROUPS, dtype=jnp.int32)[None, :]).astype(
        jnp.int32
    ) * row_valid[:, None]
    counts = jnp.sum(member, axis=0)
    before = jnp.cumsum(member, axis=0) - member
    offset = jnp.sum(before * member, axis=1)
    length = jnp.maximum(jnp.sum(member * counts[None, :], axis=1), 1)
    return (offset, length)


def latitude_tables(row_group, row_valid):
    offset, length = row_tables(row_group, row_valid)
    phases = offset[:, None] * offset[None, :] % length[:, None]
    lengths = length[:, None].astype(F32)
    angles = 2.0 * math.pi * phases.astype(F32) / lengths
    kept = (
        (row_group[:, None] == row_group[None, :])
        & (row_valid[:, None] > 0)
        & (row_valid[None, :] > 0)
    ).astype(F32) * lax.rsqrt(lengths)
    return kept * jnp.cos(angles), kept * jnp.sin(angles)


CHUNK = 512
GELU_A = math.sqrt(2.0 / math.pi)
GELU_B = 0.044715


def longitude_tables(parts, share, rows_dev, columns, padded):
    freq = np.arange(parts * share).reshape(parts, share)
    cols = np.arange(columns)
    pairs = []
    for width in (LON_COARSE, LON_FINE):
        angles = 2.0 * np.pi * ((freq[..., None] * cols) % width) / width
        inside = (freq[..., None] * 2 <= width) & (cols < width)
        scale = inside / np.sqrt(width)
        pairs.append(np.stack([scale * np.cos(angles), -scale * np.sin(angles)], axis=1))
    full = np.zeros((2**rows_dev, parts, rows_dev, 2, share, rows_dev, padded), np.float32)
    for choice in range(2**rows_dev):
        for r in range(rows_dev):
            full[choice, :, r, :, :, r, :columns] = pairs[(choice >> r) & 1]
    return np_split(full.reshape(2**rows_dev, parts * rows_dev * 2 * share, rows_dev * padded))


def latitude_spread(rows, share):
    left = np.kron(np.eye(rows), np.ones((share, 1)))
    right = np.zeros((2, 2, 2, rows, rows, 2, share))
    signs = {
        (0, 0): ((1, 0), (0, 1)),
        (1, 0): ((0, 1), (-1, 0)),
        (0, 1): ((1, 0), (0, -1)),
        (1, 1): ((0, -1), (-1, 0)),
    }
    eye = np.eye(rows)[:, :, None]
    for (part, sign), (cos_sign, sin_sign) in signs.items():
        for inner in range(2):
            right[part, sign, 0, :, :, inner, :] = cos_sign[inner] * eye
            right[part, sign, 1, :, :, inner, :] = sin_sign[inner] * eye
    same = np.kron(np.ones((rows, 2 * rows)), np.eye(share))
    low = jnp.bfloat16
    return left.astype(low), right.reshape(4, 2 * rows, -1).astype(low), same.astype(low)


def split_in(values):
    high = values.astype(BF)
    return high, (values - high.astype(F32)).astype(BF)


def times(pair, values):
    high, low = split_in(values)
    width = values.shape[1]
    both = mm(pair[0], jnp.concatenate([high, low], axis=1))
    return both[:, :width] + both[:, width:] + mm(pair[1], high)


def times_t(pair, values):
    high, low = split_in(values)
    width = values.shape[1]
    both = mm_t(pair[0], jnp.concatenate([high, low], axis=1))
    return both[:, :width] + both[:, width:] + mm_t(pair[1], high)


def gelu_pair(v):
    square = v * v
    tanh = jnp.tanh(GELU_A * v * (1.0 + GELU_B * square))
    half = 0.5 * (1.0 + tanh)
    slope = half + 0.5 * v * (1.0 - tanh * tanh) * (GELU_A * (1.0 + 3.0 * GELU_B * square))
    return v * half, slope


def put_rows(ref, value, r, padded):
    ref[r * padded : r * padded + value.shape[0], :] = value


def column_sum(values):
    return jnp.sum(values, axis=0, keepdims=True)


def norm_one_kernel(columns, padded, groups, all_ref, gain, bias, high, low, freq, pad, tables, sems):
    mp, rows_dev = all_ref.shape[0], all_ref.shape[1]
    width = mp * all_ref.shape[3]
    choice = width_choice(groups, rows_dev)
    copies = [
        pltpu.make_async_copy(src.at[choice], tables.at[i], sems.at[i])
        for i, src in enumerate((high, low))
    ]
    for copy in copies:
        copy.start()
    pad[...] = jnp.zeros_like(pad)
    for r in range(rows_dev):
        for m in range(mp):
            pad[m, r * padded : r * padded + columns, :] = all_ref[m, r].astype(F32)
    total = sum(jnp.sum(pad[m], axis=1, keepdims=True) for m in range(mp))
    average = total / width
    spread = sum(
        jnp.sum((pad[m] - average) * (pad[m] - average), axis=1, keepdims=True) for m in range(mp)
    )
    inv = lax.rsqrt(spread / width + EPSILON)
    x = pad[lax.axis_index("mp")]
    hat = (x - average) * inv
    u = hat * gain[...] + bias[...]
    for copy in copies:
        copy.wait()
    freq[...] = times((tables[0], tables[1]), u)


def latitude_kernel(share, tables, left, right, same, keep, high_out, low_out):
    high, low = split_in(tables[...])
    for values, out in ((high, high_out), (low, low_out)):
        spread = mm(left[...], values).astype(BF)
        n = left.shape[0]
        for i in range(4):
            block = mm(spread, right[i]) * same[...].astype(F32)
            if i % 2:
                block = block * keep[...]
            out[i * n : (i + 1) * n, :] = block.astype(BF)


def block_mask(blocks, size):
    shape = (blocks * size, blocks * size)
    row = lax.broadcasted_iota(jnp.int32, shape, 0)
    col = lax.broadcasted_iota(jnp.int32, shape, 1)
    inside = None
    for n in range(blocks):
        one = (row >= n * size) & (row < (n + 1) * size) & (col >= n * size) & (col < (n + 1) * size)
        inside = one if inside is None else inside | one
    return inside


def diagonal(packed, blocks, size):
    whole = jnp.concatenate([packed.astype(F32)] * blocks, axis=0)
    return jnp.where(block_mask(blocks, size), whole, 0.0).astype(BF)


def gather_blocks(full, blocks, size):
    col = lax.broadcasted_iota(jnp.int32, (size, blocks * size), 1)
    out = None
    for n in range(blocks):
        piece = full[n * size : (n + 1) * size, :]
        piece = jnp.where((col >= n * size) & (col < (n + 1) * size), piece, 0.0)
        out = piece if out is None else out + piece
    return out


class Mover:
    def __init__(self, sems):
        self.sems, self.count, self.pending = sems, 0, []

    def start(self, src, dst):
        copy = pltpu.make_async_copy(src, dst, self.sems.at[self.count])
        self.count += 1
        copy.start()
        return copy

    def store(self, src, dst):
        self.pending.append(self.start(src, dst))

    def finish(self):
        for copy in self.pending:
            copy.wait()


def complex_blocks(real, imag, blocks, size):
    real, imag = diagonal(real, blocks, size), diagonal(imag, blocks, size)
    return jnp.concatenate(
        [jnp.concatenate([real, imag], axis=1), jnp.concatenate([-imag, real], axis=1)], axis=0
    )


def side_by_side(values):
    half = values.shape[0] // 2
    return jnp.concatenate([values[:half], values[half:]], axis=1)


def one_below(values):
    half = values.shape[1] // 2
    return jnp.concatenate([values[:, :half], values[:, half:]], axis=0)


def filter_kernel(blocks, size, z, high, low, weights, biases, eo, s_h, h_h, slope_h, gate_h, s_s, h_s, slope_s, gate_s, sems):
    move = Mover(sems)
    first = complex_blocks(weights[0], weights[1], blocks, size)
    second = complex_blocks(weights[2], weights[3], blocks, size)
    s = side_by_side(times((high[...], low[...]), z[...]).astype(BF))
    s_s[...] = s
    move.store(s_s, s_h)
    h, slope = gelu_pair(mm(s, first) + biases[0:1, :])
    h = h.astype(BF)
    slope_s[...] = slope
    move.store(slope_s, slope_h)
    h_s[...] = h
    move.store(h_s, h_h)
    a2 = mm(h, second) + biases[1:2, :]
    tanh = jnp.tanh(a2 * (1.0 / SHRINK))
    gate_s[...] = tanh * tanh
    move.store(gate_s, gate_h)
    eo[...] = times_t((high[...], low[...]), one_below(a2 - SHRINK * tanh)).astype(BF)
    move.finish()


def second_norm(parts_of):
    width = len(parts_of) * parts_of[0].shape[1]
    total = sum(jnp.sum(v, axis=1, keepdims=True) for v in parts_of)
    average = total / width
    spread = sum(jnp.sum((v - average) * (v - average), axis=1, keepdims=True) for v in parts_of)
    return average, lax.rsqrt(spread / width + EPSILON)


def swap_matrix(places):
    width = places.shape[0]
    lane = lax.broadcasted_iota(jnp.int32, (width, width), 1)
    share = width // lax.axis_size("lat")
    target = (places[:, 0:1] ^ lax.axis_index("lat")) * share + places[:, 1:2]
    return jnp.where(lane == target, 1.0, 0.0).astype(BF)


def cotangent_kernel(columns, padded, dy_all, places, field_all, vectors, dyt, dy_s, base, xh, inverse, pad):
    mp, rows_dev, ch = dy_all.shape[0], dy_all.shape[1], dy_all.shape[3]

    for m in range(mp):
        pad[...] = jnp.zeros_like(pad)
        for r in range(rows_dev):
            pad[r * padded : r * padded + columns, :] = dy_all[m, r].astype(F32)
        dy_s[:, m * ch : (m + 1) * ch] = pad[...].astype(BF)
    dyt[...] = mm_nt(swap_matrix(places), dy_s[...]).astype(BF)
    for m in range(mp):
        base[m] = jnp.zeros(base.shape[1:], F32)
        for r in range(rows_dev):
            base[m, r * padded : r * padded + columns, :] = field_all[m, r].astype(F32)
    average, inv = second_norm([base[m] for m in range(mp)])
    inverse[...] = inv
    xh[...] = (base[lax.axis_index("mp")] - average) * inv
    for m in range(mp):
        x = base[m]
        base[m] = x + (x - average) * inv * vectors[m, 0:1, :] + vectors[m, 1:2, :]


def width_choice(groups, rows_dev):
    first = lax.axis_index("lat") * rows_dev
    choice = jnp.int32(0)
    for r in range(rows_dev):
        choice = choice + jnp.where(groups[first + r] == 0, 1 << r, 0).astype(jnp.int32)
    return choice


def mlp_kernel(orders, rows_dev, groups, vectors, b1, places, eo_h, high_h, low_h, base_h, w1_h, dy_h, w2_h, dyt_h, *refs):
    mp, pieces = vectors.shape[0], len(orders)
    kept_h, away_h, gb1, norm_out, own_h = refs[:5]
    grads_h = refs[5 : 5 + 2 * pieces]
    eo, table, base, w1, dy, w2, dyt, kept_send, away_send = refs[5 + 2 * pieces : 14 + 2 * pieces]
    grads = refs[14 + 2 * pieces : 14 + 4 * pieces]
    n_s, nt_s, q_s, dp_s, sems = refs[14 + 4 * pieces :]
    ch, width, hidden = base.shape[2], w1.shape[0], w1.shape[1]
    chunk = hidden // pieces
    mine = lax.axis_index("mp")
    choice = width_choice(groups, rows_dev)
    move = Mover(sems)
    first = [
        move.start(high_h.at[choice], table.at[0]),
        move.start(low_h.at[choice], table.at[1]),
        move.start(eo_h, eo),
        move.start(base_h, base),
    ]
    spans = [slice(p * chunk, (p + 1) * chunk) for p in range(pieces)]
    load_dy = move.start(dy_h, dy)
    loads = [
        (
            move.start(w1_h.at[:, span], w1.at[:, span]),
            move.start(w2_h.at[span, :], w2.at[span, :]),
        )
        for span in spans
    ]
    load_dyt = move.start(dyt_h, dyt)
    swap = swap_matrix(places)
    for copy in first[:3]:
        copy.wait()
    every = jnp.concatenate([eo[m] for m in range(mp)], axis=1)
    filtered = mm_t(table[0], every) + mm_t(table[1], every)
    first[3].wait()
    for m in range(mp):
        base[m] = base[m] + filtered[:, m * ch : (m + 1) * ch]
    move.store(base.at[mine], own_h)
    average, inv = second_norm([base[m] for m in range(mp)])
    spot = lax.broadcasted_iota(jnp.int32, norm_out.shape, 1)
    norm_out[...] = jnp.where(spot == 0, average, inv)
    for m in range(mp):
        hat = (base[m] - average) * inv
        n_s[:, m * ch : (m + 1) * ch] = (hat * vectors[m, 2:3, :] + vectors[m, 3:4, :]).astype(BF)
    nt_s[...] = mm_nt(swap, n_s[...]).astype(BF)

    for piece, bits in enumerate(orders):
        span = spans[piece]
        for copy in loads[piece]:
            copy.wait()
        if piece == 0:
            load_dy.wait()
        dact = mm_nt(dy[...], w2[span, :])
        q, slope = gelu_pair(mm(n_s[...], w1[:, span]) + b1[:, span])
        q = q.astype(BF)
        q_s[:, span] = q
        dp = (dact * slope).astype(BF)
        dp_s[:, span] = dp
        gb1[:, span] = column_sum(dp.astype(F32))

    dn = mm_nt(dp_s[...], w1[...])
    plain, cross = 0.0, 0.0
    for m in range(mp):
        scaled = dn[:, m * ch : (m + 1) * ch] * vectors[m, 2:3, :]
        plain += jnp.sum(scaled, axis=1, keepdims=True)
        cross += jnp.sum(scaled * ((base[m] - average) * inv), axis=1, keepdims=True)
    spot = lax.broadcasted_iota(jnp.int32, (plain.shape[0], 128), 1)
    stat = jnp.zeros(spot.shape, F32)
    for at, value in ((0, plain), (3, cross)):
        for i in range(3):
            term = value.astype(BF).astype(F32)
            value = value - term
            stat = jnp.where(spot == at + i, term, stat)
    stat = stat.astype(BF)
    out = mm(q_s[...], w2[...])
    for m in range(mp):
        lanes = slice(m * ch, (m + 1) * ch)

        def put(ref):
            ref[:, :ch] = dn[:, lanes].astype(BF)
            ref[:, ch : ch + 128] = stat
            ref[:, ch + 128 :] = out[:, lanes].astype(BF)

        @pl.when(mine == m)
        def _():
            put(kept_send)

        for other in range(mp):
            if other != m:

                @pl.when(mine == other)
                def _():
                    put(away_send.at[(m - other) % mp - 1])

    move.store(away_send, away_h)
    move.store(kept_send, kept_h)
    load_dyt.wait()
    for piece, bits in enumerate(orders):
        span = spans[piece]
        kept, away = grads[2 * piece : 2 * piece + 2]
        count = len(bits)
        rows = width >> count
        for i, grad in enumerate((mm(nt_s[...], dp_s[:, span]), mm(dyt[...], q_s[:, span]))):
            for place in range(2**count):
                who = sum(((place >> (count - 1 - b)) & 1) * bit for b, bit in enumerate(bits))
                block = grad[who * rows : (who + 1) * rows, :].astype(BF)
                at = (place % 2 ** (count - 1)) * rows
                (away if place >> (count - 1) else kept)[i, at : at + rows, :] = block
            move.store(away.at[i], grads_h[2 * piece + 1].at[i])
            move.store(kept.at[i], grads_h[2 * piece].at[i])
    move.finish()


def back_mix_kernel(columns, padded, width, choice, dy, gain, high, low, norm_in, own, *refs):
    got, (dx1, freq, sums, pad) = refs[:-4], refs[-4:]
    ch, rows_dev = own.shape[1], dy.shape[1]
    mine = lax.axis_index("mp")
    x1 = own[...]
    average, inv = norm_in[:, 0:1], norm_in[:, 1:2]
    hat = (x1 - average) * inv
    total = sum(piece[:, : ch + 128].astype(F32) for piece in got)
    dn = total[:, :ch]
    pad[...] = jnp.zeros_like(pad)
    for r in range(rows_dev):
        put_rows(pad, dy[mine, r].astype(F32), r, padded)
    grad = pad[...]
    sums[0:1, :] = column_sum(dn * hat)
    sums[1:2, :] = column_sum(dn)
    sums[2:3, :] = column_sum(grad)
    sums[3:8, :] = jnp.zeros((5, ch), F32)
    stats = total[:, ch:]
    plain = (stats[:, 0:1] + stats[:, 1:2] + stats[:, 2:3]) / width
    cross = (stats[:, 3:4] + stats[:, 4:5] + stats[:, 5:6]) / width
    grad = grad + inv * (dn * gain[...] - plain - hat * cross)
    dx1[...] = grad
    freq[...] = times((high[0], low[0]), grad).astype(BF)


def filter_back_kernel(blocks, size, group, dz, high, low, weights, s_ref, h_ref, slope_ref, gate_ref, mlp_sums, hidden_sums, send, rows, grads_s, sums_s):
    first = complex_blocks(weights[0], weights[1], blocks, size)
    second = complex_blocks(weights[2], weights[3], blocks, size)
    ch = dz.shape[1]
    dsh = mm(high[...], dz[...]) + mm(low[...], dz[...])
    da = (side_by_side(dsh) * gate_ref[...]).astype(BF)
    dc = (mm_nt(da, second) * slope_ref[...]).astype(BF)
    out = times_t((high[...], low[...]), one_below(mm_nt(dc, first)))
    parts = rows.shape[0]
    for d in range(parts):
        rows[d, :group, :] = out[d * group : (d + 1) * group, :]
    for i, (left, right) in enumerate(((s_ref, dc), (h_ref, da))):
        outer = mm_t(left[...], right)
        pair = (outer[:ch, :ch] + outer[ch:, ch:], outer[:ch, ch:] - outer[ch:, :ch])
        for k, grad in enumerate(pair):
            at = (2 * i + k) * size
            grads_s[at : at + size, :] = gather_blocks(grad, blocks, size)
    sums_s[...] = jnp.zeros_like(sums_s)
    for i, grad in enumerate((dc, da)):
        total = column_sum(grad.astype(F32))
        sums_s[2 * i : 2 * i + 1, :] = total[:, :ch]
        sums_s[2 * i + 1 : 2 * i + 2, :] = total[:, ch:]
    sums_s[4:7, :] = mlp_sums[0:3, :]
    for i in range(hidden_sums.shape[1] // ch):
        sums_s[7 + i : 8 + i, :] = hidden_sums[:, i * ch : (i + 1) * ch]
    share = grads_s.shape[0] // parts
    at = group + share
    for d in range(parts):
        rows[d, group:at, :] = grads_s[d * share : (d + 1) * share, :]
        row = sums_s[d : d + 1, :]
        first = row.astype(BF).astype(F32)
        rows[d, at : at + 1, :] = first
        rows[d, at + 1 : at + 2, :] = row - first
        if at + 2 < rows.shape[1]:
            rows[d, at + 2 :, :] = jnp.zeros((rows.shape[1] - at - 2, rows.shape[2]), F32)
    send[...] = rows[...].astype(BF)


def back_norm_kernel(group, share, shares, choice, got, high, low, dx1, xh, inverse, gain, du_out, stat, tail, tail_s):
    parts, _, ch = got.shape
    every = got[...].astype(F32)
    deo = every[:, :group, :].reshape(parts * group, ch).astype(BF)
    at = group + share
    tail_s[...] = jnp.zeros_like(tail_s)
    tail_s[:share, :] = jnp.sum(every[:, group:at, :], axis=0)
    total = jnp.sum(every[:, at : at + 1, :], axis=0) + jnp.sum(every[:, at + 1 : at + 2, :], axis=0)
    du = dx1[...] + mm_t(high[0], deo) + mm_t(low[0], deo)
    du_out[...] = du
    hat = xh[...]
    scaled = du * gain[...]
    spot = lax.broadcasted_iota(jnp.int32, stat.shape, 1)
    plain = jnp.sum(scaled, axis=1, keepdims=True)
    cross = jnp.sum(scaled * hat, axis=1, keepdims=True)
    stat[...] = jnp.where(spot == 0, plain, jnp.where(spot == 1, cross, inverse[...] / shares))
    for i, row in enumerate((total, column_sum(du * hat), column_sum(du))):
        first = row.astype(BF).astype(F32)
        tail_s[share + 2 * i : share + 2 * i + 1, :] = first
        tail_s[share + 2 * i + 1 : share + 2 * i + 2, :] = row - first
    whole_tail = tail_s[...].astype(BF)
    for d in range(parts):
        tail[d] = whole_tail


def close_kernel(share, blocks, size, tail, n1g, n1b, w1, b1, w2, b2, n2g, n2b, gb1, gb2, rows):
    parts = tail.shape[0]
    for d in range(parts):
        rows[d * share : (d + 1) * share, :] = tail[d, :share, :].astype(F32)
    for i, out in enumerate((w1, w1, w2, w2)):
        for n in range(blocks):
            out[i % 2, n] = rows[i * size : (i + 1) * size, n * size : (n + 1) * size]

    def pair(d, i):
        both = tail[d, share + 2 * i : share + 2 * i + 2, :].astype(F32)
        return both[0:1] + both[1:2]

    for i, out in enumerate((b1, b1, b2, b2)):
        row = pair(i, 0)
        for n in range(blocks):
            out[i % 2, n : n + 1, :] = row[:, n * size : (n + 1) * size]
    n2g[...] = pair(4, 0)[0]
    n2b[...] = pair(5, 0)[0]
    gb2[...] = pair(6, 0)[0]
    ch = tail.shape[2]
    for i in range(math.prod(gb1.shape) // ch):
        row = pair(7 + i, 0)
        if gb1.ndim == 1:
            gb1[i * ch : (i + 1) * ch] = row[0]
        else:
            gb1[i : i + 1, :] = row
    n1g[...] = sum(pair(d, 1) for d in range(parts))[0]
    n1b[...] = sum(pair(d, 2) for d in range(parts))[0]


def whole(shape, extra=0):
    return pl.BlockSpec(shape, lambda *_: (0,) * len(shape))


def run(kernel, outs, args, scratch=(), picked=(), choice=None, flops=0, limit=56, narrow=(), lanes=0):
    moved = sum(math.prod(a.shape) * a.dtype.itemsize for a in args)
    moved += sum(math.prod(o.shape) * o.dtype.itemsize for o in outs)
    params = pltpu.CompilerParams(vmem_limit_bytes=limit * 2**20)
    cost = pl.CostEstimate(flops=flops, bytes_accessed=moved, transcendentals=0)
    out_shape = [jax.ShapeDtypeStruct(o.shape, o.dtype) for o in outs]
    if choice is None:
        return pl.pallas_call(
            kernel,
            out_shape=out_shape,
            in_specs=[pl.BlockSpec(memory_space=pltpu.VMEM)] * len(args),
            out_specs=[pl.BlockSpec(memory_space=pltpu.VMEM)] * len(outs),
            scratch_shapes=list(scratch),
            compiler_params=params,
            cost_estimate=cost,
        )(*args)
    specs = [
        pl.BlockSpec((1, *a.shape[1:]), lambda i, c: (c[0], 0, 0))
        if i in picked
        else whole((a.shape[0], lanes) if i in narrow else a.shape)
        for i, a in enumerate(args)
    ]
    return pl.pallas_call(
        kernel,
        out_shape=out_shape,
        grid_spec=pltpu.PrefetchScalarGridSpec(
            num_scalar_prefetch=1,
            grid=(1,),
            in_specs=specs,
            out_specs=[whole(o.shape) for o in outs],
            scratch_shapes=list(scratch),
        ),
        compiler_params=params,
        cost_estimate=cost,
    )(choice, *args)


def added(terms):
    return sum(term.astype(F32) for term in terms)


def swapped(away, bit, parts):
    return lax.ppermute(away, "lat", [(d, d ^ bit) for d in range(parts)])


def added(terms, first, end):
    return sum(t[:, first:end].astype(F32) for t in terms)


def later(value, arrays):
    return lax.optimization_barrier((value, arrays))[0]


def together(value, arrays):
    return lax.optimization_barrier((value, arrays))


def body(
    field,
    row_group,
    row_valid,
    norm1_gain,
    norm1_bias,
    spec_w1,
    spec_b1,
    spec_w2,
    spec_b2,
    norm2_gain,
    norm2_bias,
    fc1_weight,
    fc1_bias,
    fc2_weight,
    fc2_bias,
    cotangent,
):
    rows_dev, columns, ch = field.shape
    parts, mp = lax.axis_size("lat"), lax.axis_size("mp")
    me = lax.axis_index("lat")
    rows = rows_dev * parts
    full_width = ch * mp
    padded = -(-columns // 16) * 16
    tokens = rows_dev * padded
    blocks, size = spec_w1.shape[1], spec_w1.shape[2]
    hidden = fc1_weight.shape[1]
    share = -(-HALVES // parts)
    group = 2 * rows_dev * share
    patches = parts * group

    def f32(*shape):
        return jax.ShapeDtypeStruct(shape, F32)

    def bf(*shape):
        return jax.ShapeDtypeStruct(shape, BF)

    lon = [jnp.asarray(t) for t in longitude_tables(parts, share, rows_dev, columns, padded)]
    local_group = lax.dynamic_slice_in_dim(row_group, me * rows_dev, rows_dev)
    choice = sum(
        jnp.where(local_group[r] == 0, 1 << r, 0) for r in range(rows_dev)
    ).astype(jnp.int32).reshape(1)

    field_all = lax.all_gather(field, "mp", axis=0)
    table = pltpu.VMEM((2, patches, tokens), BF)
    (freq,) = pl.pallas_call(
        functools.partial(norm_one_kernel, columns, padded),
        out_shape=[f32(patches, ch)],
        in_specs=[pl.BlockSpec(memory_space=pltpu.SMEM)]
        + [pl.BlockSpec(memory_space=pltpu.VMEM)] * 3
        + [pl.BlockSpec(memory_space=pl.ANY)] * 2,
        out_specs=[pl.BlockSpec(memory_space=pltpu.VMEM)],
        scratch_shapes=[
            pltpu.VMEM((mp, tokens, ch), F32),
            table,
            pltpu.SemaphoreType.DMA((2,)),
        ],
        compiler_params=pltpu.CompilerParams(vmem_limit_bytes=56 * 2**20),
    )(row_group, field_all, norm1_gain, norm1_bias, *lon)

    def to_other(values, rows_each):
        return lax.all_to_all(values.reshape(parts, rows_each, ch), "lat", 0, 0, tiled=True)

    z = to_other(freq, group).reshape(patches, ch)

    cos_mat, sin_mat = latitude_tables(row_group, row_valid)
    width = jnp.where(row_group == 0, LON_FINE, LON_COARSE).astype(jnp.int32)
    here = me * share + jnp.arange(share, dtype=jnp.int32)
    lone = (here[None, :] == 0) | (2 * here[None, :] == width[:, None])
    keep = (1.0 - lone.astype(F32)).reshape(rows * share, 1)
    lat = run(
        functools.partial(latitude_kernel, share),
        [bf(2 * patches, patches)] * 2,
        [
            jnp.concatenate([cos_mat, sin_mat], axis=1),
            *(jnp.asarray(t) for t in latitude_spread(rows, share)),
            keep,
        ],
    )
    spec = jnp.stack([spec_w1, spec_w2]).transpose(0, 1, 3, 2, 4).reshape(4, size, ch)
    spec_bias = jnp.concatenate([spec_b1.reshape(1, 2 * ch), spec_b2.reshape(1, 2 * ch)], axis=0)
    vectors = jnp.concatenate([norm1_gain, norm1_bias, norm2_gain, norm2_bias]).reshape(4, ch)
    vectors_all = lax.all_gather(vectors, "mp", axis=0)
    dy_all = lax.all_gather(cotangent, "mp", axis=0)
    z, vectors_all, dy_all = lax.optimization_barrier((z, vectors_all, dy_all))

    saved = [bf(patches, 2 * ch), bf(patches, 2 * ch), f32(patches, 2 * ch), f32(patches, 2 * ch)]
    vmem, hbm = pl.BlockSpec(memory_space=pltpu.VMEM), pl.BlockSpec(memory_space=pl.ANY)
    eo, s, h, slope, gate = pl.pallas_call(
        functools.partial(filter_kernel, blocks, size),
        out_shape=[bf(patches, ch), *saved],
        in_specs=[vmem] * 5,
        out_specs=[vmem] + [hbm] * 4,
        scratch_shapes=[pltpu.VMEM(a.shape, a.dtype) for a in saved]
        + [pltpu.SemaphoreType.DMA((4,))],
        compiler_params=pltpu.CompilerParams(vmem_limit_bytes=56 * 2**20),
    )(z, *lat, spec, spec_bias)
    chunk = CHUNK if hidden % (3 * CHUNK) == 0 else 256
    steps = hidden // chunk
    bits = [1 << b for b in range(parts.bit_length() - 1)]
    orders = [bits[i:3] + bits[:i] + bits[3:] for i in range(3)]
    pieces = len(orders)
    share_rows = full_width // parts
    places = np.stack(
        [np.arange(full_width) // share_rows, np.arange(full_width) % share_rows], axis=1
    ).astype(np.int32)
    dyt, dy_pad, base, xh1, inv1 = run(
        functools.partial(cotangent_kernel, columns, padded),
        [
            bf(full_width, tokens),
            bf(tokens, full_width),
            f32(mp, tokens, ch),
            f32(tokens, ch),
            f32(tokens, 1),
        ],
        [dy_all, jnp.asarray(places), field_all, vectors_all],
        [pltpu.VMEM((tokens, ch), F32)],
    )
    eo = to_other(eo, group).reshape(patches, ch)
    eo, dyt, dy_pad, base = lax.optimization_barrier((eo, dyt, dy_pad, base))
    eo = lax.all_gather(eo, "mp", axis=0)

    send_lanes = 2 * ch + 128
    piece_shape = (2, full_width // 2, hidden // pieces)
    kept_send, away_send, g_fc1_bias, norm2, x1, *grads = pl.pallas_call(
        functools.partial(mlp_kernel, orders, rows_dev),
        out_shape=[
            bf(tokens, send_lanes),
            bf(mp - 1, tokens, send_lanes),
            f32(1, hidden),
            f32(tokens, 2),
            f32(tokens, ch),
            *[bf(*piece_shape)] * (2 * pieces),
        ],
        in_specs=[pl.BlockSpec(memory_space=pltpu.SMEM), vmem, vmem, vmem] + [hbm] * 8,
        out_specs=[hbm, hbm, vmem, vmem, hbm] + [hbm] * (2 * pieces),
        scratch_shapes=[
            pltpu.VMEM(eo.shape, BF),
            table,
            pltpu.VMEM(base.shape, F32),
            pltpu.VMEM(fc1_weight.shape, BF),
            pltpu.VMEM(dy_pad.shape, BF),
            pltpu.VMEM(fc2_weight.shape, BF),
            pltpu.VMEM(dyt.shape, BF),
            pltpu.VMEM((tokens, send_lanes), BF),
            pltpu.VMEM((mp - 1, tokens, send_lanes), BF),
            *[pltpu.VMEM(piece_shape, BF)] * (2 * pieces),
            pltpu.VMEM((tokens, full_width), BF),
            pltpu.VMEM((full_width, tokens), BF),
            pltpu.VMEM((tokens, hidden), BF),
            pltpu.VMEM((tokens, hidden), BF),
            pltpu.SemaphoreType.DMA((16 + 8 * pieces,)),
        ],
        compiler_params=pltpu.CompilerParams(vmem_limit_bytes=56 * 2**20),
        cost_estimate=pl.CostEstimate(
            flops=10 * tokens * full_width * hidden, bytes_accessed=16 * 2**20, transcendentals=0
        ),
    )(
        row_group,
        vectors_all,
        fc1_bias.reshape(1, hidden),
        jnp.asarray(places),
        eo,
        *lon,
        base,
        fc1_weight,
        dy_pad,
        fc2_weight,
        dyt,
    )
    got = [
        lax.ppermute(away_send[i - 1], "mp", [(d, (d + i) % mp) for d in range(mp)])
        for i in range(1, mp)
    ]

    def exchanged(away, turn):
        return [swapped(a, order[turn], parts) for a, order in zip(away, orders)]

    rows_each = full_width // 4
    streams = [[kept] for kept in grads[0::2]]
    got_rows = exchanged(grads[1::2], 0)
    streams = [[*terms, part] for terms, part in zip(streams, got_rows)]
    away = [added(terms, rows_each, 2 * rows_each).astype(BF) for terms in streams]

    dx1, dfreq, sums2 = run(
        functools.partial(back_mix_kernel, columns, padded, full_width),
        [f32(tokens, ch), bf(patches, ch), f32(8, ch)],
        [dy_all, norm2_gain, *lon, norm2, x1, kept_send, *got],
        [pltpu.VMEM((tokens, ch), F32)],
        (2, 3),
        choice,
        narrow=range(6, 6 + mp),
        lanes=ch + 128 if ch % 128 == 0 else send_lanes,
    )

    dz = to_other(dfreq, group).reshape(patches, ch)
    dz = later(dz, away)
    got_rows = exchanged(away, 1)
    spec_rows = 4 * size // parts
    send_rows = -(-(group + spec_rows + 2) // 8) * 8
    (sent,) = run(
        functools.partial(filter_back_kernel, blocks, size, group),
        [bf(parts, send_rows, ch)],
        [dz, *lat, spec, s, h, slope, gate, sums2, g_fc1_bias],
        [
            pltpu.VMEM((parts, send_rows, ch), F32),
            pltpu.VMEM((4 * size, ch), F32),
            pltpu.VMEM((max(parts, 16), ch), F32),
        ],
        limit=53,
    )
    sent, got_rows, (x1, halves) = lax.optimization_barrier(
        (sent, got_rows, (x1, [kept_send, *got]))
    )
    out_field = x1 + sum(part[:, ch + 128 :].astype(F32) for part in halves) + fc2_bias
    out_field = out_field.astype(BF).reshape(rows_dev, padded, ch)[:, :columns]
    streams = [[*terms, part] for terms, part in zip(streams, got_rows)]
    half = rows_each // 2
    kept = [added(terms, 0, half) for terms in streams]
    got_rows = exchanged([added(terms, half, rows_each).astype(BF) for terms in streams], 2)
    quarter = half // 2
    pairs = list(zip(kept, got_rows))
    away = [added(pair, quarter, half).astype(BF) for pair in pairs]
    kept = [added(pair, 0, quarter) for pair in pairs]
    sent = lax.all_to_all(sent, "lat", 0, 0, tiled=True)
    sent, out_field = together(sent, out_field)
    sent, kept, away = lax.optimization_barrier((sent, kept, away))
    kept, away = (jnp.concatenate(arrays, axis=2) for arrays in (kept, away))
    for bit in bits[3:-1]:
        pair = (kept, swapped(away, bit, parts))
        quarter //= 2
        kept, away = added(pair, 0, quarter), added(pair, quarter, 2 * quarter).astype(BF)
    got_last = swapped(away, bits[-1], parts)
    tail_rows = -(-(spec_rows + 6) // 16) * 16
    du, stat1, tail = run(
        functools.partial(back_norm_kernel, group, spec_rows, mp),
        [f32(tokens, ch), f32(tokens, 3), bf(parts, tail_rows, ch)],
        [sent, *lon, dx1, xh1, inv1, norm1_gain],
        [pltpu.VMEM((tail_rows, ch), F32)],
        (1, 2),
        choice,
    )
    stat1 = lax.psum(stat1, "mp")
    stat1, got_last = together(stat1, got_last)
    weights = kept + got_last.astype(F32)
    grad_field = dx1 + stat1[:, 2:] * (
        du * norm1_gain - (stat1[:, :1] + xh1 * stat1[:, 1:2]) * (1.0 / full_width)
    )
    grad_field = grad_field.reshape(rows_dev, padded, ch)[:, :columns]

    tail = lax.all_to_all(tail, "lat", 0, 0, tiled=True)
    hidden_bias = f32(hidden) if ch % 128 == 0 else f32(hidden // ch, ch)
    vector, weight, bias = f32(ch), f32(2, blocks, size, size), f32(2, blocks, size)
    g_n1g, g_n1b, g_w1, g_b1, g_w2, g_b2, g_n2g, g_n2b, g_fc1b, g_fc2b = run(
        functools.partial(close_kernel, spec_rows, blocks, size),
        [vector, vector, weight, bias, weight, bias, vector, vector, hidden_bias, vector],
        [tail],
        [pltpu.VMEM((4 * size, ch), F32)],
        limit=24,
    )
    return (
        out_field,
        grad_field,
        g_n1g,
        g_n1b,
        g_w1,
        g_b1,
        g_w2,
        g_b2,
        g_n2g,
        g_n2b,
        weights[0],
        g_fc1b.reshape(hidden),
        weights[1].T,
        g_fc2b,
    )


def solution(mesh):
    placed = (
        P("lat", None, "mp"),
        P(),
        P(),
        P("mp"),
        P("mp"),
        P(None, "mp", None, None),
        P(None, "mp", None),
        P(None, "mp", None, None),
        P(None, "mp", None),
        P("mp"),
        P("mp"),
        P(None, "mp"),
        P("mp"),
        P("mp", None),
        P("mp"),
        P("lat", None, "mp"),
    )
    return jax.shard_map(
        body,
        mesh=mesh,
        in_specs=placed,
        out_specs=(
            P("lat", None, "mp"),
            P("lat", None, "mp"),
            P("mp"),
            P("mp"),
            P(None, "mp", None, None),
            P(None, "mp", None),
            P(None, "mp", None, None),
            P(None, "mp", None),
            P("mp"),
            P("mp"),
            P("lat", "mp"),
            P("mp"),
            P("mp", "lat"),
            P("mp"),
        ),
        check_vma=False,
    )
```
